32 devices in a mesh: row: 2 (over core), col: 2 (over x), layer: 8 (over z, y).
Axes of the slice: x: 2, y: 2, z: 4, core: 2. Of those that a mesh axis runs over, the one named last changes fastest.
Arguments:
- a_tiles: bfloat16 [2, 2, 8, 64, 128, 128], P('row', 'col', 'layer'), may hold values from -6 to 6
- p_tiles: bfloat16 [2, 2, 8, 16, 128, 128], P('row', 'col', 'layer'), may hold values from -0.03125 to 0.03125
- pair_a: int32 [2, 2, 8, 2, 32, 16], P('row', 'col', 'layer'), may hold values from 0 to 63
- pair_p: int32 [2, 2, 8, 2, 32, 16], P('row', 'col', 'layer'), may hold values from 0 to 31
Outputs:
- c_tiles: bfloat16 [2, 2, 32, 128, 128], P('row', 'col', 'layer')
The draws below stay inside these ranges and needn't reach their ends.
All inputs are finite; a program needn't handle non-finite values.
Results may differ from the reference program's by a relative error of at most 0.0014.
Values may be sent and summed in bfloat16 or wider, within the bound.
No kernel may reach another device: no remote copies, remote signals or barrier semaphores. Data moves between devices by JAX's collectives and lax.ppermute only.
A program may use at most 128 MiB of HBM per device.

```python
import jax
import jax.numpy as jnp
from jax import lax

TB = 128
SA = 64
SP = 16
FPC = 16
SC = 32
FAN = 32
N_ROW = 2
N_COL = 2
N_LAYER = 8


def set_ends(array, rng, smallest, high):
    longest = array.shape.index(max(array.shape))
    spots = []
    for shift in (0, 1):
        where = [jax.random.randint(jax.random.fold_in(rng, axis), (), 0, length) for axis, length in enumerate(array.shape)]
        where[longest] = (where[longest] + shift) % array.shape[longest]
        spots.append(tuple(where))
    return array.at[spots[0]].set(smallest).at[spots[1]].set(high)


def level_of(rng, dims, split, low, largest):
    def one(axis_at, parts):
        draws = jax.random.uniform(jax.random.fold_in(jax.random.fold_in(rng, 6), axis_at), (parts,), jnp.float32, low / len(split), largest / len(split))
        return jnp.repeat(jnp.exp(draws), dims[axis_at] // parts).reshape((-1,) + (1,) * (len(dims) - axis_at - 1))

    level = one(*split[0])
    for cut in split[1:]:
        level = level * one(*cut)
    return level


def gaussian(own_key, shape, scale, reach, pieces=(), kind=jnp.bfloat16):
    entries = scale * jax.random.normal(own_key, shape, jnp.float32)
    if pieces:
        entries = entries * level_of(own_key, shape, pieces, -0.22, 0.18)
    return jnp.clip(entries, -reach, reach).astype(kind)


def setup_inputs(seed: int = 0) -> dict:
    splits = jax.random.split(jax.random.key(seed), 5)
    a_tiles = gaussian(splits[0], (N_ROW, N_COL, N_LAYER, SA, TB, TB), 1.0, 6.0, ((0, 2), (1, 2), (2, 8)))
    p_tiles = gaussian(splits[1], (N_ROW, N_COL, N_LAYER, SP, TB, TB), (TB * FAN * N_LAYER) ** -0.5, 0.03125, ((0, 2), (1, 2), (2, 8)))
    pair_a = set_ends(jax.random.randint(splits[2], (N_ROW, N_COL, N_LAYER, N_COL, SC, FPC), 0, SA), jax.random.fold_in(splits[2], 1), 0, SA - 1).astype(jnp.int32)
    pair_p = set_ends(jax.random.randint(splits[3], (N_ROW, N_COL, N_LAYER, N_COL, SC, FPC), 0, N_ROW * SP), jax.random.fold_in(splits[3], 1), 0, (N_ROW * SP) - 1).astype(jnp.int32)
    return dict(a_tiles=a_tiles, p_tiles=p_tiles, pair_a=pair_a, pair_p=pair_p)


def reference(a_tiles, p_tiles, pair_a, pair_p):
    offsets = (jnp.arange(N_COL, dtype=jnp.int32) * SA)[:, None, None]

    def block(flat):
        r_index = flat // N_COL
        c_index = flat % N_COL
        a_row = lax.dynamic_index_in_dim(a_tiles, r_index, 0, keepdims=False)
        p_col = lax.dynamic_index_in_dim(p_tiles, c_index, 1, keepdims=False)
        pairs_a = lax.dynamic_index_in_dim(lax.dynamic_index_in_dim(pair_a, r_index, 0, keepdims=False), c_index, 0, keepdims=False)
        pairs_p = lax.dynamic_index_in_dim(lax.dynamic_index_in_dim(pair_p, r_index, 0, keepdims=False), c_index, 0, keepdims=False)
        a_layers = jnp.moveaxis(a_row, 1, 0)
        p_layers = jnp.moveaxis(p_col, 1, 0)

        def layer_step(total, inputs):
            a_layer, p_layer, index_a, index_p = inputs
            a_flat = a_layer.reshape(N_COL * SA, TB, TB)
            p_flat = p_layer.reshape(N_ROW * SP, TB, TB)
            glob_a = jnp.transpose(index_a + offsets, (1, 0, 2)).reshape(SC, FAN)
            glob_p = jnp.transpose(index_p, (1, 0, 2)).reshape(SC, FAN)

            def pair_step(acc, column):
                left = a_flat[column[0]].astype(jnp.float32)
                right = p_flat[column[1]].astype(jnp.float32)
                return acc + jnp.einsum("sij,sjk->sik", left, right), None

            total, _ = lax.scan(pair_step, total, (glob_a.T, glob_p.T))
            return total, None

        start = jnp.zeros((SC, TB, TB), jnp.float32)
        total, _ = lax.scan(layer_step, start, (a_layers, p_layers, pairs_a, pairs_p))
        return total.astype(jnp.bfloat16)

    blocks = lax.map(block, jnp.arange(N_ROW * N_COL, dtype=jnp.int32))
    return blocks.reshape(N_ROW, N_COL, SC, TB, TB)
```

```python
import jax
import jax.numpy as jnp
from jax import lax
from jax.experimental import pallas as pl
from jax.experimental.pallas import tpu as pltpu
from jax.sharding import PartitionSpec as P

PEAK = 32766.0
HEAD = 16
SMEM = pltpu.MemorySpace.SMEM
VMEM = pltpu.MemorySpace.VMEM


def encode(tile):
    top = jnp.max(jnp.abs(tile), axis=0, keepdims=True)
    power = jnp.floor(jnp.log2(jnp.maximum(top, 2.0**-100)) + 0.001) + 1.0
    scaled = jnp.round(tile * (jnp.exp2(-power) * PEAK))
    return scaled.astype(jnp.int32).astype(jnp.int16), power.astype(jnp.int32)


def decode(coded, power):
    return coded.astype(jnp.int32).astype(jnp.float32) * (jnp.exp2(power.astype(jnp.float32)) * (1.0 / PEAK))


def store_unit(out_ref, unit, tiles):
    width = tiles[0].shape[0]
    count = len(tiles)
    rows = lax.broadcasted_iota(jnp.int32, (HEAD, width), 0)
    head = jnp.zeros((HEAD, width), jnp.int32)
    for i, tile in enumerate(tiles):
        coded, power = encode(tile)
        out_ref[unit, pl.ds(i * width, width), :] = coded
        head = jnp.where(rows == i, power, head)
    out_ref[unit, pl.ds(count * width, HEAD), :] = head.astype(jnp.int16)


def load_unit(in_ref, unit, count):
    width = in_ref.shape[-1]
    head = in_ref[unit, pl.ds(count * width, HEAD), :].astype(jnp.int32)
    return [decode(in_ref[unit, pl.ds(i * width, width), :], head[i : i + 1]) for i in range(count)]


def one_tile(a_ref, p_refs, look, fan):
    held = p_refs[0].shape[0]
    lefts, rights = [], []
    for f in range(fan):
        pa, pp = look(f)
        lefts.append(a_ref[pa])
        rights.append(p_refs[0][pp])
    left = jnp.concatenate(lefts, axis=1)
    right = jnp.concatenate(rights, axis=0)
    return jnp.dot(left, right, preferred_element_type=jnp.float32)


def own_kernel(me_ref, ia_ref, ip_ref, a_ref, p0_ref, p1_ref, out_ref, p_ref):
    held = p0_ref.shape[0]
    row = me_ref[0]
    col = me_ref[1]
    p_ref[pl.ds(row * held, held)] = p0_ref[...]
    p_ref[pl.ds((1 - row) * held, held)] = p1_ref[...]
    fan = ia_ref.shape[-1]

    def body(t, _):
        out_ref[t] = one_tile(a_ref, (p_ref,), lambda f: (ia_ref[col, t, f], ip_ref[col, t, f]), fan)
        return 0

    lax.fori_loop(0, out_ref.shape[0], body, 0)


def other_kernel(me_ref, ia_ref, ip_ref, a_ref, p0_ref, p1_ref, out_ref, p_ref):
    held = p0_ref.shape[0]
    row = me_ref[0]
    col = me_ref[1]
    p_ref[pl.ds(row * held, held)] = p0_ref[...]
    p_ref[pl.ds((1 - row) * held, held)] = p1_ref[...]
    fan = ia_ref.shape[-1]
    units = out_ref.shape[0]
    width = out_ref.shape[-1]
    count = (out_ref.shape[1] - HEAD) // width

    def body(unit, _):
        tiles = []
        for i in range(count):
            t = unit * count + i
            tiles.append(one_tile(a_ref, (p_ref,), lambda f: (ia_ref[col, t, f], ip_ref[col, t, f]), fan))
        store_unit(out_ref, unit, tiles)
        return 0

    lax.fori_loop(0, units, body, 0)


def add_kernel(own_ref, in_ref, out_ref):
    units = out_ref.shape[0]
    width = out_ref.shape[-1]
    count = (out_ref.shape[1] - HEAD) // width

    def body(unit, _):
        got = load_unit(in_ref, unit, count)
        tiles = [own_ref[unit * count + i] + got[i] for i in range(count)]
        store_unit(out_ref, unit, tiles)
        return 0

    lax.fori_loop(0, units, body, 0)


def last_kernel(in_ref, out_ref):
    units = in_ref.shape[0]
    width = out_ref.shape[-1]
    count = out_ref.shape[0]
    for i in range(count):
        total = jnp.zeros((width, width), jnp.float32)
        for unit in range(units):
            power = in_ref[unit, pl.ds(count * width, HEAD), :].astype(jnp.int32)[i : i + 1]
            total += decode(in_ref[unit, pl.ds(i * width, width), :], power)
        out_ref[i] = total.astype(out_ref.dtype)


def call(kernel, out_shape, smem, vmem, scratch=(), flops=0):
    moved = sum(x.size * x.dtype.itemsize for x in vmem) + out_shape.size * out_shape.dtype.itemsize
    return pl.pallas_call(
        kernel,
        out_shape=out_shape,
        in_specs=[pl.BlockSpec(memory_space=SMEM)] * len(smem) + [pl.BlockSpec(memory_space=VMEM)] * len(vmem),
        out_specs=pl.BlockSpec(memory_space=VMEM),
        scratch_shapes=list(scratch),
        compiler_params=pltpu.CompilerParams(vmem_limit_bytes=40 * 2**20),
        cost_estimate=pl.CostEstimate(flops=flops, bytes_accessed=moved, transcendentals=0),
    )(*smem, *vmem)


def on_device(a_tiles, p_tiles, pair_a, pair_p):
    a, p, ia, ip = a_tiles[0, 0, 0], p_tiles[0, 0, 0], pair_a[0, 0, 0], pair_p[0, 0, 0]
    slots, fan = ia.shape[1:]
    held, width = p.shape[0], p.shape[-1]
    layers = lax.axis_size("layer")
    count = slots // layers
    swap = [(0, 1), (1, 0)]
    me = jnp.stack([lax.axis_index("row"), lax.axis_index("col")]).astype(jnp.int32)

    p_x = lax.ppermute(p, "col", swap)
    p_r = lax.ppermute(p, "row", swap)
    ia_x = lax.ppermute(ia, "col", swap)
    ip_x = lax.ppermute(ip, "col", swap)
    p_xr = lax.ppermute(p_x, "row", swap)

    flops = 2 * slots * fan * width**3
    both = pltpu.VMEM((2 * held, width, width), jnp.bfloat16)
    whole = jax.ShapeDtypeStruct((slots, width, width), jnp.float32)
    coded = jax.ShapeDtypeStruct((layers, count * width + HEAD, width), jnp.int16)
    own = call(own_kernel, whole, (me, ia, ip), (a, p, p_r), (both,), flops)
    other = call(other_kernel, coded, (me, ia_x, ip_x), (a, p_x, p_xr), (both,), flops)
    came = lax.ppermute(other, "col", swap)
    sums = call(add_kernel, coded, (), (own, came))
    spread = lax.all_to_all(sums, "layer", split_axis=0, concat_axis=0, tiled=True)
    out = call(last_kernel, jax.ShapeDtypeStruct((count, width, width), jnp.bfloat16), (), (spread,))
    return out[None, None]


def solution(mesh):
    spec = P("row", "col", "layer", None, None, None)
    return jax.shard_map(
        on_device,
        mesh=mesh,
        in_specs=(spec,) * 4,
        out_specs=P("row", "col", "layer", None, None),
        check_vma=False,
    )
```

```python
import jax
import jax.numpy as jnp
from jax import lax
from jax.experimental import pallas as pl
from jax.experimental.pallas import tpu as pltpu
from jax.sharding import PartitionSpec as P

PEAK = 32766.0
ROWS = 16
GROUP = 4
SMEM = pltpu.MemorySpace.SMEM
VMEM = pltpu.MemorySpace.VMEM


def head_rows(count):
    return -(-count // ROWS) * ROWS


def message(count, width):
    return jax.ShapeDtypeStruct((count * width + head_rows(count), width), jnp.int16)


def encode(tile):
    top = jnp.max(jnp.abs(tile), axis=0, keepdims=True)
    power = jnp.floor(jnp.log2(jnp.maximum(top, 2.0**-100)) + 0.001) + 1.0
    scaled = jnp.round(tile * (jnp.exp2(-power) * PEAK))
    return scaled.astype(jnp.int32).astype(jnp.int16), power.astype(jnp.int32)


def new_head(count, width):
    return jnp.zeros((head_rows(count), width), jnp.int32)


def put_tile(ref, slot, tile, head):
    width = tile.shape[0]
    coded, power = encode(tile)
    ref[pl.ds(pl.multiple_of(slot * width, width), width), :] = coded
    rows = lax.broadcasted_iota(jnp.int32, head.shape, 0)
    return jnp.where(rows == slot, power, head)


def put_head(ref, head):
    ref[pl.ds(ref.shape[0] - head.shape[0], head.shape[0]), :] = head.astype(jnp.int16)


def get_head(ref, count):
    rows = head_rows(count)
    return ref[pl.ds(ref.shape[0] - rows, rows), :].astype(jnp.int32)


def get_tile(ref, slot, head):
    width = ref.shape[-1]
    rows = lax.broadcasted_iota(jnp.int32, head.shape, 0)
    power = jnp.sum(jnp.where(rows == slot, head, 0), axis=0, keepdims=True)
    coded = ref[pl.ds(pl.multiple_of(slot * width, width), width), :]
    return coded.astype(jnp.int32).astype(jnp.float32) * (jnp.exp2(power.astype(jnp.float32)) * (1.0 / PEAK))


def product(a_ref, p_ref, look, fan):
    chosen = [look(f) for f in range(fan)]
    left = jnp.concatenate([a_ref[pa] for pa, _ in chosen], axis=1)
    right = jnp.concatenate([p_ref[pp] for _, pp in chosen], axis=0)
    return jnp.dot(left, right, preferred_element_type=jnp.float32)


def join(me_ref, p0_ref, p1_ref, p_ref):
    held = p0_ref.shape[0]
    p_ref[pl.ds(me_ref[0] * held, held)] = p0_ref[...]
    p_ref[pl.ds((1 - me_ref[0]) * held, held)] = p1_ref[...]


def finder(me_ref, index_refs, fan):
    if len(index_refs) == 2:
        ia_ref, ip_ref = index_refs
        col = me_ref[1]
        return lambda t: lambda f: (ia_ref[col, f, t], ip_ref[col, f, t])
    (both_ref,) = index_refs
    return lambda t: lambda f: (both_ref[f, t], both_ref[fan + f, t])


def send_kernel(n_index, fan, count, chunk):
    first, size = chunk

    def kernel(me_ref, *refs):
        index_refs = refs[:n_index]
        a_ref, p0_ref, p1_ref = refs[n_index : n_index + 3]
        out_ref, p_ref = refs[-2:]
        width = out_ref.shape[-1]
        join(me_ref, p0_ref, p1_ref, p_ref)
        find = finder(me_ref, index_refs, fan)
        side = 1 - (me_ref[2] & 1)
        places = out_ref.shape[0] // (width * size)

        def body(step, head):
            for k in range(GROUP):
                slot = step * GROUP + k
                place, i = slot // size, slot % size
                tile = product(a_ref, p_ref, find((place * 2 + side) * count + first + i), fan)
                head = put_tile(out_ref, slot, tile, head)
            return head

        head = lax.fori_loop(0, places * size // GROUP, body, new_head(places * size, width))
        put_head(out_ref, head)

    return kernel


def keep_kernel(n_index, fan, count, chunks):
    def kernel(me_ref, *refs):
        index_refs = refs[:n_index]
        a_ref, p0_ref, p1_ref = refs[n_index : n_index + 3]
        out_refs, p_ref = refs[-1 - len(chunks) : -1], refs[-1]
        join(me_ref, p0_ref, p1_ref, p_ref)
        find = finder(me_ref, index_refs, fan)
        side = me_ref[2] & 1
        for (first, size), out_ref in zip(chunks, out_refs):

            def body(step, _):
                for k in range(GROUP):
                    slot = step * GROUP + k
                    place, i = slot // size, slot % size
                    out_ref[slot] = product(a_ref, p_ref, find((place * 2 + side) * count + first + i), fan)
                return 0

            lax.fori_loop(0, out_ref.shape[0] // GROUP, body, 0)

    return kernel


def add_kernel(size, keeps_own):
    def kernel(me_ref, kept_ref, in_ref, *refs):
        total = kept_ref.shape[0]
        places = total // size
        out_refs = refs[-places:]
        head_in = get_head(in_ref, total)
        mine = me_ref[2] >> 1
        for d, out_ref in enumerate(out_refs):
            place = mine ^ d
            sums = [kept_ref[place * size + i] + get_tile(in_ref, place * size + i, head_in) for i in range(size)]
            if d == 0 and keeps_own:
                for i in range(size):
                    out_ref[i] = sums[i]
            else:
                head = new_head(size, kept_ref.shape[-1])
                for i in range(size):
                    head = put_tile(out_ref, i, sums[i], head)
                put_head(out_ref, head)

    return kernel


def last_kernel(size, n_messages, n_before):
    def kernel(*refs):
        own_ref, in_refs, before_refs = refs[0], refs[1 : 1 + n_messages], refs[1 + n_messages : 1 + n_messages + n_before]
        out_ref = refs[-1]
        at = 0
        for ref in before_refs:
            out_ref[pl.ds(at, ref.shape[0])] = ref[...]
            at += ref.shape[0]
        heads = [get_head(ref, size) for ref in in_refs]
        for i in range(size):
            total = own_ref[i]
            for ref, head in zip(in_refs, heads):
                total += get_tile(ref, i, head)
            out_ref[at + i] = total.astype(out_ref.dtype)

    return kernel


def call(kernel, out_shape, smem, vmem, after=(), scratch=(), flops=0):
    outs = out_shape if isinstance(out_shape, (list, tuple)) else [out_shape]
    moved = sum(x.size * x.dtype.itemsize for x in (*vmem, *outs))
    n_real = len(smem) + len(vmem)

    def wrapped(*refs):
        kernel(*refs[:n_real], *refs[n_real + len(after) :])

    return pl.pallas_call(
        wrapped,
        out_shape=out_shape,
        in_specs=[pl.BlockSpec(memory_space=SMEM)] * len(smem)
        + [pl.BlockSpec(memory_space=VMEM)] * len(vmem)
        + [pl.BlockSpec(memory_space=pl.ANY)] * len(after),
        out_specs=jax.tree.map(lambda _: pl.BlockSpec(memory_space=VMEM), out_shape),
        scratch_shapes=list(scratch),
        compiler_params=pltpu.CompilerParams(vmem_limit_bytes=40 * 2**20),
        cost_estimate=pl.CostEstimate(flops=flops, bytes_accessed=moved, transcendentals=0),
    )(*smem, *vmem, *after)


def on_device(a_tiles, p_tiles, pair_a, pair_p):
    a, p = a_tiles[0, 0, 0], p_tiles[0, 0, 0]
    ia, ip = jnp.swapaxes(pair_a[0, 0, 0], 1, 2), jnp.swapaxes(pair_p[0, 0, 0], 1, 2)
    fan, slots = ia.shape[1:]
    held, width = p.shape[0], p.shape[-1]
    layers = lax.axis_size("layer")
    count, places = slots // layers, layers // 2
    swap = [(0, 1), (1, 0)]
    me = jnp.stack([lax.axis_index("row"), lax.axis_index("col"), lax.axis_index("layer")]).astype(jnp.int32)

    p_x = lax.ppermute(p, "col", swap)
    p_r = lax.ppermute(p, "row", swap)
    far = 1 - lax.axis_index("col")
    lists = jnp.concatenate([ia[far], ip[far]], axis=0)
    lists_x = lax.ppermute(lists, "col", swap)
    p_xr = lax.ppermute(p_x, "row", swap)

    both = (pltpu.VMEM((2 * held, width, width), jnp.bfloat16),)
    half = count // 2
    chunks = [(0, half), (half, count - half)]
    flops = 2 * places * half * fan * width**3
    pairs = [(i, i ^ 1) for i in range(layers)]

    def floats(size):
        return jax.ShapeDtypeStruct((size, width, width), jnp.float32)

    def send(smem, vmem, chunk, after):
        shape = message(places * chunk[1], width)
        kernel = send_kernel(len(smem) - 1, fan, count, chunk)
        return call(kernel, shape, smem, vmem, after, both, flops)

    def keep(smem, vmem, after):
        shapes = [floats(places * size) for _, size in chunks]
        kernel = keep_kernel(len(smem) - 1, fan, count, chunks)
        return call(kernel, shapes, smem, vmem, after, both, 2 * flops)

    def add(kept, came, size, keeps_own, after):
        shapes = [floats(size) if d == 0 and keeps_own else message(size, width) for d in range(places)]
        return call(add_kernel(size, keeps_own), shapes, (me,), (kept, came), after)

    own_in = ((me, ia, ip), (a, p, p_r))
    own_sent, after = [], ()
    for chunk in chunks:
        made = send(*own_in, chunk, after)
        after = (made,)
        own_sent.append(lax.ppermute(made, "layer", pairs))
    own_kept = keep(*own_in, after)
    after = (own_kept[0],)

    def own_second(n, after):
        out = add(own_kept[n], own_sent[n], chunks[n][1], True, after)
        moved = [
            lax.ppermute(out[d], "layer", [(i, i ^ (2 * d)) for i in range(layers)]) for d in range(1, places)
        ]
        return out[0], moved

    other_in = ((me, lists_x), (a, p_x, p_xr))
    owns, other_sent = [], []
    owns.append(own_second(0, after))
    after = (owns[0][0],)
    for n, chunk in enumerate(chunks):
        made = send(*other_in, chunk, after)
        after = (made,)
        other_sent.append(lax.ppermute(made, "layer", pairs))
    owns.append(own_second(1, after))
    after = (owns[1][0],)
    other_kept = keep(*other_in, after)
    results = []
    for n, (first, size) in enumerate(chunks):
        out = add(other_kept[n], other_sent[n], size, False, ())
        moved = []
        for d in reversed(range(places)):
            perm = [(c * layers + i, (1 - c) * layers + (i ^ (2 * d))) for c in range(2) for i in range(layers)]
            moved.append(lax.ppermute(out[d], ("col", "layer"), perm))
        mine, came = owns[n]
        final = n == len(chunks) - 1
        shape = jax.ShapeDtypeStruct((count if final else size, width, width), jnp.bfloat16)
        before = tuple(results) if final else ()
        kernel = last_kernel(size, len(came) + len(moved), len(before))
        results.append(call(kernel, shape, (), (mine, *came, *moved, *before)))
    return results[-1][None, None]


def solution(mesh):
    spec = P("row", "col", "layer", None, None, None)
    return jax.shard_map(
        on_device,
        mesh=mesh,
        in_specs=(spec,) * 4,
        out_specs=P("row", "col", "layer", None, None),
        check_vma=False,
    )
```

```python
import jax
import jax.numpy as jnp
from jax import lax
from jax.experimental import pallas as pl
from jax.experimental.pallas import tpu as pltpu
from jax.sharding import PartitionSpec as P

PEAK = 32766.0
ROWS = 16
GROUP = 4
SMEM = pltpu.MemorySpace.SMEM
VMEM = pltpu.MemorySpace.VMEM


def head_rows(count):
    return -(-count // ROWS) * ROWS


def message(count, width):
    return jax.ShapeDtypeStruct((count * width + head_rows(count), width), jnp.int16)


def encode(tile):
    top = jnp.max(jnp.abs(tile), axis=0, keepdims=True)
    power = jnp.floor(jnp.log2(jnp.maximum(top, 2.0**-100)) + 0.001) + 1.0
    scaled = jnp.round(tile * (jnp.exp2(-power) * PEAK))
    return scaled.astype(jnp.int32).astype(jnp.int16), power.astype(jnp.int32)


def new_head(count, width):
    return jnp.zeros((head_rows(count), width), jnp.int32)


def rows_at(slot, width):
    start = slot * width
    return pl.ds(start if isinstance(start, int) else pl.multiple_of(start, width), width)


def put_tile(ref, slot, tile, head):
    coded, power = encode(tile)
    ref[rows_at(slot, tile.shape[0]), :] = coded
    rows = lax.broadcasted_iota(jnp.int32, head.shape, 0)
    return jnp.where(rows == slot, power, head)


def put_head(ref, head):
    ref[pl.ds(ref.shape[0] - head.shape[0], head.shape[0]), :] = head.astype(jnp.int16)


def get_head(ref, count):
    rows = head_rows(count)
    return ref[pl.ds(ref.shape[0] - rows, rows), :].astype(jnp.int32)


def get_tile(ref, slot, head):
    rows = lax.broadcasted_iota(jnp.int32, head.shape, 0)
    power = jnp.sum(jnp.where(rows == slot, head, 0), axis=0, keepdims=True)
    coded = ref[rows_at(slot, ref.shape[-1]), :]
    return coded.astype(jnp.int32).astype(jnp.float32) * (jnp.exp2(power.astype(jnp.float32)) * (1.0 / PEAK))


def product(a_ref, p_ref, look, fan):
    chosen = [look(f) for f in range(fan)]
    left = jnp.concatenate([a_ref[pa] for pa, _ in chosen], axis=1)
    right = jnp.concatenate([p_ref[pp] for _, pp in chosen], axis=0)
    return jnp.dot(left, right, preferred_element_type=jnp.float32)


def insert(rest, at, bit):
    low = rest & ((1 << at) - 1)
    return ((rest >> at) << (at + 1)) | (bit << at) | low


def finder(me_ref, index_refs, fan):
    if len(index_refs) == 2:
        ia_ref, ip_ref = index_refs
        col = me_ref[1]
        return lambda t: lambda f: (ia_ref[col, f, t], ip_ref[col, f, t])
    (both_ref,) = index_refs
    return lambda t: lambda f: (both_ref[f, t], both_ref[fan + f, t])


def send_kernel(n_index, n_p, fan, count, chunk, bit):
    first, size = chunk

    def kernel(me_ref, *refs):
        find = finder(me_ref, refs[:n_index], fan)
        a_ref = refs[n_index]
        p_refs = refs[n_index + 1 : n_index + 1 + n_p]
        out_ref = refs[n_index + 1 + n_p]
        width = out_ref.shape[-1]
        if n_p == 2:
            p_ref = refs[-1]
            held = p_refs[0].shape[0]
            p_ref[pl.ds(me_ref[0] * held, held)] = p_refs[0][...]
            p_ref[pl.ds((1 - me_ref[0]) * held, held)] = p_refs[1][...]
        else:
            (p_ref,) = p_refs
        side = 1 - ((me_ref[2] >> bit) & 1)
        total = out_ref.shape[0] // width

        def body(step, head):
            for k in range(GROUP):
                slot = step * GROUP + k
                layer = insert(slot // size, bit, side)
                tile = product(a_ref, p_ref, find(layer * count + first + slot % size), fan)
                head = put_tile(out_ref, slot, tile, head)
            return head

        put_head(out_ref, lax.fori_loop(0, total // GROUP, body, new_head(total, width)))

    return kernel


def keep_kernel(n_index, fan, count, chunks, bit):
    def kernel(me_ref, *refs):
        find = finder(me_ref, refs[:n_index], fan)
        a_ref, p_ref = refs[n_index : n_index + 2]
        side = (me_ref[2] >> bit) & 1
        for (first, size), out_ref in zip(chunks, refs[n_index + 2 :]):

            def body(step, _):
                for k in range(GROUP):
                    slot = step * GROUP + k
                    layer = insert(slot // size, bit, side)
                    out_ref[slot] = product(a_ref, p_ref, find(layer * count + first + slot % size), fan)
                return 0

            lax.fori_loop(0, out_ref.shape[0] // GROUP, body, 0)

    return kernel


def add_kernel(sizes, rest, bit, keeps):
    at = rest.index(bit)
    full = sum(sizes)
    halves = 1 << (len(rest) - 1)

    def kernel(me_ref, *refs):
        n = len(sizes)
        kept_refs, in_refs, (sent_ref, stay_ref) = refs[:n], refs[n : 2 * n], refs[2 * n : 2 * n + 2]
        width = sent_ref.shape[-1]
        mine = (me_ref[2] >> bit) & 1
        heads = [get_head(ref, ref.shape[0] // width) for ref in in_refs]

        def sums(place):
            for size, kept_ref, in_ref, head in zip(sizes, kept_refs, in_refs, heads):
                for i in range(size):
                    slot = place * size + i
                    yield kept_ref[slot] + get_tile(in_ref, slot, head)

        def send(ref, side):
            def body(half, head):
                for i, tile in enumerate(sums(insert(half, at, side))):
                    head = put_tile(ref, half * full + i, tile, head)
                return head

            put_head(ref, lax.fori_loop(0, halves, body, new_head(halves * full, width), unroll=halves <= 4))

        send(sent_ref, 1 - mine)
        if keeps:

            def body(half, _):
                for i, tile in enumerate(sums(insert(half, at, mine))):
                    stay_ref[half * full + i] = tile
                return 0

            lax.fori_loop(0, halves, body, 0, unroll=halves <= 4)
        else:
            send(stay_ref, mine)

    return kernel


def last_kernel(first, size, n_own, n_messages, n_before):
    def kernel(own_ref, own_in_ref, *refs):
        in_refs, before_refs, out_ref = refs[:n_messages], refs[n_messages:-1], refs[-1]
        at = 0
        for ref in before_refs:
            out_ref[pl.ds(at, ref.shape[0])] = ref[...]
            at += ref.shape[0]
        own_head = get_head(own_in_ref, n_own)
        heads = [get_head(ref, size) for ref in in_refs]
        for i in range(size):
            total = own_ref[first + i] + get_tile(own_in_ref, first + i, own_head)
            for ref, head in zip(in_refs, heads):
                total += get_tile(ref, i, head)
            out_ref[at + i] = total.astype(out_ref.dtype)

    return kernel


def call(kernel, out_shape, smem, vmem, after=(), scratch=(), flops=0):
    n_real = len(smem) + len(vmem)

    def wrapped(*refs):
        kernel(*refs[:n_real], *refs[n_real + len(after) :])

    return pl.pallas_call(
        wrapped,
        out_shape=out_shape,
        in_specs=[pl.BlockSpec(memory_space=SMEM)] * len(smem)
        + [pl.BlockSpec(memory_space=VMEM)] * len(vmem)
        + [pl.BlockSpec(memory_space=pl.ANY)] * len(after),
        out_specs=jax.tree.map(lambda _: pl.BlockSpec(memory_space=VMEM), out_shape),
        scratch_shapes=list(scratch),
        compiler_params=pltpu.CompilerParams(vmem_limit_bytes=40 * 2**20),
        cost_estimate=pl.CostEstimate(flops=1, bytes_accessed=1, transcendentals=0),
    )(*smem, *vmem, *after)


def hold(x, after):
    def kernel(*refs):
        pass

    return pl.pallas_call(
        kernel,
        out_shape=jax.ShapeDtypeStruct(x.shape, x.dtype),
        in_specs=[pl.BlockSpec(memory_space=pl.ANY)] * (1 + len(after)),
        out_specs=pl.BlockSpec(memory_space=pl.ANY),
        input_output_aliases={0: 0},
    )(x, *after)


def on_device(a_tiles, p_tiles, pair_a, pair_p):
    a, p = a_tiles[0, 0, 0], p_tiles[0, 0, 0]
    ia, ip = jnp.swapaxes(pair_a[0, 0, 0], 1, 2), jnp.swapaxes(pair_p[0, 0, 0], 1, 2)
    fan, slots = ia.shape[1:]
    held, width = p.shape[0], p.shape[-1]
    layers = lax.axis_size("layer")
    bits = layers.bit_length() - 1
    count = slots // layers
    swap = [(0, 1), (1, 0)]
    me = jnp.stack([lax.axis_index("row"), lax.axis_index("col"), lax.axis_index("layer")]).astype(jnp.int32)

    half = count // 2
    chunks = [(0, half), (half, count - half)]
    flops = layers * half * fan * width**3

    def floats(size):
        return jax.ShapeDtypeStruct((size, width, width), jnp.float32)

    def exchange(x, bit):
        return lax.ppermute(x, "layer", [(i, i ^ (1 << bit)) for i in range(layers)])

    def cross(x, bit):
        flip = 0 if bit is None else 1 << bit
        perm = [(c * layers + i, (1 - c) * layers + (i ^ flip)) for c in range(2) for i in range(layers)]
        return lax.ppermute(x, ("col", "layer"), perm)

    def start(smem, vmem, chunk, bit, after):
        shapes = [message(layers // 2 * chunk[1], width), jax.ShapeDtypeStruct((2 * held, width, width), p.dtype)]
        return call(send_kernel(len(smem) - 1, 2, fan, count, chunk, bit), shapes, smem, vmem, after, (), flops)

    def send(smem, vmem, chunk, bit, after):
        shape = message(layers // 2 * chunk[1], width)
        return call(send_kernel(len(smem) - 1, 1, fan, count, chunk, bit), shape, smem, vmem, after, (), flops)

    def keep(smem, vmem, bit, after):
        shapes = [floats(layers // 2 * size) for _, size in chunks]
        return call(keep_kernel(len(smem) - 1, fan, count, chunks, bit), shapes, smem, vmem, after, (), 2 * flops)

    def add(kept, came, sizes, rest, bit, keeps, after):
        n = sum(sizes) << (len(rest) - 1)
        shapes = [message(n, width), floats(n) if keeps else message(n, width)]
        return call(add_kernel(sizes, rest, bit, keeps), shapes, (me,), (*kept, *came), after)

    p_x = lax.ppermute(p, "col", swap)
    p_r = lax.ppermute(p, "row", swap)
    far = 1 - lax.axis_index("col")
    lists_x = lax.ppermute(jnp.concatenate([ia[far], ip[far]], axis=0), "col", swap)
    own_bits = [*range(1, bits), 0]
    gate = call(lambda *refs: None, jax.ShapeDtypeStruct((8, width), jnp.float32), (ia, ip), (a, p))
    smem, bit = (me, ia, ip), own_bits[0]
    made, joined = start(smem, (a, p, p_r), chunks[0], bit, (gate,))
    own_sent = [exchange(made, bit)]
    made = send(smem, (a, joined), chunks[1], bit, (made,))
    own_sent.append(exchange(made, bit))
    own_kept = keep(smem, (a, joined), bit, (made,))

    p_x = hold(p_x, (own_kept[0], own_sent[0], lists_x))
    p_xr = lax.ppermute(p_x, "row", swap)

    smem, bit = (me, lists_x), 0
    made, joined = start(smem, (a, p_x, p_xr), chunks[0], bit, ())
    other_sent = [exchange(made, bit)]
    made = send(smem, (a, joined), chunks[1], bit, (made,))
    other_sent.append(exchange(made, bit))
    rest = sorted(own_bits[1:])
    sent, own_kept = add(own_kept, own_sent, [s for _, s in chunks], rest, own_bits[1], True, (made,))
    own_sent = exchange(sent, own_bits[1])
    other_kept = keep(smem, (a, joined), bit, (sent,))

    streams = [(other_kept[n], other_sent[n]) for n in range(len(chunks))]
    rest = list(range(1, bits))
    after = ()
    for b in range(1, bits - 1):
        for n, (kept, came) in enumerate(streams):
            sent, kept = add((kept,), (came,), [chunks[n][1]], rest, b, True, after)
            after = (sent,)
            streams[n] = (kept, exchange(sent, b))
            if n == 0 and len(own_bits) > 2:
                own_rest = sorted(own_bits[2:])
                sent, own_kept = add((own_kept,), (own_sent,), [count], own_rest, own_bits[2], True, after)
                own_sent = exchange(sent, own_bits[2])
                own_bits = own_bits[:2] + own_bits[3:]
                after = (sent,)
        rest.remove(b)
    for b in own_bits[2:]:
        own_rest = sorted(own_bits[own_bits.index(b) :])
        sent, own_kept = add((own_kept,), (own_sent,), [count], own_rest, b, True, after)
        own_sent = exchange(sent, b)
        after = (sent,)

    moved = []
    for n, (kept, came) in enumerate(streams):
        sent, stay = add((kept,), (came,), [chunks[n][1]], rest, rest[0], False, after)
        after = (sent,)
        moved.append((cross(sent, rest[0]), cross(stay, None)))
    result = ()
    for n, (first, size) in enumerate(chunks):
        final = n == len(chunks) - 1
        shape = jax.ShapeDtypeStruct((count if final else size, width, width), jnp.bfloat16)
        kernel = last_kernel(first, size, count, len(moved[n]), len(result))
        result = (call(kernel, shape, (), (own_kept, own_sent, *moved[n], *result)),)
    return result[0][None, None]


def solution(mesh):
    spec = P("row", "col", "layer", None, None, None)
    return jax.shard_map(
        on_device,
        mesh=mesh,
        in_specs=(spec,) * 4,
        out_specs=P("row", "col", "layer", None, None),
        check_vma=False,
    )
```

```python
import jax
import jax.numpy as jnp
from jax import lax
from jax.experimental import pallas as pl
from jax.experimental.pallas import tpu as pltpu
from jax.sharding import PartitionSpec as P

PEAK = 32766.0
ROWS = 16
GROUP = 4
SMEM = pltpu.MemorySpace.SMEM
VMEM = pltpu.MemorySpace.VMEM


def head_rows(count):
    return -(-count // ROWS) * ROWS


def message(count, width):
    return jax.ShapeDtypeStruct((count * width + head_rows(count), width), jnp.int16)


def encode(tile):
    top = jnp.max(jnp.abs(tile), axis=0, keepdims=True)
    power = jnp.floor(jnp.log2(jnp.maximum(top, 2.0**-100)) + 0.001) + 1.0
    scaled = jnp.round(tile * (jnp.exp2(-power) * PEAK))
    return scaled.astype(jnp.int32).astype(jnp.int16), power.astype(jnp.int32)


def new_head(count, width):
    return jnp.zeros((head_rows(count), width), jnp.int32)


def rows_at(slot, width):
    start = slot * width
    return pl.ds(start if isinstance(start, int) else pl.multiple_of(start, width), width)


def put_tile(ref, slot, tile, head):
    coded, power = encode(tile)
    ref[rows_at(slot, tile.shape[0]), :] = coded
    rows = lax.broadcasted_iota(jnp.int32, head.shape, 0)
    return jnp.where(rows == slot, power, head)


def put_head(ref, head):
    ref[pl.ds(ref.shape[0] - head.shape[0], head.shape[0]), :] = head.astype(jnp.int16)


def get_head(ref, count):
    rows = head_rows(count)
    return ref[pl.ds(ref.shape[0] - rows, rows), :].astype(jnp.int32)


def get_tile(ref, slot, head):
    rows = lax.broadcasted_iota(jnp.int32, head.shape, 0)
    power = jnp.sum(jnp.where(rows == slot, head, 0), axis=0, keepdims=True)
    coded = ref[rows_at(slot, ref.shape[-1]), :]
    return coded.astype(jnp.int32).astype(jnp.float32) * (jnp.exp2(power.astype(jnp.float32)) * (1.0 / PEAK))


def product(a_ref, p_ref, look, fan):
    chosen = [look(f) for f in range(fan)]
    left = jnp.concatenate([a_ref[pa] for pa, _ in chosen], axis=1)
    right = jnp.concatenate([p_ref[pp] for _, pp in chosen], axis=0)
    return jnp.dot(left, right, preferred_element_type=jnp.float32)


def own_bit(bit):
    return (lax.axis_index("layer") >> bit) & 1


def insert(rest, at, bit):
    low = rest & ((1 << at) - 1)
    return ((rest >> at) << (at + 1)) | (bit << at) | low


def finder(lists_ref, fan):
    return lambda t: lambda f: (lists_ref[f, t], lists_ref[fan + f, t])


def send_kernel(n_p, fan, count, chunk, bit):
    first, size = chunk

    def kernel(lists_ref, a_ref, *refs):
        find = finder(lists_ref, fan)
        p_refs, out_ref = refs[:n_p], refs[n_p]
        width = out_ref.shape[-1]
        if n_p == 2:
            p_ref = refs[-1]
            held = p_refs[0].shape[0]
            row = lax.axis_index("row")
            p_ref[pl.ds(row * held, held)] = p_refs[0][...]
            p_ref[pl.ds((1 - row) * held, held)] = p_refs[1][...]
        else:
            (p_ref,) = p_refs
        side = 1 - own_bit(bit)
        total = out_ref.shape[0] // width

        def body(step, head):
            for k in range(GROUP):
                slot = step * GROUP + k
                layer = insert(slot // size, bit, side)
                tile = product(a_ref, p_ref, find(layer * count + first + slot % size), fan)
                head = put_tile(out_ref, slot, tile, head)
            return head

        put_head(out_ref, lax.fori_loop(0, total // GROUP, body, new_head(total, width)))

    return kernel


def keep_kernel(fan, count, chunks, bit):
    def kernel(lists_ref, a_ref, p_ref, *out_refs):
        find = finder(lists_ref, fan)
        side = own_bit(bit)
        for (first, size), out_ref in zip(chunks, out_refs):

            def body(step, _):
                for k in range(GROUP):
                    slot = step * GROUP + k
                    layer = insert(slot // size, bit, side)
                    out_ref[slot] = product(a_ref, p_ref, find(layer * count + first + slot % size), fan)
                return 0

            lax.fori_loop(0, out_ref.shape[0] // GROUP, body, 0)

    return kernel


def add_kernel(sizes, rest, bit, keeps):
    at = rest.index(bit)
    full = sum(sizes)
    halves = 1 << (len(rest) - 1)

    def kernel(*refs):
        n = len(sizes)
        kept_refs, in_refs, (sent_ref, stay_ref) = refs[:n], refs[n : 2 * n], refs[2 * n : 2 * n + 2]
        width = sent_ref.shape[-1]
        mine = own_bit(bit)
        heads = [get_head(ref, ref.shape[0] // width) for ref in in_refs]

        def sums(place):
            for size, kept_ref, in_ref, head in zip(sizes, kept_refs, in_refs, heads):
                for i in range(size):
                    slot = place * size + i
                    yield kept_ref[slot] + get_tile(in_ref, slot, head)

        def send(ref, side):
            def body(half, head):
                for i, tile in enumerate(sums(insert(half, at, side))):
                    head = put_tile(ref, half * full + i, tile, head)
                return head

            put_head(ref, lax.fori_loop(0, halves, body, new_head(halves * full, width), unroll=halves <= 4))

        send(sent_ref, 1 - mine)
        if keeps:

            def body(half, _):
                for i, tile in enumerate(sums(insert(half, at, mine))):
                    stay_ref[half * full + i] = tile
                return 0

            lax.fori_loop(0, halves, body, 0, unroll=halves <= 4)
        else:
            send(stay_ref, mine)

    return kernel


def last_kernel(first, size, n_own, n_messages, n_before):
    def kernel(own_ref, own_in_ref, *refs):
        in_refs, before_refs, out_ref = refs[:n_messages], refs[n_messages:-1], refs[-1]
        at = 0
        for ref in before_refs:
            out_ref[pl.ds(at, ref.shape[0])] = ref[...]
            at += ref.shape[0]
        own_head = get_head(own_in_ref, n_own)
        heads = [get_head(ref, size) for ref in in_refs]
        for i in range(size):
            total = own_ref[first + i] + get_tile(own_in_ref, first + i, own_head)
            for ref, head in zip(in_refs, heads):
                total += get_tile(ref, i, head)
            out_ref[at + i] = total.astype(out_ref.dtype)

    return kernel


def call(kernel, out_shape, smem, vmem, after=(), scratch=(), flops=0):
    outs = out_shape if isinstance(out_shape, (list, tuple)) else [out_shape]
    moved = sum(x.size * x.dtype.itemsize for x in (*smem, *vmem, *outs))
    n_real = len(smem) + len(vmem)

    def wrapped(*refs):
        kernel(*refs[:n_real], *refs[n_real + len(after) :])

    return pl.pallas_call(
        wrapped,
        out_shape=out_shape,
        in_specs=[pl.BlockSpec(memory_space=SMEM)] * len(smem)
        + [pl.BlockSpec(memory_space=VMEM)] * len(vmem)
        + [pl.BlockSpec(memory_space=pl.ANY)] * len(after),
        out_specs=jax.tree.map(lambda _: pl.BlockSpec(memory_space=VMEM), out_shape),
        scratch_shapes=list(scratch),
        compiler_params=pltpu.CompilerParams(vmem_limit_bytes=moved + 4 * 2**20),
        cost_estimate=pl.CostEstimate(flops=5 * flops, bytes_accessed=moved, transcendentals=0),
    )(*smem, *vmem, *after)


def hold(x, after):
    def kernel(*refs):
        pass

    return pl.pallas_call(
        kernel,
        out_shape=jax.ShapeDtypeStruct(x.shape, x.dtype),
        in_specs=[pl.BlockSpec(memory_space=pl.ANY)] * (1 + len(after)),
        out_specs=pl.BlockSpec(memory_space=pl.ANY),
        input_output_aliases={0: 0},
        compiler_params=pltpu.CompilerParams(vmem_limit_bytes=2**20),
    )(x, *after)


def on_device(a_tiles, p_tiles, pair_a, pair_p):
    a, p = a_tiles[0, 0, 0], p_tiles[0, 0, 0]
    ia, ip = jnp.swapaxes(pair_a[0, 0, 0], 1, 2), jnp.swapaxes(pair_p[0, 0, 0], 1, 2)
    fan, slots = ia.shape[1:]
    held, width = p.shape[0], p.shape[-1]
    layers = lax.axis_size("layer")
    bits = layers.bit_length() - 1
    count = slots // layers
    swap = [(0, 1), (1, 0)]

    half = count // 2
    chunks = [(0, half), (half, count - half)]
    flops = layers * half * fan * width**3

    def floats(size):
        return jax.ShapeDtypeStruct((size, width, width), jnp.float32)

    def exchange(x, bit):
        return lax.ppermute(x, "layer", [(i, i ^ (1 << bit)) for i in range(layers)])

    def cross(x, bit):
        flip = 0 if bit is None else 1 << bit
        perm = [(c * layers + i, (1 - c) * layers + (i ^ flip)) for c in range(2) for i in range(layers)]
        return lax.ppermute(x, ("col", "layer"), perm)

    def start(smem, vmem, chunk, bit, after):
        shapes = [message(layers // 2 * chunk[1], width), jax.ShapeDtypeStruct((2 * held, width, width), p.dtype)]
        return call(send_kernel(2, fan, count, chunk, bit), shapes, smem, vmem, after, (), flops)

    def send(smem, vmem, chunk, bit, after):
        shape = message(layers // 2 * chunk[1], width)
        return call(send_kernel(1, fan, count, chunk, bit), shape, smem, vmem, after, (), flops)

    def keep(smem, vmem, bit, after):
        shapes = [floats(layers // 2 * size) for _, size in chunks]
        return call(keep_kernel(fan, count, chunks, bit), shapes, smem, vmem, after, (), 2 * flops)

    def add(kept, came, sizes, rest, bit, keeps, after):
        n = sum(sizes) << (len(rest) - 1)
        shapes = [message(n, width), floats(n) if keeps else message(n, width)]
        return call(add_kernel(sizes, rest, bit, keeps), shapes, (), (*kept, *came), after)

    p_x = lax.ppermute(p, "col", swap)
    p_r = lax.ppermute(p, "row", swap)
    col = lax.axis_index("col")
    lists = jnp.concatenate([ia[col], ip[col]], axis=0)
    lists_x = lax.ppermute(jnp.concatenate([ia[1 - col], ip[1 - col]], axis=0), "col", swap)
    own_bits = [*range(bits)]
    gate = call(lambda *refs: None, jax.ShapeDtypeStruct((8, width), jnp.float32), (lists,), (a, p))
    smem, bit = (lists,), own_bits[0]
    made, joined = start(smem, (a, p, p_r), chunks[0], bit, (gate,))
    own_sent = [exchange(made, bit)]
    made = send(smem, (a, joined), chunks[1], bit, (made,))
    own_sent.append(exchange(made, bit))
    own_kept = keep(smem, (a, joined), bit, (made,))

    p_x = hold(p_x, (own_kept[0], own_sent[0], lists_x))
    p_xr = lax.ppermute(p_x, "row", swap)

    smem, bit = (lists_x,), 0
    made, joined = start(smem, (a, p_x, p_xr), chunks[0], bit, ())
    other_sent = [exchange(made, bit)]
    made = send(smem, (a, joined), chunks[1], bit, (made,))
    other_sent.append(exchange(made, bit))
    rest = sorted(own_bits[1:])
    sent, own_kept = add(own_kept, own_sent, [s for _, s in chunks], rest, own_bits[1], True, (made,))
    own_sent = exchange(sent, own_bits[1])
    other_kept = keep(smem, (a, joined), bit, (sent,))

    streams = [(other_kept[n], other_sent[n]) for n in range(len(chunks))]
    rest = list(range(1, bits))
    after = ()
    for b in range(1, bits - 1):
        for n, (kept, came) in enumerate(streams):
            sent, kept = add((kept,), (came,), [chunks[n][1]], rest, b, True, after)
            after = (sent,)
            streams[n] = (kept, exchange(sent, b))
            if n == 0 and len(own_bits) > 2:
                own_rest = sorted(own_bits[2:])
                sent, own_kept = add((own_kept,), (own_sent,), [count], own_rest, own_bits[2], True, after)
                own_sent = exchange(sent, own_bits[2])
                own_bits = own_bits[:2] + own_bits[3:]
                after = (sent,)
        rest.remove(b)
    for b in own_bits[2:]:
        own_rest = sorted(own_bits[own_bits.index(b) :])
        sent, own_kept = add((own_kept,), (own_sent,), [count], own_rest, b, True, after)
        own_sent = exchange(sent, b)
        after = (sent,)

    moved = []
    for n, (kept, came) in enumerate(streams):
        sent, stay = add((kept,), (came,), [chunks[n][1]], rest, rest[0], False, after)
        after = (sent,)
        moved.append((cross(sent, rest[0]), cross(stay, None)))
    result = ()
    for n, (first, size) in enumerate(chunks):
        final = n == len(chunks) - 1
        shape = jax.ShapeDtypeStruct((count if final else size, width, width), jnp.bfloat16)
        kernel = last_kernel(first, size, count, len(moved[n]), len(result))
        result = (call(kernel, shape, (), (own_kept, own_sent, *moved[n], *result)),)
    return result[0][None, None]


def solution(mesh):
    spec = P("row", "col", "layer", None, None, None)
    return jax.shard_map(
        on_device,
        mesh=mesh,
        in_specs=(spec,) * 4,
        out_specs=P("row", "col", "layer", None, None),
        check_vma=False,
    )
```

```python
import jax
import jax.numpy as jnp
from jax import lax
from jax.experimental import pallas as pl
from jax.experimental.pallas import tpu as pltpu
from jax.sharding import PartitionSpec as P

PEAK = 32766.0
ROWS = 16
GROUP = 4
SMEM = pltpu.MemorySpace.SMEM
VMEM = pltpu.MemorySpace.VMEM


def head_rows(count):
    return -(-count // ROWS) * ROWS


def message(count, width):
    return jax.ShapeDtypeStruct((count * width + head_rows(count), width), jnp.int16)


def encode(tile):
    top = jnp.max(jnp.abs(tile), axis=0, keepdims=True)
    power = jnp.floor(jnp.log2(jnp.maximum(top, 2.0**-100)) + 0.001) + 1.0
    scaled = jnp.round(tile * (jnp.exp2(-power) * PEAK))
    return scaled.astype(jnp.int32).astype(jnp.int16), power.astype(jnp.int32)


def new_head(count, width):
    return jnp.zeros((head_rows(count), width), jnp.int32)


def rows_at(slot, width):
    start = slot * width
    return pl.ds(start if isinstance(start, int) else pl.multiple_of(start, width), width)


def put_tile(ref, slot, tile, head):
    coded, power = encode(tile)
    ref[rows_at(slot, tile.shape[0]), :] = coded
    rows = lax.broadcasted_iota(jnp.int32, head.shape, 0)
    return jnp.where(rows == slot, power, head)


def put_head(ref, head):
    ref[pl.ds(ref.shape[0] - head.shape[0], head.shape[0]), :] = head.astype(jnp.int16)


def get_head(ref, count):
    rows = head_rows(count)
    return ref[pl.ds(ref.shape[0] - rows, rows), :].astype(jnp.int32)


def get_tile(ref, slot, head):
    rows = lax.broadcasted_iota(jnp.int32, head.shape, 0)
    power = jnp.sum(jnp.where(rows == slot, head, 0), axis=0, keepdims=True)
    coded = ref[rows_at(slot, ref.shape[-1]), :]
    return coded.astype(jnp.int32).astype(jnp.float32) * (jnp.exp2(power.astype(jnp.float32)) * (1.0 / PEAK))


def product(a_ref, p_ref, look, fan):
    chosen = [look(f) for f in range(fan)]
    left = jnp.concatenate([a_ref[pa] for pa, _ in chosen], axis=1)
    right = jnp.concatenate([p_ref[pp] for _, pp in chosen], axis=0)
    return jnp.dot(left, right, preferred_element_type=jnp.float32)


def own_bit(bit):
    return (lax.axis_index("layer") >> bit) & 1


def insert(rest, at, bit):
    low = rest & ((1 << at) - 1)
    return ((rest >> at) << (at + 1)) | (bit << at) | low


def finder(lists_ref, fan):
    return lambda t: lambda f: (lists_ref[f, t], lists_ref[fan + f, t])


def send_kernel(n_p, fan, count, chunk, bit):
    first, size = chunk

    def kernel(lists_ref, a_ref, *refs):
        find = finder(lists_ref, fan)
        p_refs, out_ref = refs[:n_p], refs[n_p]
        width = out_ref.shape[-1]
        if n_p == 2:
            p_ref = refs[-1]
            held = p_refs[0].shape[0]
            row = lax.axis_index("row")
            p_ref[pl.ds(row * held, held)] = p_refs[0][...]
            p_ref[pl.ds((1 - row) * held, held)] = p_refs[1][...]
        else:
            (p_ref,) = p_refs
        side = 1 - own_bit(bit)
        total = out_ref.shape[0] // width

        def body(step, head):
            for k in range(GROUP):
                slot = step * GROUP + k
                layer = insert(slot // size, bit, side)
                tile = product(a_ref, p_ref, find(layer * count + first + slot % size), fan)
                head = put_tile(out_ref, slot, tile, head)
            return head

        put_head(out_ref, lax.fori_loop(0, total // GROUP, body, new_head(total, width)))

    return kernel


def keep_kernel(fan, count, chunks, bits):
    def kernel(lists_ref, a_ref, p_ref, *out_refs):
        find = finder(lists_ref, fan)
        for (first, size), bit, out_ref in zip(chunks, bits, out_refs):
            side = own_bit(bit)

            def body(step, _):
                for k in range(GROUP):
                    slot = step * GROUP + k
                    layer = insert(slot // size, bit, side)
                    out_ref[slot] = product(a_ref, p_ref, find(layer * count + first + slot % size), fan)
                return 0

            lax.fori_loop(0, out_ref.shape[0] // GROUP, body, 0)

    return kernel


def add_kernel(sizes, rest, bit, keeps):
    at = rest.index(bit)
    full = sum(sizes)
    halves = 1 << (len(rest) - 1)

    def kernel(*refs):
        n = len(sizes)
        kept_refs, in_refs, (sent_ref, stay_ref) = refs[:n], refs[n : 2 * n], refs[2 * n : 2 * n + 2]
        width = sent_ref.shape[-1]
        mine = own_bit(bit)
        heads = [get_head(ref, ref.shape[0] // width) for ref in in_refs]

        def sums(place):
            for size, kept_ref, in_ref, head in zip(sizes, kept_refs, in_refs, heads):
                for i in range(size):
                    slot = place * size + i
                    yield kept_ref[slot] + get_tile(in_ref, slot, head)

        def send(ref, side):
            def body(half, head):
                for i, tile in enumerate(sums(insert(half, at, side))):
                    head = put_tile(ref, half * full + i, tile, head)
                return head

            put_head(ref, lax.fori_loop(0, halves, body, new_head(halves * full, width), unroll=halves <= 4))

        send(sent_ref, 1 - mine)
        if keeps:

            def body(half, _):
                for i, tile in enumerate(sums(insert(half, at, mine))):
                    stay_ref[half * full + i] = tile
                return 0

            lax.fori_loop(0, halves, body, 0, unroll=halves <= 4)
        else:
            send(stay_ref, mine)

    return kernel


def last_kernel(first, size, n_own, n_messages, n_before):
    def kernel(own_ref, own_in_ref, *refs):
        in_refs, before_refs, out_ref = refs[:n_messages], refs[n_messages:-1], refs[-1]
        at = 0
        for ref in before_refs:
            out_ref[pl.ds(at, ref.shape[0])] = ref[...]
            at += ref.shape[0]
        own_head = get_head(own_in_ref, n_own)
        heads = [get_head(ref, size) for ref in in_refs]
        for i in range(size):
            total = own_ref[first + i] + get_tile(own_in_ref, first + i, own_head)
            for ref, head in zip(in_refs, heads):
                total += get_tile(ref, i, head)
            out_ref[at + i] = total.astype(out_ref.dtype)

    return kernel


def call(kernel, out_shape, smem, vmem, after=(), scratch=(), flops=0):
    outs = out_shape if isinstance(out_shape, (list, tuple)) else [out_shape]
    moved = sum(x.size * x.dtype.itemsize for x in (*smem, *vmem, *outs))
    n_real = len(smem) + len(vmem)

    def wrapped(*refs):
        kernel(*refs[:n_real], *refs[n_real + len(after) :])

    return pl.pallas_call(
        wrapped,
        out_shape=out_shape,
        in_specs=[pl.BlockSpec(memory_space=SMEM)] * len(smem)
        + [pl.BlockSpec(memory_space=VMEM)] * len(vmem)
        + [pl.BlockSpec(memory_space=pl.ANY)] * len(after),
        out_specs=jax.tree.map(lambda _: pl.BlockSpec(memory_space=VMEM), out_shape),
        scratch_shapes=list(scratch),
        compiler_params=pltpu.CompilerParams(vmem_limit_bytes=moved + 4 * 2**20),
        cost_estimate=pl.CostEstimate(flops=5 * flops, bytes_accessed=moved, transcendentals=0),
    )(*smem, *vmem, *after)


def hold(x, after):
    def kernel(*refs):
        pass

    return pl.pallas_call(
        kernel,
        out_shape=jax.ShapeDtypeStruct(x.shape, x.dtype),
        in_specs=[pl.BlockSpec(memory_space=pl.ANY)] * (1 + len(after)),
        out_specs=pl.BlockSpec(memory_space=pl.ANY),
        input_output_aliases={0: 0},
        compiler_params=pltpu.CompilerParams(vmem_limit_bytes=2**20),
    )(x, *after)


def on_device(a_tiles, p_tiles, pair_a, pair_p):
    a, p = a_tiles[0, 0, 0], p_tiles[0, 0, 0]
    ia, ip = jnp.swapaxes(pair_a[0, 0, 0], 1, 2), jnp.swapaxes(pair_p[0, 0, 0], 1, 2)
    fan, slots = ia.shape[1:]
    held, width = p.shape[0], p.shape[-1]
    layers = lax.axis_size("layer")
    bits = layers.bit_length() - 1
    count = slots // layers
    swap = [(0, 1), (1, 0)]

    half = count // 2
    chunks = [(0, half), (half, count - half)]
    flops = layers * half * fan * width**3

    def floats(size):
        return jax.ShapeDtypeStruct((size, width, width), jnp.float32)

    def exchange(x, bit):
        return lax.ppermute(x, "layer", [(i, i ^ (1 << bit)) for i in range(layers)])

    def cross(x, bit):
        flip = 0 if bit is None else 1 << bit
        perm = [(c * layers + i, (1 - c) * layers + (i ^ flip)) for c in range(2) for i in range(layers)]
        return lax.ppermute(x, ("col", "layer"), perm)

    def start(lists, vmem, n, after):
        shapes = [message(layers // 2 * chunks[n][1], width), jax.ShapeDtypeStruct((2 * held, width, width), p.dtype)]
        return call(send_kernel(2, fan, count, chunks[n], first_bits[n]), shapes, (lists,), vmem, after, (), flops)

    def send(lists, vmem, n, after):
        shape = message(layers // 2 * chunks[n][1], width)
        return call(send_kernel(1, fan, count, chunks[n], first_bits[n]), shape, (lists,), vmem, after, (), flops)

    def keep(lists, vmem, after):
        shapes = [floats(layers // 2 * size) for _, size in chunks]
        kernel = keep_kernel(fan, count, chunks, first_bits)
        return call(kernel, shapes, (lists,), vmem, after, (), 2 * flops)

    def add(parts, sizes, rest, bit, keeps, after):
        n = sum(sizes) << (len(rest) - 1)
        shapes = [message(n, width), floats(n) if keeps else message(n, width)]
        kept, came = zip(*parts)
        return call(add_kernel(sizes, rest, bit, keeps), shapes, (), (*kept, *came), after)

    first_bits = (0, 1)
    sizes = [size for _, size in chunks]
    every = list(range(bits))

    def less(rest, bit):
        return [b for b in rest if b != bit]

    p_x = lax.ppermute(p, "col", swap)
    p_r = lax.ppermute(p, "row", swap)
    col = lax.axis_index("col")
    lists = jnp.concatenate([ia[col], ip[col]], axis=0)
    lists_x = lax.ppermute(jnp.concatenate([ia[1 - col], ip[1 - col]], axis=0), "col", swap)

    token = jax.ShapeDtypeStruct((8, width), jnp.float32)
    gate = call(lambda *refs: None, token, (), (), (), (), 10**9)
    gate = call(lambda *refs: None, token, (), (a, p), (gate,))

    made, joined = start(lists, (a, p, p_r), 0, (gate,))
    own_came = [exchange(made, first_bits[0])]
    made = send(lists, (a, joined), 1, (made,))
    own_came.append(exchange(made, first_bits[1]))
    own_kept = keep(lists, (a, joined), (made,))
    p_x = hold(p_x, (own_kept[0], own_came[0], lists_x))
    p_xr = lax.ppermute(p_x, "row", swap)

    def own_second(n, after):
        b, other = first_bits[n], first_bits[1 - n]
        sent, kept = add([(own_kept[n], own_came[n])], [sizes[n]], less(every, b), other, True, after)
        return sent, (kept, exchange(sent, other))

    sent, part_0 = own_second(0, ())

    made, joined = start(lists_x, (a, p_x, p_xr), 0, (sent,))
    other_came = [exchange(made, first_bits[0])]
    made = send(lists_x, (a, joined), 1, (made,))
    other_came.append(exchange(made, first_bits[1]))
    sent, part_1 = own_second(1, (made,))
    other_kept = keep(lists_x, (a, joined), (sent,))

    streams, after = [], (other_kept[0],)
    for n in range(2):
        b, other = first_bits[n], first_bits[1 - n]
        sent, kept = add([(other_kept[n], other_came[n])], [sizes[n]], less(every, b), other, True, after)
        after = (sent,)
        streams.append((kept, exchange(sent, other)))
    rest = every[2:]
    parts, part_sizes = [part_0, part_1], sizes
    for b in every[2:]:
        sent, kept = add(parts, part_sizes, rest, b, True, after)
        after = (sent,)
        parts, part_sizes = [(kept, exchange(sent, b))], [count]
        rest = less(rest, b)
    (own,) = parts
    rest = every[2:]
    for b in every[2:-1]:
        for n in range(2):
            sent, kept = add([streams[n]], [sizes[n]], rest, b, True, after)
            after = (sent,)
            streams[n] = (kept, exchange(sent, b))
        rest = less(rest, b)

    moved = []
    for n in range(2):
        sent, stay = add([streams[n]], [sizes[n]], rest, rest[0], False, after)
        after = (sent,)
        moved.append((cross(sent, rest[0]), cross(stay, None)))
    result = ()
    for n, (first, size) in enumerate(chunks):
        final = n == len(chunks) - 1
        shape = jax.ShapeDtypeStruct((count if final else size, width, width), jnp.bfloat16)
        kernel = last_kernel(first, size, count, len(moved[n]), len(result))
        result = (call(kernel, shape, (), (*own, *moved[n], *result)),)
    return result[0][None, None]


def solution(mesh):
    spec = P("row", "col", "layer", None, None, None)
    return jax.shard_map(
        on_device,
        mesh=mesh,
        in_specs=(spec,) * 4,
        out_specs=P("row", "col", "layer", None, None),
        check_vma=False,
    )
```

```python
import jax
import jax.numpy as jnp
from jax import lax
from jax.experimental import pallas as pl
from jax.experimental.pallas import tpu as pltpu
from jax.sharding import PartitionSpec as P

PEAK = 32766.0
ROWS = 16
GROUP = 8
SMEM = pltpu.MemorySpace.SMEM
VMEM = pltpu.MemorySpace.VMEM


def head_rows(count):
    return -(-count // ROWS) * ROWS


def message(count, width):
    return jax.ShapeDtypeStruct((count * width + head_rows(count), width), jnp.int16)


def encode(tile):
    top = jnp.max(jnp.abs(tile), axis=0, keepdims=True)
    power = jnp.floor(jnp.log2(jnp.maximum(top, 2.0**-100)) + 0.001) + 1.0
    scaled = jnp.round(tile * (jnp.exp2(-power) * PEAK))
    return scaled.astype(jnp.int32).astype(jnp.int16), power.astype(jnp.int32)


def new_head(count, width):
    return jnp.zeros((head_rows(count), width), jnp.int32)


def rows_at(slot, width):
    start = slot * width
    return pl.ds(start if isinstance(start, int) else pl.multiple_of(start, width), width)


def put_tile(ref, slot, tile, head):
    coded, power = encode(tile)
    ref[rows_at(slot, tile.shape[0]), :] = coded
    rows = lax.broadcasted_iota(jnp.int32, head.shape, 0)
    return jnp.where(rows == slot, power, head)


def put_head(ref, head):
    ref[pl.ds(ref.shape[0] - head.shape[0], head.shape[0]), :] = head.astype(jnp.int16)


def get_head(ref, count):
    rows = head_rows(count)
    return ref[pl.ds(ref.shape[0] - rows, rows), :].astype(jnp.int32)


def get_tile(ref, slot, head):
    rows = lax.broadcasted_iota(jnp.int32, head.shape, 0)
    power = jnp.sum(jnp.where(rows == slot, head, 0), axis=0, keepdims=True)
    coded = ref[rows_at(slot, ref.shape[-1]), :]
    return coded.astype(jnp.int32).astype(jnp.float32) * (jnp.exp2(power.astype(jnp.float32)) * (1.0 / PEAK))


def product(a_ref, p_ref, look, fan):
    chosen = [look(f) for f in range(fan)]
    left = jnp.concatenate([a_ref[pa] for pa, _ in chosen], axis=1)
    right = jnp.concatenate([p_ref[pp] for _, pp in chosen], axis=0)
    return jnp.dot(left, right, preferred_element_type=jnp.float32)


def own_bit(bit):
    return (lax.axis_index("layer") >> bit) & 1


def insert(rest, at, bit):
    low = rest & ((1 << at) - 1)
    return ((rest >> at) << (at + 1)) | (bit << at) | low


def finder(lists_ref, fan):
    return lambda t: lambda f: (lists_ref[f, t], lists_ref[fan + f, t])


def send_kernel(fan, count, chunks, bits):
    def kernel(lists_ref, a_ref, p0_ref, p1_ref, *refs):
        find = finder(lists_ref, fan)
        out_refs, p_ref = refs[:-1], refs[-1]
        held, width = p0_ref.shape[:2]
        row = lax.axis_index("row")
        p_ref[pl.ds(row * held, held)] = p0_ref[...]
        p_ref[pl.ds((1 - row) * held, held)] = p1_ref[...]
        for (first, size), bit, out_ref in zip(chunks, bits, out_refs):
            side = 1 - own_bit(bit)
            total = out_ref.shape[0] // width

            def body(step, head):
                for k in range(GROUP):
                    slot = step * GROUP + k
                    layer = insert(slot // size, bit, side)
                    tile = product(a_ref, p_ref, find(layer * count + first + slot % size), fan)
                    head = put_tile(out_ref, slot, tile, head)
                return head

            put_head(out_ref, lax.fori_loop(0, total // GROUP, body, new_head(total, width)))

    return kernel


def keep_kernel(fan, count, chunks, bits):
    def kernel(lists_ref, a_ref, p_ref, *out_refs):
        find = finder(lists_ref, fan)
        for (first, size), bit, out_ref in zip(chunks, bits, out_refs):
            side = own_bit(bit)

            def body(step, _):
                for k in range(GROUP):
                    slot = step * GROUP + k
                    layer = insert(slot // size, bit, side)
                    out_ref[slot] = product(a_ref, p_ref, find(layer * count + first + slot % size), fan)
                return 0

            lax.fori_loop(0, out_ref.shape[0] // GROUP, body, 0)

    return kernel


def add_kernel(sizes, rest, bit, keeps):
    at = rest.index(bit)
    full = sum(sizes)
    halves = 1 << (len(rest) - 1)

    def kernel(*refs):
        n = len(sizes)
        kept_refs, in_refs, (sent_ref, stay_ref) = refs[:n], refs[n : 2 * n], refs[2 * n : 2 * n + 2]
        width = sent_ref.shape[-1]
        mine = own_bit(bit)
        heads = [get_head(ref, ref.shape[0] // width) for ref in in_refs]

        def sums(place):
            for size, kept_ref, in_ref, head in zip(sizes, kept_refs, in_refs, heads):
                for i in range(size):
                    slot = place * size + i
                    yield kept_ref[slot] + get_tile(in_ref, slot, head)

        def send(ref, side):
            def body(half, head):
                for i, tile in enumerate(sums(insert(half, at, side))):
                    head = put_tile(ref, half * full + i, tile, head)
                return head

            put_head(ref, lax.fori_loop(0, halves, body, new_head(halves * full, width), unroll=halves <= 4))

        send(sent_ref, 1 - mine)
        if keeps:

            def body(half, _):
                for i, tile in enumerate(sums(insert(half, at, mine))):
                    stay_ref[half * full + i] = tile
                return 0

            lax.fori_loop(0, halves, body, 0, unroll=halves <= 4)
        else:
            send(stay_ref, mine)

    return kernel


def sum_kernel(kept_ref, in_ref, out_ref):
    count = out_ref.shape[0]
    head = get_head(in_ref, count)
    for i in range(count):
        out_ref[i] = kept_ref[i] + get_tile(in_ref, i, head)


def last_kernel(first, size, n_messages, n_before):
    def kernel(own_ref, *refs):
        in_refs, before_refs, out_ref = refs[:n_messages], refs[n_messages:-1], refs[-1]
        at = 0
        for ref in before_refs:
            out_ref[pl.ds(at, ref.shape[0])] = ref[...]
            at += ref.shape[0]
        heads = [get_head(ref, size) for ref in in_refs]
        for i in range(size):
            total = own_ref[first + i]
            for ref, head in zip(in_refs, heads):
                total += get_tile(ref, i, head)
            out_ref[at + i] = total.astype(out_ref.dtype)

    return kernel


def call(kernel, out_shape, smem, vmem, after=(), scratch=(), flops=0):
    outs = out_shape if isinstance(out_shape, (list, tuple)) else [out_shape]
    moved = sum(x.size * x.dtype.itemsize for x in (*smem, *vmem, *outs))
    n_real = len(smem) + len(vmem)

    def wrapped(*refs):
        kernel(*refs[:n_real], *refs[n_real + len(after) :])

    return pl.pallas_call(
        wrapped,
        out_shape=out_shape,
        in_specs=[pl.BlockSpec(memory_space=SMEM)] * len(smem)
        + [pl.BlockSpec(memory_space=VMEM)] * len(vmem)
        + [pl.BlockSpec(memory_space=pl.ANY)] * len(after),
        out_specs=jax.tree.map(lambda _: pl.BlockSpec(memory_space=VMEM), out_shape),
        scratch_shapes=list(scratch),
        compiler_params=pltpu.CompilerParams(vmem_limit_bytes=moved + 4 * 2**20),
        cost_estimate=pl.CostEstimate(flops=5 * flops, bytes_accessed=moved, transcendentals=0),
    )(*smem, *vmem, *after)


def hold(x, after):
    def kernel(*refs):
        pass

    return pl.pallas_call(
        kernel,
        out_shape=jax.ShapeDtypeStruct(x.shape, x.dtype),
        in_specs=[pl.BlockSpec(memory_space=pl.ANY)] * (1 + len(after)),
        out_specs=pl.BlockSpec(memory_space=pl.ANY),
        input_output_aliases={0: 0},
        compiler_params=pltpu.CompilerParams(vmem_limit_bytes=2**20),
    )(x, *after)


def on_device(a_tiles, p_tiles, pair_a, pair_p):
    a, p = a_tiles[0, 0, 0], p_tiles[0, 0, 0]
    ia, ip = jnp.swapaxes(pair_a[0, 0, 0], 1, 2), jnp.swapaxes(pair_p[0, 0, 0], 1, 2)
    fan, slots = ia.shape[1:]
    held, width = p.shape[0], p.shape[-1]
    layers = lax.axis_size("layer")
    bits = layers.bit_length() - 1
    count = slots // layers
    swap = [(0, 1), (1, 0)]

    half = count // 2
    chunks = [(0, half), (half, count - half)]
    flops = layers * half * fan * width**3

    def floats(size):
        return jax.ShapeDtypeStruct((size, width, width), jnp.float32)

    def exchange(x, bit):
        return lax.ppermute(x, "layer", [(i, i ^ (1 << bit)) for i in range(layers)])

    def cross(x, bit):
        flip = 0 if bit is None else 1 << bit
        perm = [(c * layers + i, (1 - c) * layers + (i ^ flip)) for c in range(2) for i in range(layers)]
        return lax.ppermute(x, ("col", "layer"), perm)

    def send(lists, vmem, after):
        shapes = [message(layers // 2 * size, width) for _, size in chunks]
        shapes.append(jax.ShapeDtypeStruct((2 * held, width, width), p.dtype))
        *made, joined = call(send_kernel(fan, count, chunks, first_bits), shapes, (lists,), vmem, after, (), 2 * flops)
        return made, joined, [exchange(x, b) for x, b in zip(made, first_bits)]

    def keep(lists, vmem, after):
        shapes = [floats(layers // 2 * size) for _, size in chunks]
        kernel = keep_kernel(fan, count, chunks, first_bits)
        return call(kernel, shapes, (lists,), vmem, after, (), 2 * flops)

    def add(parts, sizes, rest, bit, keeps, after):
        n = sum(sizes) << (len(rest) - 1)
        shapes = [message(n, width), floats(n) if keeps else message(n, width)]
        kept, came = zip(*parts)
        return call(add_kernel(sizes, rest, bit, keeps), shapes, (), (*kept, *came), after)

    first_bits = (0, 1)
    sizes = [size for _, size in chunks]
    every = list(range(bits))

    def less(rest, bit):
        return [b for b in rest if b != bit]

    p_x = lax.ppermute(p, "col", swap)
    p_r = lax.ppermute(p, "row", swap)
    col = lax.axis_index("col")
    lists = jnp.concatenate([ia[col], ip[col]], axis=0)
    lists_far = jnp.concatenate([ia[1 - col], ip[1 - col]], axis=0)

    token = jax.ShapeDtypeStruct((8, width), jnp.float32)
    gate = call(lambda *refs: None, token, (), (), (), (), 10**9)
    gate = call(lambda *refs: None, token, (), (a, p), (gate,))

    made, joined, own_came = send(lists, (a, p, p_r), (gate,))
    lists_x = lax.ppermute(hold(lists_far, made[:1]), "col", swap)
    own_kept = keep(lists, (a, joined), made[:1])
    parts, after = [], ()
    for n in range(2):
        b, other = first_bits[n], first_bits[1 - n]
        sent, kept = add([(own_kept[n], own_came[n])], [sizes[n]], less(every, b), other, True, after)
        after = (sent,)
        parts.append((kept, exchange(sent, other)))
    p_x = hold(p_x, (*after, lists_x))
    p_xr = lax.ppermute(p_x, "row", swap)

    made, joined, other_came = send(lists_x, (a, p_x, p_xr), ())
    rest, part_sizes, after = every[2:], sizes, made[:1]
    for b in every[2:]:
        sent, kept = add(parts, part_sizes, rest, b, True, after)
        after = (sent,)
        parts, part_sizes = [(kept, exchange(sent, b))], [count]
        rest = less(rest, b)
    (own,) = parts
    other_kept = keep(lists_x, (a, joined), after)

    streams, after = [], (other_kept[0],)
    for n in range(2):
        b, other = first_bits[n], first_bits[1 - n]
        sent, kept = add([(other_kept[n], other_came[n])], [sizes[n]], less(every, b), other, True, after)
        after = (sent,)
        streams.append((kept, exchange(sent, other)))
    rest = every[2:]
    for b in every[2:-1]:
        for n in range(2):
            sent, kept = add([streams[n]], [sizes[n]], rest, b, True, after)
            after = (sent,)
            streams[n] = (kept, exchange(sent, b))
        rest = less(rest, b)

    own = call(sum_kernel, floats(count), (), own, after)
    moved, after = [], (own,)
    for n in range(2):
        sent, stay = add([streams[n]], [sizes[n]], rest, rest[0], False, after)
        after = (sent,)
        moved.append((cross(sent, rest[0]), cross(stay, None)))
    result = ()
    for n, (first, size) in enumerate(chunks):
        final = n == len(chunks) - 1
        shape = jax.ShapeDtypeStruct((count if final else size, width, width), jnp.bfloat16)
        kernel = last_kernel(first, size, len(moved[n]), len(result))
        result = (call(kernel, shape, (), (own, *moved[n], *result)),)
    return result[0][None, None]


def solution(mesh):
    spec = P("row", "col", "layer", None, None, None)
    return jax.shard_map(
        on_device,
        mesh=mesh,
        in_specs=(spec,) * 4,
        out_specs=P("row", "col", "layer", None, None),
        check_vma=False,
    )
```

```python
import jax
import jax.numpy as jnp
from jax import lax
from jax.experimental import pallas as pl
from jax.experimental.pallas import tpu as pltpu
from jax.sharding import PartitionSpec as P

PEAK = 32766.0
ROWS = 16
GROUP = 8
SMEM = pltpu.MemorySpace.SMEM
VMEM = pltpu.MemorySpace.VMEM


def head_rows(count):
    return -(-count // ROWS) * ROWS


def message(count, width):
    return jax.ShapeDtypeStruct((count * width + head_rows(count), width), jnp.int16)


def encode(tile):
    top = jnp.max(jnp.abs(tile), axis=0, keepdims=True)
    power = jnp.floor(jnp.log2(jnp.maximum(top, 2.0**-100)) + 0.001) + 1.0
    scaled = jnp.round(tile * (jnp.exp2(-power) * PEAK))
    return scaled.astype(jnp.int32).astype(jnp.int16), power.astype(jnp.int32)


def new_head(count, width):
    return jnp.zeros((head_rows(count), width), jnp.int32)


def rows_at(slot, width):
    start = slot * width
    return pl.ds(start if isinstance(start, int) else pl.multiple_of(start, width), width)


def put_tile(ref, slot, tile, head):
    coded, power = encode(tile)
    ref[rows_at(slot, tile.shape[0]), :] = coded
    rows = lax.broadcasted_iota(jnp.int32, head.shape, 0)
    return jnp.where(rows == slot, power, head)


def put_head(ref, head):
    ref[pl.ds(ref.shape[0] - head.shape[0], head.shape[0]), :] = head.astype(jnp.int16)


def get_head(ref, count):
    rows = head_rows(count)
    return ref[pl.ds(ref.shape[0] - rows, rows), :].astype(jnp.int32)


def get_tile(ref, slot, head):
    rows = lax.broadcasted_iota(jnp.int32, head.shape, 0)
    power = jnp.sum(jnp.where(rows == slot, head, 0), axis=0, keepdims=True)
    coded = ref[rows_at(slot, ref.shape[-1]), :]
    return coded.astype(jnp.int32).astype(jnp.float32) * (jnp.exp2(power.astype(jnp.float32)) * (1.0 / PEAK))


def product(a_ref, p_ref, look, fan):
    chosen = [look(f) for f in range(fan)]
    left = jnp.concatenate([a_ref[pa] for pa, _ in chosen], axis=1)
    right = jnp.concatenate([p_ref[pp] for _, pp in chosen], axis=0)
    return jnp.dot(left, right, preferred_element_type=jnp.float32)


def own_bit(bit):
    return (lax.axis_index("layer") >> bit) & 1


def insert(rest, at, bit):
    low = rest & ((1 << at) - 1)
    return ((rest >> at) << (at + 1)) | (bit << at) | low


def finder(lists_ref, fan):
    return lambda t: lambda f: (lists_ref[f, t], lists_ref[fan + f, t])


def send_kernel(fan, count, chunks, bits, joins):
    def kernel(lists_ref, a_ref, *refs):
        find = finder(lists_ref, fan)
        n_out = len(chunks) + joins
        p_refs, out_refs = refs[:-n_out], refs[-n_out:]
        if joins:
            out_refs, p_ref = out_refs[:-1], out_refs[-1]
            held = p_ref.shape[0] // 2
            row = lax.axis_index("row")
            p_ref[pl.ds(row * held, held)] = p_refs[0][...]
            at = (1 - row) * held
            for ref in p_refs[1:]:
                p_ref[pl.ds(at, ref.shape[0])] = ref[...]
                at += ref.shape[0]
        else:
            (p_ref,) = p_refs
        width = p_ref.shape[-1]
        for (first, size), bit, out_ref in zip(chunks, bits, out_refs):
            side = 1 - own_bit(bit)
            total = out_ref.shape[0] // width

            def body(step, head):
                for k in range(GROUP):
                    slot = step * GROUP + k
                    layer = insert(slot // size, bit, side)
                    tile = product(a_ref, p_ref, find(layer * count + first + slot % size), fan)
                    head = put_tile(out_ref, slot, tile, head)
                return head

            put_head(out_ref, lax.fori_loop(0, total // GROUP, body, new_head(total, width)))

    return kernel


def split_kernel(in_ref, *out_refs):
    at = 0
    for ref in out_refs:
        ref[...] = in_ref[pl.ds(at, ref.shape[0])]
        at += ref.shape[0]


def keep_kernel(fan, count, chunks, bits):
    def kernel(lists_ref, a_ref, p_ref, *out_refs):
        find = finder(lists_ref, fan)
        for (first, size), bit, out_ref in zip(chunks, bits, out_refs):
            side = own_bit(bit)

            def body(step, _):
                for k in range(GROUP):
                    slot = step * GROUP + k
                    layer = insert(slot // size, bit, side)
                    out_ref[slot] = product(a_ref, p_ref, find(layer * count + first + slot % size), fan)
                return 0

            lax.fori_loop(0, out_ref.shape[0] // GROUP, body, 0)

    return kernel


def add_kernel(sizes, rest, bit, keeps):
    at = rest.index(bit)
    full = sum(sizes)
    halves = 1 << (len(rest) - 1)

    def kernel(*refs):
        n = len(sizes)
        kept_refs, in_refs, (sent_ref, stay_ref) = refs[:n], refs[n : 2 * n], refs[2 * n : 2 * n + 2]
        width = sent_ref.shape[-1]
        mine = own_bit(bit)
        heads = [get_head(ref, ref.shape[0] // width) for ref in in_refs]

        def sums(place):
            for size, kept_ref, in_ref, head in zip(sizes, kept_refs, in_refs, heads):
                for i in range(size):
                    slot = place * size + i
                    yield kept_ref[slot] + get_tile(in_ref, slot, head)

        def send(ref, side):
            def body(half, head):
                for i, tile in enumerate(sums(insert(half, at, side))):
                    head = put_tile(ref, half * full + i, tile, head)
                return head

            put_head(ref, lax.fori_loop(0, halves, body, new_head(halves * full, width), unroll=halves <= 4))

        send(sent_ref, 1 - mine)
        if keeps:

            def body(half, _):
                for i, tile in enumerate(sums(insert(half, at, mine))):
                    stay_ref[half * full + i] = tile
                return 0

            lax.fori_loop(0, halves, body, 0, unroll=halves <= 4)
        else:
            send(stay_ref, mine)

    return kernel


def sum_kernel(kept_ref, in_ref, out_ref):
    count = out_ref.shape[0]
    head = get_head(in_ref, count)
    for i in range(count):
        out_ref[i] = kept_ref[i] + get_tile(in_ref, i, head)


def last_kernel(first, size, n_messages, n_before):
    def kernel(own_ref, *refs):
        in_refs, before_refs, out_ref = refs[:n_messages], refs[n_messages:-1], refs[-1]
        at = 0
        for ref in before_refs:
            out_ref[pl.ds(at, ref.shape[0])] = ref[...]
            at += ref.shape[0]
        heads = [get_head(ref, size) for ref in in_refs]
        for i in range(size):
            total = own_ref[first + i]
            for ref, head in zip(in_refs, heads):
                total += get_tile(ref, i, head)
            out_ref[at + i] = total.astype(out_ref.dtype)

    return kernel


def call(kernel, out_shape, smem, vmem, after=(), scratch=(), flops=0):
    outs = out_shape if isinstance(out_shape, (list, tuple)) else [out_shape]
    moved = sum(x.size * x.dtype.itemsize for x in (*smem, *vmem, *outs))
    n_real = len(smem) + len(vmem)

    def wrapped(*refs):
        kernel(*refs[:n_real], *refs[n_real + len(after) :])

    return pl.pallas_call(
        wrapped,
        out_shape=out_shape,
        in_specs=[pl.BlockSpec(memory_space=SMEM)] * len(smem)
        + [pl.BlockSpec(memory_space=VMEM)] * len(vmem)
        + [pl.BlockSpec(memory_space=pl.ANY)] * len(after),
        out_specs=jax.tree.map(lambda _: pl.BlockSpec(memory_space=VMEM), out_shape),
        scratch_shapes=list(scratch),
        compiler_params=pltpu.CompilerParams(vmem_limit_bytes=moved + 4 * 2**20),
        cost_estimate=pl.CostEstimate(flops=5 * flops, bytes_accessed=moved if flops else 1, transcendentals=0),
    )(*smem, *vmem, *after)


def hold(x, after):
    def kernel(*refs):
        pass

    return pl.pallas_call(
        kernel,
        out_shape=jax.ShapeDtypeStruct(x.shape, x.dtype),
        in_specs=[pl.BlockSpec(memory_space=pl.ANY)] * (1 + len(after)),
        out_specs=pl.BlockSpec(memory_space=pl.ANY),
        input_output_aliases={0: 0},
        compiler_params=pltpu.CompilerParams(vmem_limit_bytes=2**20),
    )(x, *after)


def on_device(a_tiles, p_tiles, pair_a, pair_p):
    a, p = a_tiles[0, 0, 0], p_tiles[0, 0, 0]
    ia, ip = jnp.swapaxes(pair_a[0, 0, 0], 1, 2), jnp.swapaxes(pair_p[0, 0, 0], 1, 2)
    fan, slots = ia.shape[1:]
    held, width = p.shape[0], p.shape[-1]
    layers = lax.axis_size("layer")
    bits = layers.bit_length() - 1
    count = slots // layers
    swap = [(0, 1), (1, 0)]

    half = count // 2
    chunks = [(0, half), (half, count - half)]
    flops = layers * half * fan * width**3

    def floats(size):
        return jax.ShapeDtypeStruct((size, width, width), jnp.float32)

    def exchange(x, bit):
        return lax.ppermute(x, "layer", [(i, i ^ (1 << bit)) for i in range(layers)])

    def cross(x, bit):
        flip = 0 if bit is None else 1 << bit
        perm = [(c * layers + i, (1 - c) * layers + (i ^ flip)) for c in range(2) for i in range(layers)]
        return lax.ppermute(x, ("col", "layer"), perm)

    def send(lists, vmem, which, bits, joins, after, cost):
        picked = [chunks[n] for n in which]
        shapes = [message(layers // 2 * size, width) for _, size in picked]
        if joins:
            shapes.append(jax.ShapeDtypeStruct((2 * held, width, width), p.dtype))
        kernel = send_kernel(fan, count, picked, bits, joins)
        made = call(kernel, shapes, (lists,), vmem, after, (), cost * len(which) * flops)
        return made, [exchange(x, b) for x, b in zip(made, bits)]

    def keep(lists, vmem, bits, after, cost):
        shapes = [floats(layers // 2 * size) for _, size in chunks]
        kernel = keep_kernel(fan, count, chunks, bits)
        return call(kernel, shapes, (lists,), vmem, after, (), cost * 2 * flops)

    def add(parts, sizes, rest, bit, keeps, after):
        n = sum(sizes) << (len(rest) - 1)
        shapes = [message(n, width), floats(n) if keeps else message(n, width)]
        kept, came = zip(*parts)
        return call(add_kernel(sizes, rest, bit, keeps), shapes, (), (*kept, *came), after)

    own_bits, other_bits = (0, 1), (1, 0)
    sizes = [size for _, size in chunks]
    every = list(range(bits))

    def less(rest, bit):
        return [b for b in rest if b != bit]

    def second(kept, came, size, bit, after):
        sent, kept = add([(kept, came)], [size], less(every, bit), 1 - bit, True, after)
        return sent, (kept, exchange(sent, 1 - bit))

    p_x = lax.ppermute(p, "col", swap)
    p_r = lax.ppermute(p, "row", swap)
    col = lax.axis_index("col")
    lists = jnp.concatenate([ia[col], ip[col]], axis=0)
    lists_far = jnp.concatenate([ia[1 - col], ip[1 - col]], axis=0)

    token = jax.ShapeDtypeStruct((8, width), jnp.float32)
    gate = call(lambda *refs: None, token, (), (), (), (), 10**9)
    gate = call(lambda *refs: None, token, (), (a, p), (gate,))

    (*made, joined), own_came = send(lists, (a, p, p_r), (0, 1), own_bits, True, (gate,), 1)
    own_kept = keep(lists, (a, joined), own_bits, made[:1], 1)
    lists_x = lax.ppermute(hold(lists_far, own_kept[:1]), "col", swap)
    pieces = [jax.ShapeDtypeStruct((held // 2, width, width), p.dtype)] * 2
    pieces = call(split_kernel, pieces, (), (p_x,), (own_kept[0], lists_x))
    p_xr = [lax.ppermute(x, "row", swap) for x in pieces]
    parts, after = [], ()
    for n in range(2):
        sent, part = second(own_kept[n], own_came[n], sizes[n], own_bits[n], after)
        parts.append(part)
        after = (sent,)

    (made, joined), came_0 = send(lists_x, (a, p_x, *p_xr), (0,), other_bits[:1], True, after, 0)
    (made,), came_1 = send(lists_x, (a, joined), (1,), other_bits[1:], False, (made,), 0)
    other_came = came_0 + came_1
    rest, part_sizes, after = every[2:], sizes, (made,)
    for b in every[2:]:
        sent, kept = add(parts, part_sizes, rest, b, True, after)
        after = (sent,)
        parts, part_sizes = [(kept, exchange(sent, b))], [count]
        rest = less(rest, b)
    (own,) = parts
    other_kept = keep(lists_x, (a, joined), other_bits, after, 1)

    streams, after = [], (other_kept[0],)
    for n in range(2):
        sent, part = second(other_kept[n], other_came[n], sizes[n], other_bits[n], after)
        streams.append(part)
        after = (sent,)
    rest = every[2:]
    for b in every[2:-1]:
        for n in range(2):
            sent, kept = add([streams[n]], [sizes[n]], rest, b, True, after)
            after = (sent,)
            streams[n] = (kept, exchange(sent, b))
        rest = less(rest, b)

    own = call(sum_kernel, floats(count), (), own, after)
    moved, after = [], (own,)
    for n in range(2):
        sent, stay = add([streams[n]], [sizes[n]], rest, rest[0], False, after)
        after = (sent,)
        moved.append((cross(sent, rest[0]), cross(stay, None)))
    result = ()
    for n, (first, size) in enumerate(chunks):
        final = n == len(chunks) - 1
        shape = jax.ShapeDtypeStruct((count if final else size, width, width), jnp.bfloat16)
        kernel = last_kernel(first, size, len(moved[n]), len(result))
        result = (call(kernel, shape, (), (own, *moved[n], *result)),)
    return result[0][None, None]


def solution(mesh):
    spec = P("row", "col", "layer", None, None, None)
    return jax.shard_map(
        on_device,
        mesh=mesh,
        in_specs=(spec,) * 4,
        out_specs=P("row", "col", "layer", None, None),
        check_vma=False,
    )
```

```python
import jax
import jax.numpy as jnp
from jax import lax
from jax.experimental import pallas as pl
from jax.experimental.pallas import tpu as pltpu
from jax.sharding import PartitionSpec as P

PEAK = 32766.0
ROWS = 16
LANES = 128
GROUP = 8
SMEM = pltpu.MemorySpace.SMEM
VMEM = pltpu.MemorySpace.VMEM


def head_rows(count):
    return -(-count // ROWS) * ROWS


def message(count, width):
    return jax.ShapeDtypeStruct((count * width + head_rows(count), width), jnp.int16)


def encode(tile):
    top = jnp.max(jnp.abs(tile), axis=0, keepdims=True)
    power = jnp.floor(jnp.log2(jnp.maximum(top, 2.0**-100)) + 0.001) + 1.0
    scaled = jnp.round(tile * (jnp.exp2(-power) * PEAK))
    return scaled.astype(jnp.int32).astype(jnp.int16), power.astype(jnp.int32)


def new_head(count, width):
    return jnp.zeros((head_rows(count), width), jnp.int32)


def rows_at(slot, width):
    start = slot * width
    return pl.ds(start if isinstance(start, int) else pl.multiple_of(start, width), width)


def put_tile(ref, slot, tile, head):
    coded, power = encode(tile)
    ref[rows_at(slot, tile.shape[0]), :] = coded
    rows = lax.broadcasted_iota(jnp.int32, head.shape, 0)
    return jnp.where(rows == slot, power, head)


def put_head(ref, head):
    ref[pl.ds(ref.shape[0] - head.shape[0], head.shape[0]), :] = head.astype(jnp.int16)


def get_head(ref, count):
    rows = head_rows(count)
    return ref[pl.ds(ref.shape[0] - rows, rows), :].astype(jnp.int32)


def get_tile(ref, slot, head):
    rows = lax.broadcasted_iota(jnp.int32, head.shape, 0)
    power = jnp.sum(jnp.where(rows == slot, head, 0), axis=0, keepdims=True)
    coded = ref[rows_at(slot, ref.shape[-1]), :]
    return coded.astype(jnp.int32).astype(jnp.float32) * (jnp.exp2(power.astype(jnp.float32)) * (1.0 / PEAK))


def product(a_ref, p_ref, look, fan):
    chosen = [look(f) for f in range(fan)]
    left = jnp.concatenate([a_ref[pa] for pa, _ in chosen], axis=1)
    right = jnp.concatenate([p_ref[pp] for _, pp in chosen], axis=0)
    return jnp.dot(left, right, preferred_element_type=jnp.float32)


def own_bit(bit):
    return (lax.axis_index("layer") >> bit) & 1


def insert(rest, at, bit):
    low = rest & ((1 << at) - 1)
    return ((rest >> at) << (at + 1)) | (bit << at) | low


def loop(turns, body, start):
    return body(0, start) if turns == 1 else lax.fori_loop(0, turns, body, start)


def packing(slots, lanes):
    return max(1, lanes // slots)


def pack_kernel(ia_ref, ip_ref, own_ref, far_ref):
    fan, slots = ia_ref.shape[1:]
    per = packing(slots, own_ref.shape[1])
    col = lax.axis_index("col")
    for out_ref, column in ((own_ref, col), (far_ref, 1 - col)):
        for which, ref in enumerate((ia_ref, ip_ref)):
            lists = ref[column]
            for f in range(fan):
                row, at = divmod(which * fan + f, per)
                out_ref[pl.ds(row, 1), pl.ds(at * slots, slots)] = lists[f : f + 1]


def finder(lists_ref, fan, slots):
    per = packing(slots, lists_ref.shape[1])

    def place(which, f, t):
        row, at = divmod(which * fan + f, per)
        return lists_ref[row, at * slots + t]

    return lambda t: lambda f: (place(0, f, t), place(1, f, t))


def send_kernel(fan, slots, count, chunks, bits, joins):
    def kernel(lists_ref, a_ref, *refs):
        find = finder(lists_ref, fan, slots)
        n_out = len(chunks) + joins
        p_refs, out_refs = refs[:-n_out], refs[-n_out:]
        if joins:
            out_refs, p_ref = out_refs[:-1], out_refs[-1]
            held = p_ref.shape[0] // 2
            row = lax.axis_index("row")
            p_ref[pl.ds(row * held, held)] = p_refs[0][...]
            at = (1 - row) * held
            for ref in p_refs[1:]:
                p_ref[pl.ds(at, ref.shape[0])] = ref[...]
                at += ref.shape[0]
        else:
            (p_ref,) = p_refs
        width = p_ref.shape[-1]
        for (first, size), bit, out_ref in zip(chunks, bits, out_refs):
            side = 1 - own_bit(bit)
            total = out_ref.shape[0] // width

            def body(step, head):
                for k in range(GROUP):
                    slot = step * GROUP + k
                    layer = insert(slot // size, bit, side)
                    tile = product(a_ref, p_ref, find(layer * count + first + slot % size), fan)
                    head = put_tile(out_ref, slot, tile, head)
                return head

            put_head(out_ref, loop(total // GROUP, body, new_head(total, width)))

    return kernel


def split_kernel(in_ref, *out_refs):
    at = 0
    for ref in out_refs:
        ref[...] = in_ref[pl.ds(at, ref.shape[0])]
        at += ref.shape[0]


def keep_kernel(fan, slots, count, chunks, bits):
    def kernel(lists_ref, a_ref, p_ref, *out_refs):
        find = finder(lists_ref, fan, slots)
        for (first, size), bit, out_ref in zip(chunks, bits, out_refs):
            side = own_bit(bit)

            def body(step, _):
                for k in range(GROUP):
                    slot = step * GROUP + k
                    layer = insert(slot // size, bit, side)
                    out_ref[slot] = product(a_ref, p_ref, find(layer * count + first + slot % size), fan)
                return 0

            loop(out_ref.shape[0] // GROUP, body, 0)

    return kernel


def add_kernel(sizes, rest, bit, keeps):
    at = rest.index(bit)
    full = sum(sizes)
    halves = 1 << (len(rest) - 1)

    def kernel(*refs):
        n = len(sizes)
        kept_refs, in_refs, (sent_ref, stay_ref) = refs[:n], refs[n : 2 * n], refs[2 * n : 2 * n + 2]
        width = sent_ref.shape[-1]
        mine = own_bit(bit)
        heads = [get_head(ref, ref.shape[0] // width) for ref in in_refs]

        def sums(place):
            for size, kept_ref, in_ref, head in zip(sizes, kept_refs, in_refs, heads):
                for i in range(size):
                    slot = place * size + i
                    yield kept_ref[slot] + get_tile(in_ref, slot, head)

        def send(ref, side):
            def body(half, head):
                for i, tile in enumerate(sums(insert(half, at, side))):
                    head = put_tile(ref, half * full + i, tile, head)
                return head

            put_head(ref, lax.fori_loop(0, halves, body, new_head(halves * full, width), unroll=halves <= 4))

        send(sent_ref, 1 - mine)
        if keeps:

            def body(half, _):
                for i, tile in enumerate(sums(insert(half, at, mine))):
                    stay_ref[half * full + i] = tile
                return 0

            lax.fori_loop(0, halves, body, 0, unroll=halves <= 4)
        else:
            send(stay_ref, mine)

    return kernel


def sum_kernel(kept_ref, in_ref, out_ref):
    count = out_ref.shape[0]
    head = get_head(in_ref, count)
    for i in range(count):
        out_ref[i] = kept_ref[i] + get_tile(in_ref, i, head)


def last_kernel(first, size, n_messages, n_before):
    def kernel(own_ref, *refs):
        in_refs, before_refs, out_ref = refs[:n_messages], refs[n_messages:-1], refs[-1]
        at = 0
        for ref in before_refs:
            out_ref[pl.ds(at, ref.shape[0])] = ref[...]
            at += ref.shape[0]
        heads = [get_head(ref, size) for ref in in_refs]
        for i in range(size):
            total = own_ref[first + i]
            for ref, head in zip(in_refs, heads):
                total += get_tile(ref, i, head)
            out_ref[at + i] = total.astype(out_ref.dtype)

    return kernel


def call(kernel, out_shape, smem, vmem, after=(), scratch=(), flops=0):
    outs = out_shape if isinstance(out_shape, (list, tuple)) else [out_shape]
    moved = sum(x.size * x.dtype.itemsize for x in (*smem, *vmem, *outs))
    n_real = len(smem) + len(vmem)

    def wrapped(*refs):
        kernel(*refs[:n_real], *refs[n_real + len(after) :])

    return pl.pallas_call(
        wrapped,
        out_shape=out_shape,
        in_specs=[pl.BlockSpec(memory_space=SMEM)] * len(smem)
        + [pl.BlockSpec(memory_space=VMEM)] * len(vmem)
        + [pl.BlockSpec(memory_space=pl.ANY)] * len(after),
        out_specs=jax.tree.map(lambda _: pl.BlockSpec(memory_space=VMEM), out_shape),
        scratch_shapes=list(scratch),
        compiler_params=pltpu.CompilerParams(vmem_limit_bytes=moved + 4 * 2**20),
        cost_estimate=pl.CostEstimate(flops=5 * flops, bytes_accessed=moved if flops else 1, transcendentals=0),
    )(*smem, *vmem, *after)


def hold(x, after):
    def kernel(*refs):
        pass

    return pl.pallas_call(
        kernel,
        out_shape=jax.ShapeDtypeStruct(x.shape, x.dtype),
        in_specs=[pl.BlockSpec(memory_space=pl.ANY)] * (1 + len(after)),
        out_specs=pl.BlockSpec(memory_space=pl.ANY),
        input_output_aliases={0: 0},
        compiler_params=pltpu.CompilerParams(vmem_limit_bytes=2**20),
    )(x, *after)


def on_device(a_tiles, p_tiles, pair_a, pair_p):
    a, p = a_tiles[0, 0, 0], p_tiles[0, 0, 0]
    ia, ip = jnp.swapaxes(pair_a[0, 0, 0], 1, 2), jnp.swapaxes(pair_p[0, 0, 0], 1, 2)
    fan, slots = ia.shape[1:]
    held, width = p.shape[0], p.shape[-1]
    layers = lax.axis_size("layer")
    bits = layers.bit_length() - 1
    count = slots // layers
    swap = [(0, 1), (1, 0)]

    half = count // 2
    chunks = [(0, half), (half, count - half)]
    flops = layers * half * fan * width**3

    def floats(size):
        return jax.ShapeDtypeStruct((size, width, width), jnp.float32)

    def exchange(x, bit):
        return lax.ppermute(x, "layer", [(i, i ^ (1 << bit)) for i in range(layers)])

    def cross(x, bit):
        flip = 0 if bit is None else 1 << bit
        perm = [(c * layers + i, (1 - c) * layers + (i ^ flip)) for c in range(2) for i in range(layers)]
        return lax.ppermute(x, ("col", "layer"), perm)

    def send(lists, vmem, which, bits, joins, after, cost):
        picked = [chunks[n] for n in which]
        shapes = [message(layers // 2 * size, width) for _, size in picked]
        if joins:
            shapes.append(jax.ShapeDtypeStruct((2 * held, width, width), p.dtype))
        kernel = send_kernel(fan, slots, count, picked, bits, joins)
        made = call(kernel, shapes, (lists,), vmem, after, (), cost * len(which) * flops)
        return made, [exchange(x, b) for x, b in zip(made, bits)]

    def keep(lists, vmem, bits, after, cost):
        shapes = [floats(layers // 2 * size) for _, size in chunks]
        kernel = keep_kernel(fan, slots, count, chunks, bits)
        return call(kernel, shapes, (lists,), vmem, after, (), cost * 2 * flops)

    def add(parts, sizes, rest, bit, keeps, after):
        n = sum(sizes) << (len(rest) - 1)
        shapes = [message(n, width), floats(n) if keeps else message(n, width)]
        kept, came = zip(*parts)
        return call(add_kernel(sizes, rest, bit, keeps), shapes, (), (*kept, *came), after)

    own_bits, other_bits = (0, 1), (1, 0)
    sizes = [size for _, size in chunks]
    every = list(range(bits))

    def less(rest, bit):
        return [b for b in rest if b != bit]

    def second(kept, came, size, bit, after):
        sent, kept = add([(kept, came)], [size], less(every, bit), 1 - bit, True, after)
        return sent, (kept, exchange(sent, 1 - bit))

    p_x = lax.ppermute(p, "col", swap)
    p_r = lax.ppermute(p, "row", swap)
    packed = jax.ShapeDtypeStruct((-(-2 * fan // packing(slots, LANES)), max(slots, LANES)), jnp.int32)
    lists, lists_far = call(pack_kernel, [packed] * 2, (), (ia, ip))

    token = jax.ShapeDtypeStruct((8, width), jnp.float32)
    gate = call(lambda *refs: None, token, (), (), (), (), 10**9)
    gate = call(lambda *refs: None, token, (), (a, p), (gate,))

    (*made, joined), own_came = send(lists, (a, p, p_r), (0, 1), own_bits, True, (gate,), 1)
    own_kept = keep(lists, (a, joined), own_bits, made[:1], 1)
    lists_x = lax.ppermute(hold(lists_far, own_kept[:1]), "col", swap)
    pieces = [jax.ShapeDtypeStruct((held // 2, width, width), p.dtype)] * 2
    pieces = call(split_kernel, pieces, (), (p_x,), (own_kept[0], lists_x))
    p_xr = [lax.ppermute(x, "row", swap) for x in pieces]
    parts, after = [], ()
    for n in range(2):
        sent, part = second(own_kept[n], own_came[n], sizes[n], own_bits[n], after)
        parts.append(part)
        after = (sent,)

    (made, joined), came_0 = send(lists_x, (a, p_x, *p_xr), (0,), other_bits[:1], True, after, 0)
    (made,), came_1 = send(lists_x, (a, joined), (1,), other_bits[1:], False, (made,), 0)
    other_came = came_0 + came_1
    rest, part_sizes, after = every[2:], sizes, (made,)
    for b in every[2:]:
        sent, kept = add(parts, part_sizes, rest, b, True, after)
        after = (sent,)
        parts, part_sizes = [(kept, exchange(sent, b))], [count]
        rest = less(rest, b)
    (own,) = parts
    other_kept = keep(lists_x, (a, joined), other_bits, after, 1)

    streams, after = [], (other_kept[0],)
    for n in range(2):
        sent, part = second(other_kept[n], other_came[n], sizes[n], other_bits[n], after)
        streams.append(part)
        after = (sent,)
    rest = every[2:]
    for b in every[2:-1]:
        for n in range(2):
            sent, kept = add([streams[n]], [sizes[n]], rest, b, True, after)
            after = (sent,)
            streams[n] = (kept, exchange(sent, b))
        rest = less(rest, b)

    own = call(sum_kernel, floats(count), (), own, after)
    moved, after = [], (own,)
    for n in range(2):
        sent, stay = add([streams[n]], [sizes[n]], rest, rest[0], False, after)
        after = (sent,)
        moved.append((cross(sent, rest[0]), cross(stay, None)))
    result = ()
    for n, (first, size) in enumerate(chunks):
        final = n == len(chunks) - 1
        shape = jax.ShapeDtypeStruct((count if final else size, width, width), jnp.bfloat16)
        kernel = last_kernel(first, size, len(moved[n]), len(result))
        result = (call(kernel, shape, (), (own, *moved[n], *result)),)
    return result[0][None, None]


def solution(mesh):
    spec = P("row", "col", "layer", None, None, None)
    return jax.shard_map(
        on_device,
        mesh=mesh,
        in_specs=(spec,) * 4,
        out_specs=P("row", "col", "layer", None, None),
        check_vma=False,
    )
```

```python
import jax
import jax.numpy as jnp
from jax import lax
from jax.experimental import pallas as pl
from jax.experimental.pallas import tpu as pltpu
from jax.sharding import PartitionSpec as P

PEAK = 32766.0
ROWS = 16
LANES = 128
GROUP = 8
SMEM = pltpu.MemorySpace.SMEM
VMEM = pltpu.MemorySpace.VMEM


def head_rows(count):
    return -(-count // ROWS) * ROWS


def message(count, width):
    return jax.ShapeDtypeStruct((count * width + head_rows(count), width), jnp.int16)


def encode(tile):
    top = jnp.max(jnp.abs(tile), axis=0, keepdims=True)
    power = jnp.floor(jnp.log2(jnp.maximum(top, 2.0**-100)) + 0.001) + 1.0
    scaled = jnp.round(tile * (jnp.exp2(-power) * PEAK))
    return scaled.astype(jnp.int32).astype(jnp.int16), power.astype(jnp.int32)


def new_head(count, width):
    return jnp.zeros((head_rows(count), width), jnp.int32)


def rows_at(slot, width):
    start = slot * width
    return pl.ds(start if isinstance(start, int) else pl.multiple_of(start, width), width)


def put_tile(ref, slot, tile, head):
    coded, power = encode(tile)
    ref[rows_at(slot, tile.shape[0]), :] = coded
    rows = lax.broadcasted_iota(jnp.int32, head.shape, 0)
    return jnp.where(rows == slot, power, head)


def put_head(ref, head):
    ref[pl.ds(ref.shape[0] - head.shape[0], head.shape[0]), :] = head.astype(jnp.int16)


def get_head(ref, count):
    rows = head_rows(count)
    return ref[pl.ds(ref.shape[0] - rows, rows), :].astype(jnp.int32)


def get_tile(ref, slot, head):
    rows = lax.broadcasted_iota(jnp.int32, head.shape, 0)
    power = jnp.sum(jnp.where(rows == slot, head, 0), axis=0, keepdims=True)
    coded = ref[rows_at(slot, ref.shape[-1]), :]
    return coded.astype(jnp.int32).astype(jnp.float32) * (jnp.exp2(power.astype(jnp.float32)) * (1.0 / PEAK))


def product(a_ref, p_ref, look, fan):
    chosen = [look(f) for f in range(fan)]
    left = jnp.concatenate([a_ref[pa] for pa, _ in chosen], axis=1)
    right = jnp.concatenate([p_ref[pp] for _, pp in chosen], axis=0)
    return jnp.dot(left, right, preferred_element_type=jnp.float32)


def place_of(bit):
    return bit ^ lax.axis_index("row") if bit < 2 else bit


def own_bit(bit):
    return (lax.axis_index("layer") >> place_of(bit)) & 1


def insert(rest, at, bit):
    low = rest & ((1 << at) - 1)
    return ((rest >> at) << (at + 1)) | (bit << at) | low


def loop(turns, body, start):
    return body(0, start) if turns == 1 else lax.fori_loop(0, turns, body, start)


def packing(slots, lanes):
    return max(1, lanes // slots)


def pack_kernel(ia_ref, ip_ref, own_ref, far_ref):
    fan, slots = ia_ref.shape[1:]
    per = packing(slots, own_ref.shape[1])
    col = lax.axis_index("col")
    for out_ref, column in ((own_ref, col), (far_ref, 1 - col)):
        for which, ref in enumerate((ia_ref, ip_ref)):
            lists = ref[column]
            for f in range(fan):
                row, at = divmod(which * fan + f, per)
                out_ref[pl.ds(row, 1), pl.ds(at * slots, slots)] = lists[f : f + 1]


def finder(lists_ref, fan, slots):
    per = packing(slots, lists_ref.shape[1])

    def place(which, f, t):
        row, at = divmod(which * fan + f, per)
        return lists_ref[row, at * slots + t]

    return lambda t: lambda f: (place(0, f, t), place(1, f, t))


def send_kernel(fan, slots, count, chunks, bits, joins):
    def kernel(lists_ref, a_ref, *refs):
        find = finder(lists_ref, fan, slots)
        n_out = len(chunks) + joins
        p_refs, out_refs = refs[:-n_out], refs[-n_out:]
        if joins:
            out_refs, p_ref = out_refs[:-1], out_refs[-1]
            held = p_ref.shape[0] // 2
            row = lax.axis_index("row")
            p_ref[pl.ds(row * held, held)] = p_refs[0][...]
            at = (1 - row) * held
            for ref in p_refs[1:]:
                p_ref[pl.ds(at, ref.shape[0])] = ref[...]
                at += ref.shape[0]
        else:
            (p_ref,) = p_refs
        width = p_ref.shape[-1]
        for (first, size), bit, out_ref in zip(chunks, bits, out_refs):
            side, place = 1 - own_bit(bit), place_of(bit)
            total = out_ref.shape[0] // width

            def body(step, head):
                for k in range(GROUP):
                    slot = step * GROUP + k
                    layer = insert(slot // size, place, side)
                    tile = product(a_ref, p_ref, find(layer * count + first + slot % size), fan)
                    head = put_tile(out_ref, slot, tile, head)
                return head

            put_head(out_ref, loop(total // GROUP, body, new_head(total, width)))

    return kernel


def split_kernel(in_ref, *out_refs):
    at = 0
    for ref in out_refs:
        ref[...] = in_ref[pl.ds(at, ref.shape[0])]
        at += ref.shape[0]


def keep_kernel(fan, slots, count, chunks, bits):
    def kernel(lists_ref, a_ref, p_ref, *out_refs):
        find = finder(lists_ref, fan, slots)
        for (first, size), bit, out_ref in zip(chunks, bits, out_refs):
            side, place = own_bit(bit), place_of(bit)

            def body(step, _):
                for k in range(GROUP):
                    slot = step * GROUP + k
                    layer = insert(slot // size, place, side)
                    out_ref[slot] = product(a_ref, p_ref, find(layer * count + first + slot % size), fan)
                return 0

            loop(out_ref.shape[0] // GROUP, body, 0)

    return kernel


def add_kernel(sizes, rest, bit, keeps):
    at = rest.index(bit)
    full = sum(sizes)
    halves = 1 << (len(rest) - 1)

    def kernel(*refs):
        n = len(sizes)
        kept_refs, in_refs, (sent_ref, stay_ref) = refs[:n], refs[n : 2 * n], refs[2 * n : 2 * n + 2]
        width = sent_ref.shape[-1]
        mine = own_bit(bit)
        heads = [get_head(ref, ref.shape[0] // width) for ref in in_refs]

        def sums(place):
            for size, kept_ref, in_ref, head in zip(sizes, kept_refs, in_refs, heads):
                for i in range(size):
                    slot = place * size + i
                    yield kept_ref[slot] + get_tile(in_ref, slot, head)

        def send(ref, side):
            def body(half, head):
                for i, tile in enumerate(sums(insert(half, at, side))):
                    head = put_tile(ref, half * full + i, tile, head)
                return head

            put_head(ref, lax.fori_loop(0, halves, body, new_head(halves * full, width), unroll=halves <= 4))

        if not keeps:
            mine = mine ^ lax.axis_index("row")
        send(sent_ref, 1 - mine)
        if keeps:

            def body(half, _):
                for i, tile in enumerate(sums(insert(half, at, mine))):
                    stay_ref[half * full + i] = tile
                return 0

            lax.fori_loop(0, halves, body, 0, unroll=halves <= 4)
        else:
            send(stay_ref, mine)

    return kernel


def sum_kernel(kept_ref, in_ref, out_ref):
    count = out_ref.shape[0]
    head = get_head(in_ref, count)
    for i in range(count):
        out_ref[i] = kept_ref[i] + get_tile(in_ref, i, head)


def last_kernel(first, size, n_messages, n_before):
    def kernel(own_ref, *refs):
        in_refs, before_refs, out_ref = refs[:n_messages], refs[n_messages:-1], refs[-1]
        at = 0
        for ref in before_refs:
            out_ref[pl.ds(at, ref.shape[0])] = ref[...]
            at += ref.shape[0]
        heads = [get_head(ref, size) for ref in in_refs]
        for i in range(size):
            total = own_ref[first + i]
            for ref, head in zip(in_refs, heads):
                total += get_tile(ref, i, head)
            out_ref[at + i] = total.astype(out_ref.dtype)

    return kernel


def call(kernel, out_shape, smem, vmem, after=(), scratch=(), flops=0):
    outs = out_shape if isinstance(out_shape, (list, tuple)) else [out_shape]
    moved = sum(x.size * x.dtype.itemsize for x in (*smem, *vmem, *outs))
    n_real = len(smem) + len(vmem)

    def wrapped(*refs):
        kernel(*refs[:n_real], *refs[n_real + len(after) :])

    return pl.pallas_call(
        wrapped,
        out_shape=out_shape,
        in_specs=[pl.BlockSpec(memory_space=SMEM)] * len(smem)
        + [pl.BlockSpec(memory_space=VMEM)] * len(vmem)
        + [pl.BlockSpec(memory_space=pl.ANY)] * len(after),
        out_specs=jax.tree.map(lambda _: pl.BlockSpec(memory_space=VMEM), out_shape),
        scratch_shapes=list(scratch),
        compiler_params=pltpu.CompilerParams(vmem_limit_bytes=moved + 4 * 2**20),
        cost_estimate=pl.CostEstimate(flops=5 * flops, bytes_accessed=moved if flops else 1, transcendentals=0),
    )(*smem, *vmem, *after)


def hold(x, after):
    def kernel(*refs):
        pass

    return pl.pallas_call(
        kernel,
        out_shape=jax.ShapeDtypeStruct(x.shape, x.dtype),
        in_specs=[pl.BlockSpec(memory_space=pl.ANY)] * (1 + len(after)),
        out_specs=pl.BlockSpec(memory_space=pl.ANY),
        input_output_aliases={0: 0},
        compiler_params=pltpu.CompilerParams(vmem_limit_bytes=2**20),
    )(x, *after)


def on_device(a_tiles, p_tiles, pair_a, pair_p):
    a, p = a_tiles[0, 0, 0], p_tiles[0, 0, 0]
    ia, ip = jnp.swapaxes(pair_a[0, 0, 0], 1, 2), jnp.swapaxes(pair_p[0, 0, 0], 1, 2)
    fan, slots = ia.shape[1:]
    held, width = p.shape[0], p.shape[-1]
    layers = lax.axis_size("layer")
    bits = layers.bit_length() - 1
    count = slots // layers
    swap = [(0, 1), (1, 0)]

    half = count // 2
    chunks = [(0, half), (half, count - half)]
    flops = layers * half * fan * width**3

    def floats(size):
        return jax.ShapeDtypeStruct((size, width, width), jnp.float32)

    def exchange(x, bit):
        if bit >= 2:
            return lax.ppermute(x, "layer", [(i, i ^ (1 << bit)) for i in range(layers)])
        perm = [(r * layers + i, r * layers + (i ^ (1 << (bit ^ r)))) for r in range(2) for i in range(layers)]
        return lax.ppermute(x, ("row", "layer"), perm)

    def cross(x, bit, first):
        perm = []
        for r in range(2):
            flip = 1 << bit if first == (r == 0) else 0
            for c in range(2):
                for i in range(layers):
                    perm.append(((r * 2 + c) * layers + i, (r * 2 + 1 - c) * layers + (i ^ flip)))
        return lax.ppermute(x, ("row", "col", "layer"), perm)

    def send(lists, vmem, which, bits, joins, after, cost):
        picked = [chunks[n] for n in which]
        shapes = [message(layers // 2 * size, width) for _, size in picked]
        if joins:
            shapes.append(jax.ShapeDtypeStruct((2 * held, width, width), p.dtype))
        kernel = send_kernel(fan, slots, count, picked, bits, joins)
        made = call(kernel, shapes, (lists,), vmem, after, (), cost * len(which) * flops)
        return made, [exchange(x, b) for x, b in zip(made, bits)]

    def keep(lists, vmem, bits, after, cost):
        shapes = [floats(layers // 2 * size) for _, size in chunks]
        kernel = keep_kernel(fan, slots, count, chunks, bits)
        return call(kernel, shapes, (lists,), vmem, after, (), cost * 2 * flops)

    def add(parts, sizes, rest, bit, keeps, after):
        n = sum(sizes) << (len(rest) - 1)
        shapes = [message(n, width), floats(n) if keeps else message(n, width)]
        kept, came = zip(*parts)
        return call(add_kernel(sizes, rest, bit, keeps), shapes, (), (*kept, *came), after)

    own_bits, other_bits = (0, 1), (1, 0)
    sizes = [size for _, size in chunks]
    every = list(range(bits))

    def less(rest, bit):
        return [b for b in rest if b != bit]

    def second(kept, came, size, bit, after):
        sent, kept = add([(kept, came)], [size], less(every, bit), 1 - bit, True, after)
        return sent, (kept, exchange(sent, 1 - bit))

    p_x = lax.ppermute(p, "col", swap)
    p_r = lax.ppermute(p, "row", swap)
    packed = jax.ShapeDtypeStruct((-(-2 * fan // packing(slots, LANES)), max(slots, LANES)), jnp.int32)
    lists, lists_far = call(pack_kernel, [packed] * 2, (), (ia, ip))

    token = jax.ShapeDtypeStruct((8, width), jnp.float32)
    gate = call(lambda *refs: None, token, (), (), (), (), 10**9)
    gate = call(lambda *refs: None, token, (), (a, p), (gate,))

    (*made, joined), own_came = send(lists, (a, p, p_r), (0, 1), own_bits, True, (gate,), 1)
    own_kept = keep(lists, (a, joined), own_bits, made[:1], 1)
    lists_x = lax.ppermute(hold(lists_far, own_kept[:1]), "col", swap)
    pieces = [jax.ShapeDtypeStruct((held // 2, width, width), p.dtype)] * 2
    pieces = call(split_kernel, pieces, (), (p_x,), (own_kept[0], lists_x))
    p_xr = [lax.ppermute(x, "row", swap) for x in pieces]
    parts, after = [], ()
    for n in range(2):
        sent, part = second(own_kept[n], own_came[n], sizes[n], own_bits[n], after)
        parts.append(part)
        after = (sent,)

    (made, joined), came_0 = send(lists_x, (a, p_x, *p_xr), (0,), other_bits[:1], True, after, 0)
    (made,), came_1 = send(lists_x, (a, joined), (1,), other_bits[1:], False, (made,), 0)
    other_came = came_0 + came_1
    rest, part_sizes, after = every[2:], sizes, (made,)
    for b in every[2:]:
        sent, kept = add(parts, part_sizes, rest, b, True, after)
        after = (sent,)
        parts, part_sizes = [(kept, exchange(sent, b))], [count]
        rest = less(rest, b)
    (own,) = parts
    other_kept = keep(lists_x, (a, joined), other_bits, after, 1)

    streams, after = [], (other_kept[0],)
    for n in range(2):
        sent, part = second(other_kept[n], other_came[n], sizes[n], other_bits[n], after)
        streams.append(part)
        after = (sent,)
    rest = every[2:]
    for b in every[2:-1]:
        for n in range(2):
            sent, kept = add([streams[n]], [sizes[n]], rest, b, True, after)
            after = (sent,)
            streams[n] = (kept, exchange(sent, b))
        rest = less(rest, b)

    own = call(sum_kernel, floats(count), (), own, after)
    moved, after = [], (own,)
    for n in range(2):
        sent, stay = add([streams[n]], [sizes[n]], rest, rest[0], False, after)
        after = (sent,)
        moved.append((cross(sent, rest[0], True), cross(stay, rest[0], False)))
    result = ()
    for n, (first, size) in enumerate(chunks):
        final = n == len(chunks) - 1
        shape = jax.ShapeDtypeStruct((count if final else size, width, width), jnp.bfloat16)
        kernel = last_kernel(first, size, len(moved[n]), len(result))
        result = (call(kernel, shape, (), (own, *moved[n], *result)),)
    return result[0][None, None]


def solution(mesh):
    spec = P("row", "col", "layer", None, None, None)
    return jax.shard_map(
        on_device,
        mesh=mesh,
        in_specs=(spec,) * 4,
        out_specs=P("row", "col", "layer", None, None),
        check_vma=False,
    )
```

```python
import jax
import jax.numpy as jnp
from jax import lax
from jax.experimental import pallas as pl
from jax.experimental.pallas import tpu as pltpu
from jax.sharding import PartitionSpec as P

PEAK = 32766.0
ROWS = 16
LANES = 128
GROUP = 8
SMEM = pltpu.MemorySpace.SMEM
VMEM = pltpu.MemorySpace.VMEM


def head_rows(count):
    return -(-count // ROWS) * ROWS


def message(count, width):
    return jax.ShapeDtypeStruct((count * width + head_rows(count), width), jnp.int16)


def encode(tile):
    top = jnp.max(jnp.abs(tile), axis=0, keepdims=True)
    power = jnp.floor(jnp.log2(jnp.maximum(top, 2.0**-100)) + 0.001) + 1.0
    scaled = jnp.round(tile * (jnp.exp2(-power) * PEAK))
    return scaled.astype(jnp.int32).astype(jnp.int16), power.astype(jnp.int32)


def new_head(count, width):
    return jnp.zeros((head_rows(count), width), jnp.int32)


def rows_at(slot, width):
    start = slot * width
    return pl.ds(start if isinstance(start, int) else pl.multiple_of(start, width), width)


def put_tile(ref, slot, tile, head):
    coded, power = encode(tile)
    ref[rows_at(slot, tile.shape[0]), :] = coded
    rows = lax.broadcasted_iota(jnp.int32, head.shape, 0)
    return jnp.where(rows == slot, power, head)


def put_head(ref, head):
    ref[pl.ds(ref.shape[0] - head.shape[0], head.shape[0]), :] = head.astype(jnp.int16)


def get_head(ref, count):
    rows = head_rows(count)
    return ref[pl.ds(ref.shape[0] - rows, rows), :].astype(jnp.int32)


def get_tile(ref, slot, head):
    rows = lax.broadcasted_iota(jnp.int32, head.shape, 0)
    power = jnp.sum(jnp.where(rows == slot, head, 0), axis=0, keepdims=True)
    coded = ref[rows_at(slot, ref.shape[-1]), :]
    return coded.astype(jnp.int32).astype(jnp.float32) * (jnp.exp2(power.astype(jnp.float32)) * (1.0 / PEAK))


def product(a_ref, p_ref, look, fan):
    chosen = [look(f) for f in range(fan)]
    left = jnp.concatenate([a_ref[pa] for pa, _ in chosen], axis=1)
    right = jnp.concatenate([p_ref[pp] for _, pp in chosen], axis=0)
    return jnp.dot(left, right, preferred_element_type=jnp.float32)


def own_bit(bit):
    return (lax.axis_index("layer") >> bit) & 1


def insert(rest, at, bit):
    low = rest & ((1 << at) - 1)
    return ((rest >> at) << (at + 1)) | (bit << at) | low


def loop(turns, body, start):
    return body(0, start) if turns == 1 else lax.fori_loop(0, turns, body, start)


def packing(slots, lanes):
    return max(1, lanes // slots)


def pack_kernel(ia_ref, ip_ref, own_ref, far_ref):
    fan, slots = ia_ref.shape[1:]
    per = packing(slots, own_ref.shape[1])
    col = lax.axis_index("col")
    for out_ref, column in ((own_ref, col), (far_ref, 1 - col)):
        for which, ref in enumerate((ia_ref, ip_ref)):
            lists = ref[column]
            for f in range(fan):
                row, at = divmod(which * fan + f, per)
                out_ref[pl.ds(row, 1), pl.ds(at * slots, slots)] = lists[f : f + 1]


def finder(lists_ref, fan, slots):
    per = packing(slots, lists_ref.shape[1])

    def place(which, f, t):
        row, at = divmod(which * fan + f, per)
        return lists_ref[row, at * slots + t]

    return lambda t: lambda f: (place(0, f, t), place(1, f, t))


def send_kernel(fan, slots, count, chunks, bits, joins):
    def kernel(lists_ref, a_ref, *refs):
        find = finder(lists_ref, fan, slots)
        n_out = len(chunks) + joins
        p_refs, out_refs = refs[:-n_out], refs[-n_out:]
        if joins:
            out_refs, p_ref = out_refs[:-1], out_refs[-1]
            held = p_ref.shape[0] // 2
            row = lax.axis_index("row")
            p_ref[pl.ds(row * held, held)] = p_refs[0][...]
            at = (1 - row) * held
            for ref in p_refs[1:]:
                p_ref[pl.ds(at, ref.shape[0])] = ref[...]
                at += ref.shape[0]
        else:
            (p_ref,) = p_refs
        width = p_ref.shape[-1]
        for (first, size), bit, out_ref in zip(chunks, bits, out_refs):
            side = 1 - own_bit(bit)
            total = out_ref.shape[0] // width

            def body(step, head):
                for k in range(GROUP):
                    slot = step * GROUP + k
                    layer = insert(slot // size, bit, side)
                    tile = product(a_ref, p_ref, find(layer * count + first + slot % size), fan)
                    head = put_tile(out_ref, slot, tile, head)
                return head

            put_head(out_ref, loop(total // GROUP, body, new_head(total, width)))

    return kernel


def split_kernel(in_ref, *out_refs):
    at = 0
    for ref in out_refs:
        ref[...] = in_ref[pl.ds(at, ref.shape[0])]
        at += ref.shape[0]


def keep_kernel(fan, slots, count, chunks, bits):
    def kernel(lists_ref, a_ref, p_ref, *out_refs):
        find = finder(lists_ref, fan, slots)
        for (first, size), bit, out_ref in zip(chunks, bits, out_refs):
            side = own_bit(bit)

            def body(step, _):
                for k in range(GROUP):
                    slot = step * GROUP + k
                    layer = insert(slot // size, bit, side)
                    out_ref[slot] = product(a_ref, p_ref, find(layer * count + first + slot % size), fan)
                return 0

            loop(out_ref.shape[0] // GROUP, body, 0)

    return kernel


def cross_kernel(sizes, bit, whose):
    def kernel(*refs):
        n = len(sizes)
        kept_refs, in_refs, out_refs = refs[:n], refs[n : 2 * n], refs[2 * n :]
        width = out_refs[0].shape[-1]
        mine = own_bit(bit)
        heads = [get_head(ref, ref.shape[0] // width) for ref in in_refs]

        def put(out_ref, side, chosen):
            count = out_ref.shape[0] // width
            head, slot = new_head(count, width), 0
            for c in chosen:
                for i in range(sizes[c]):
                    at = side * sizes[c] + i
                    tile = kept_refs[c][at] + get_tile(in_refs[c], at, heads[c])
                    head = put_tile(out_ref, slot, tile, head)
                    slot += 1
            put_head(out_ref, head)

        put(out_refs[0], 1 - mine, [whose])
        if len(out_refs) > 1:
            put(out_refs[1], mine, range(n))

    return kernel


def add_kernel(sizes, rest, bit):
    at = rest.index(bit)
    full = sum(sizes)
    halves = 1 << (len(rest) - 1)

    def kernel(*refs):
        n = len(sizes)
        kept_refs, in_refs, (sent_ref, stay_ref) = refs[:n], refs[n : 2 * n], refs[2 * n : 2 * n + 2]
        width = sent_ref.shape[-1]
        mine = own_bit(bit)
        heads = [get_head(ref, ref.shape[0] // width) for ref in in_refs]

        def sums(place):
            for size, kept_ref, in_ref, head in zip(sizes, kept_refs, in_refs, heads):
                for i in range(size):
                    slot = place * size + i
                    yield kept_ref[slot] + get_tile(in_ref, slot, head)

        def send(ref, side):
            def body(half, head):
                for i, tile in enumerate(sums(insert(half, at, side))):
                    head = put_tile(ref, half * full + i, tile, head)
                return head

            put_head(ref, lax.fori_loop(0, halves, body, new_head(halves * full, width), unroll=halves <= 4))

        send(sent_ref, 1 - mine)

        def body(half, _):
            for i, tile in enumerate(sums(insert(half, at, mine))):
                stay_ref[half * full + i] = tile
            return 0

        lax.fori_loop(0, halves, body, 0, unroll=halves <= 4)

    return kernel


def sum_kernel(kept_ref, in_ref, out_ref):
    count = out_ref.shape[0]
    head = get_head(in_ref, count)
    for i in range(count):
        out_ref[i] = kept_ref[i] + get_tile(in_ref, i, head)


def early_kernel(first):
    def kernel(own_ref, far_ref, out_ref):
        size = out_ref.shape[0]
        head = get_head(far_ref, size)
        for i in range(size):
            out_ref[i] = own_ref[first + i] + get_tile(far_ref, i, head)

    return kernel


def last_kernel(near_ref, *refs):
    early_refs, out_ref = refs[:-1], refs[-1]
    count = out_ref.shape[0]
    head, at = get_head(near_ref, count), 0
    for ref in early_refs:
        for i in range(ref.shape[0]):
            out_ref[at] = (ref[i] + get_tile(near_ref, at, head)).astype(out_ref.dtype)
            at += 1


def call(kernel, out_shape, smem, vmem, after=(), scratch=(), flops=0):
    outs = out_shape if isinstance(out_shape, (list, tuple)) else [out_shape]
    moved = sum(x.size * x.dtype.itemsize for x in (*smem, *vmem, *outs))
    n_real = len(smem) + len(vmem)

    def wrapped(*refs):
        kernel(*refs[:n_real], *refs[n_real + len(after) :])

    return pl.pallas_call(
        wrapped,
        out_shape=out_shape,
        in_specs=[pl.BlockSpec(memory_space=SMEM)] * len(smem)
        + [pl.BlockSpec(memory_space=VMEM)] * len(vmem)
        + [pl.BlockSpec(memory_space=pl.ANY)] * len(after),
        out_specs=jax.tree.map(lambda _: pl.BlockSpec(memory_space=VMEM), out_shape),
        scratch_shapes=list(scratch),
        compiler_params=pltpu.CompilerParams(vmem_limit_bytes=moved + 4 * 2**20),
        cost_estimate=pl.CostEstimate(flops=5 * flops, bytes_accessed=moved if flops else 1, transcendentals=0),
    )(*smem, *vmem, *after)


def hold(x, after):
    def kernel(*refs):
        pass

    return pl.pallas_call(
        kernel,
        out_shape=jax.ShapeDtypeStruct(x.shape, x.dtype),
        in_specs=[pl.BlockSpec(memory_space=pl.ANY)] * (1 + len(after)),
        out_specs=pl.BlockSpec(memory_space=pl.ANY),
        input_output_aliases={0: 0},
        compiler_params=pltpu.CompilerParams(vmem_limit_bytes=2**20),
    )(x, *after)


def on_device(a_tiles, p_tiles, pair_a, pair_p):
    a, p = a_tiles[0, 0, 0], p_tiles[0, 0, 0]
    ia, ip = jnp.swapaxes(pair_a[0, 0, 0], 1, 2), jnp.swapaxes(pair_p[0, 0, 0], 1, 2)
    fan, slots = ia.shape[1:]
    held, width = p.shape[0], p.shape[-1]
    layers = lax.axis_size("layer")
    bits = layers.bit_length() - 1
    count = slots // layers
    swap = [(0, 1), (1, 0)]

    half = count // 2
    chunks = [(0, half), (half, count - half)]
    flops = layers * half * fan * width**3

    def floats(size):
        return jax.ShapeDtypeStruct((size, width, width), jnp.float32)

    def exchange(x, bit):
        return lax.ppermute(x, "layer", [(i, i ^ (1 << bit)) for i in range(layers)])

    def cross(x, bit):
        flip = 0 if bit is None else 1 << bit
        perm = [(c * layers + i, (1 - c) * layers + (i ^ flip)) for c in range(2) for i in range(layers)]
        return lax.ppermute(x, ("col", "layer"), perm)

    def send(lists, vmem, which, bits, joins, after, cost):
        picked = [chunks[n] for n in which]
        shapes = [message(layers // 2 * size, width) for _, size in picked]
        if joins:
            shapes.append(jax.ShapeDtypeStruct((2 * held, width, width), p.dtype))
        kernel = send_kernel(fan, slots, count, picked, bits, joins)
        made = call(kernel, shapes, (lists,), vmem, after, (), cost * len(which) * flops)
        return made, [exchange(x, b) for x, b in zip(made, bits)]

    def keep(lists, vmem, bits, after, cost):
        shapes = [floats(layers // 2 * size) for _, size in chunks]
        kernel = keep_kernel(fan, slots, count, chunks, bits)
        return call(kernel, shapes, (lists,), vmem, after, (), cost * 2 * flops)

    def add(parts, sizes, rest, bit, after):
        n = sum(sizes) << (len(rest) - 1)
        shapes = [message(n, width), floats(n)]
        kept, came = zip(*parts)
        return call(add_kernel(sizes, rest, bit), shapes, (), (*kept, *came), after)

    own_bits, other_bits = (0, 1), (1, 0)
    sizes = [size for _, size in chunks]
    every = list(range(bits))

    def less(rest, bit):
        return [b for b in rest if b != bit]

    def second(kept, came, size, bit, after):
        sent, kept = add([(kept, came)], [size], less(every, bit), 1 - bit, after)
        return sent, (kept, exchange(sent, 1 - bit))

    p_x = lax.ppermute(p, "col", swap)
    p_r = lax.ppermute(p, "row", swap)
    packed = jax.ShapeDtypeStruct((-(-2 * fan // packing(slots, LANES)), max(slots, LANES)), jnp.int32)
    lists, lists_far = call(pack_kernel, [packed] * 2, (), (ia, ip))

    token = jax.ShapeDtypeStruct((8, width), jnp.float32)
    gate = call(lambda *refs: None, token, (), (), (), (), 10**9)
    gate = call(lambda *refs: None, token, (), (a, p), (gate,))

    (*made, joined), own_came = send(lists, (a, p, p_r), (0, 1), own_bits, True, (gate,), 1)
    own_kept = keep(lists, (a, joined), own_bits, made[:1], 1)
    lists_x = lax.ppermute(hold(lists_far, own_kept[:1]), "col", swap)
    pieces = [jax.ShapeDtypeStruct((held // 2, width, width), p.dtype)] * 2
    pieces = call(split_kernel, pieces, (), (p_x,), (own_kept[0], lists_x))
    p_xr = [lax.ppermute(x, "row", swap) for x in pieces]
    parts, after = [], ()
    for n in range(2):
        sent, part = second(own_kept[n], own_came[n], sizes[n], own_bits[n], after)
        parts.append(part)
        after = (sent,)

    (made, joined), came_0 = send(lists_x, (a, p_x, *p_xr), (0,), other_bits[:1], True, after, 0)
    (made,), came_1 = send(lists_x, (a, joined), (1,), other_bits[1:], False, (made,), 0)
    other_came = came_0 + came_1
    rest, part_sizes, after = every[2:], sizes, (made,)
    for b in every[2:]:
        sent, kept = add(parts, part_sizes, rest, b, after)
        after = (sent,)
        parts, part_sizes = [(kept, exchange(sent, b))], [count]
        rest = less(rest, b)
    (own,) = parts
    other_kept = keep(lists_x, (a, joined), other_bits, after, 1)

    streams, after = [], (other_kept[0],)
    for n in range(2):
        sent, part = second(other_kept[n], other_came[n], sizes[n], other_bits[n], after)
        streams.append(part)
        after = (sent,)
    rest = every[2:]
    for b in every[2:-1]:
        for n in range(2):
            sent, kept = add([streams[n]], [sizes[n]], rest, b, after)
            after = (sent,)
            streams[n] = (kept, exchange(sent, b))
        rest = less(rest, b)

    own = call(sum_kernel, floats(count), (), own, after)
    moved, top, after = [], rest[0], (own,)
    for n in range(2):
        shapes = [message(sizes[n], width)] + [message(count, width)] * n
        used, used_sizes = ([streams[0]], sizes[:1]) if n == 0 else (streams, sizes)
        kept, came = zip(*used)
        sent = call(cross_kernel(used_sizes, top, n), shapes, (), (*kept, *came), after)
        after = (sent[0],)
        moved.append(cross(sent[0], top))
    near = cross(sent[1], None)
    early = []
    for n, (first, size) in enumerate(chunks):
        early.append(call(early_kernel(first), floats(size), (), (own, moved[n]), early[-1:], (), 10**9))
    result = jax.ShapeDtypeStruct((count, width, width), jnp.bfloat16)
    return call(last_kernel, result, (), (near, *early))[None, None]


def solution(mesh):
    spec = P("row", "col", "layer", None, None, None)
    return jax.shard_map(
        on_device,
        mesh=mesh,
        in_specs=(spec,) * 4,
        out_specs=P("row", "col", "layer", None, None),
        check_vma=False,
    )
```

```python
import jax
import jax.numpy as jnp
from jax import lax
from jax.experimental import pallas as pl
from jax.experimental.pallas import tpu as pltpu
from jax.sharding import PartitionSpec as P

PEAK = 32766.0
ROWS = 16
LANES = 128
GROUP = 8
SMEM = pltpu.MemorySpace.SMEM
VMEM = pltpu.MemorySpace.VMEM


def head_rows(count):
    return -(-count // ROWS) * ROWS


def message(count, width):
    return jax.ShapeDtypeStruct((count * width + head_rows(count), width), jnp.int16)


def encode(tile):
    top = jnp.max(jnp.abs(tile), axis=0, keepdims=True)
    power = jnp.floor(jnp.log2(jnp.maximum(top, 2.0**-100)) + 0.001) + 1.0
    scaled = jnp.round(tile * (jnp.exp2(-power) * PEAK))
    return scaled.astype(jnp.int32).astype(jnp.int16), power.astype(jnp.int32)


def new_head(count, width):
    return jnp.zeros((head_rows(count), width), jnp.int32)


def rows_at(slot, width):
    start = slot * width
    return pl.ds(start if isinstance(start, int) else pl.multiple_of(start, width), width)


def put_tile(ref, slot, tile, head):
    coded, power = encode(tile)
    ref[rows_at(slot, tile.shape[0]), :] = coded
    rows = lax.broadcasted_iota(jnp.int32, head.shape, 0)
    return jnp.where(rows == slot, power, head)


def put_head(ref, head):
    ref[pl.ds(ref.shape[0] - head.shape[0], head.shape[0]), :] = head.astype(jnp.int16)


def get_head(ref, count):
    rows = head_rows(count)
    return ref[pl.ds(ref.shape[0] - rows, rows), :].astype(jnp.int32)


def get_tile(ref, slot, head):
    rows = lax.broadcasted_iota(jnp.int32, head.shape, 0)
    power = jnp.sum(jnp.where(rows == slot, head, 0), axis=0, keepdims=True)
    coded = ref[rows_at(slot, ref.shape[-1]), :]
    return coded.astype(jnp.int32).astype(jnp.float32) * (jnp.exp2(power.astype(jnp.float32)) * (1.0 / PEAK))


def product(a_ref, p_ref, look, fan):
    chosen = [look(f) for f in range(fan)]
    left = jnp.concatenate([a_ref[pa] for pa, _ in chosen], axis=1)
    right = jnp.concatenate([p_ref[pp] for _, pp in chosen], axis=0)
    return jnp.dot(left, right, preferred_element_type=jnp.float32)


def own_bit(bit):
    return (lax.axis_index("layer") >> bit) & 1


def insert(rest, at, bit):
    low = rest & ((1 << at) - 1)
    return ((rest >> at) << (at + 1)) | (bit << at) | low


def loop(turns, body, start):
    return body(0, start) if turns == 1 else lax.fori_loop(0, turns, body, start)


def packing(slots, lanes):
    return max(1, lanes // slots)


def pack_kernel(ia_ref, ip_ref, own_ref, far_ref):
    fan, slots = ia_ref.shape[1:]
    per = packing(slots, own_ref.shape[1])
    col = lax.axis_index("col")
    for out_ref, column in ((own_ref, col), (far_ref, 1 - col)):
        for which, ref in enumerate((ia_ref, ip_ref)):
            lists = ref[column]
            for f in range(fan):
                row, at = divmod(which * fan + f, per)
                out_ref[pl.ds(row, 1), pl.ds(at * slots, slots)] = lists[f : f + 1]


def finder(lists_ref, fan, slots):
    per = packing(slots, lists_ref.shape[1])

    def place(which, f, t):
        row, at = divmod(which * fan + f, per)
        return lists_ref[row, at * slots + t]

    return lambda t: lambda f: (place(0, f, t), place(1, f, t))


def send_kernel(fan, slots, count, chunks, bits, joins):
    def kernel(lists_ref, a_ref, *refs):
        find = finder(lists_ref, fan, slots)
        n_out = len(chunks) + joins
        p_refs, out_refs = refs[:-n_out], refs[-n_out:]
        if joins:
            out_refs, p_ref = out_refs[:-1], out_refs[-1]
            held = p_ref.shape[0] // 2
            row = lax.axis_index("row")
            p_ref[pl.ds(row * held, held)] = p_refs[0][...]
            at = (1 - row) * held
            for ref in p_refs[1:]:
                p_ref[pl.ds(at, ref.shape[0])] = ref[...]
                at += ref.shape[0]
        else:
            (p_ref,) = p_refs
        width = p_ref.shape[-1]
        for (first, size), bit, out_ref in zip(chunks, bits, out_refs):
            side = 1 - own_bit(bit)
            total = out_ref.shape[0] // width

            def body(step, head):
                for k in range(GROUP):
                    slot = step * GROUP + k
                    layer = insert(slot // size, bit, side)
                    tile = product(a_ref, p_ref, find(layer * count + first + slot % size), fan)
                    head = put_tile(out_ref, slot, tile, head)
                return head

            put_head(out_ref, loop(total // GROUP, body, new_head(total, width)))

    return kernel


def split_kernel(in_ref, *out_refs):
    at = 0
    for ref in out_refs:
        ref[...] = in_ref[pl.ds(at, ref.shape[0])]
        at += ref.shape[0]


def keep_kernel(fan, slots, count, chunks, bits):
    def kernel(lists_ref, a_ref, p_ref, *out_refs):
        find = finder(lists_ref, fan, slots)
        for (first, size), bit, out_ref in zip(chunks, bits, out_refs):
            side = own_bit(bit)

            def body(step, _):
                for k in range(GROUP):
                    slot = step * GROUP + k
                    layer = insert(slot // size, bit, side)
                    out_ref[slot] = product(a_ref, p_ref, find(layer * count + first + slot % size), fan)
                return 0

            loop(out_ref.shape[0] // GROUP, body, 0)

    return kernel


def cross_kernel(sizes, bit, whose):
    def kernel(*refs):
        n = len(sizes)
        kept_refs, in_refs, out_refs = refs[:n], refs[n : 2 * n], refs[2 * n :]
        width = out_refs[0].shape[-1]
        mine = own_bit(bit)
        heads = [get_head(ref, ref.shape[0] // width) for ref in in_refs]

        def put(out_ref, side, chosen):
            count = out_ref.shape[0] // width
            head, slot = new_head(count, width), 0
            for c in chosen:
                for i in range(sizes[c]):
                    at = side * sizes[c] + i
                    tile = kept_refs[c][at] + get_tile(in_refs[c], at, heads[c])
                    head = put_tile(out_ref, slot, tile, head)
                    slot += 1
            put_head(out_ref, head)

        put(out_refs[0], 1 - mine, [whose])
        if len(out_refs) > 1:
            put(out_refs[1], mine, range(n))

    return kernel


def add_kernel(sizes, rest, bit):
    at = rest.index(bit)
    full = sum(sizes)
    halves = 1 << (len(rest) - 1)

    def kernel(*refs):
        n = len(sizes)
        kept_refs, in_refs, (sent_ref, stay_ref) = refs[:n], refs[n : 2 * n], refs[2 * n : 2 * n + 2]
        width = sent_ref.shape[-1]
        mine = own_bit(bit)
        heads = [get_head(ref, ref.shape[0] // width) for ref in in_refs]

        def sums(place):
            for size, kept_ref, in_ref, head in zip(sizes, kept_refs, in_refs, heads):
                for i in range(size):
                    slot = place * size + i
                    yield kept_ref[slot] + get_tile(in_ref, slot, head)

        def send(ref, side):
            def body(half, head):
                for i, tile in enumerate(sums(insert(half, at, side))):
                    head = put_tile(ref, half * full + i, tile, head)
                return head

            put_head(ref, lax.fori_loop(0, halves, body, new_head(halves * full, width), unroll=halves <= 4))

        send(sent_ref, 1 - mine)

        def body(half, _):
            for i, tile in enumerate(sums(insert(half, at, mine))):
                stay_ref[half * full + i] = tile
            return 0

        lax.fori_loop(0, halves, body, 0, unroll=halves <= 4)

    return kernel


def sum_kernel(kept_ref, in_ref, out_ref):
    count = out_ref.shape[0]
    head = get_head(in_ref, count)
    for i in range(count):
        out_ref[i] = kept_ref[i] + get_tile(in_ref, i, head)


def early_kernel(first):
    def kernel(own_ref, far_ref, out_ref):
        size = out_ref.shape[0]
        head = get_head(far_ref, size)
        for i in range(size):
            out_ref[i] = own_ref[first + i] + get_tile(far_ref, i, head)

    return kernel


def last_kernel(near_ref, *refs):
    early_refs, out_ref = refs[:-1], refs[-1]
    count = out_ref.shape[0]
    head, at = get_head(near_ref, count), 0
    for ref in early_refs:
        for i in range(ref.shape[0]):
            out_ref[at] = (ref[i] + get_tile(near_ref, at, head)).astype(out_ref.dtype)
            at += 1


def call(kernel, out_shape, smem, vmem, after=(), scratch=(), flops=0):
    outs = out_shape if isinstance(out_shape, (list, tuple)) else [out_shape]
    moved = sum(x.size * x.dtype.itemsize for x in (*smem, *vmem, *outs))
    n_real = len(smem) + len(vmem)

    def wrapped(*refs):
        kernel(*refs[:n_real], *refs[n_real + len(after) :])

    return pl.pallas_call(
        wrapped,
        out_shape=out_shape,
        in_specs=[pl.BlockSpec(memory_space=SMEM)] * len(smem)
        + [pl.BlockSpec(memory_space=VMEM)] * len(vmem)
        + [pl.BlockSpec(memory_space=pl.ANY)] * len(after),
        out_specs=jax.tree.map(lambda _: pl.BlockSpec(memory_space=VMEM), out_shape),
        scratch_shapes=list(scratch),
        compiler_params=pltpu.CompilerParams(vmem_limit_bytes=moved + 4 * 2**20),
        cost_estimate=pl.CostEstimate(flops=5 * flops, bytes_accessed=moved if flops else 1, transcendentals=0),
    )(*smem, *vmem, *after)


def hold(x, after):
    def kernel(*refs):
        pass

    return pl.pallas_call(
        kernel,
        out_shape=jax.ShapeDtypeStruct(x.shape, x.dtype),
        in_specs=[pl.BlockSpec(memory_space=pl.ANY)] * (1 + len(after)),
        out_specs=pl.BlockSpec(memory_space=pl.ANY),
        input_output_aliases={0: 0},
        compiler_params=pltpu.CompilerParams(vmem_limit_bytes=2**20),
    )(x, *after)


def on_device(a_tiles, p_tiles, pair_a, pair_p):
    a, p = a_tiles[0, 0, 0], p_tiles[0, 0, 0]
    ia, ip = jnp.swapaxes(pair_a[0, 0, 0], 1, 2), jnp.swapaxes(pair_p[0, 0, 0], 1, 2)
    fan, slots = ia.shape[1:]
    held, width = p.shape[0], p.shape[-1]
    layers = lax.axis_size("layer")
    bits = layers.bit_length() - 1
    count = slots // layers
    swap = [(0, 1), (1, 0)]

    half = count // 2
    chunks = [(0, half), (half, count - half)]
    flops = layers * half * fan * width**3

    def floats(size):
        return jax.ShapeDtypeStruct((size, width, width), jnp.float32)

    def exchange(x, bit):
        return lax.ppermute(x, "layer", [(i, i ^ (1 << bit)) for i in range(layers)])

    def cross(x, bit):
        flip = 0 if bit is None else 1 << bit
        perm = [(c * layers + i, (1 - c) * layers + (i ^ flip)) for c in range(2) for i in range(layers)]
        return lax.ppermute(x, ("col", "layer"), perm)

    def send(lists, vmem, which, bits, joins, after, cost):
        picked = [chunks[n] for n in which]
        shapes = [message(layers // 2 * size, width) for _, size in picked]
        if joins:
            shapes.append(jax.ShapeDtypeStruct((2 * held, width, width), p.dtype))
        kernel = send_kernel(fan, slots, count, picked, bits, joins)
        made = call(kernel, shapes, (lists,), vmem, after, (), cost * len(which) * flops)
        return made, [exchange(x, b) for x, b in zip(made, bits)]

    def keep(lists, vmem, bits, after, cost):
        shapes = [floats(layers // 2 * size) for _, size in chunks]
        kernel = keep_kernel(fan, slots, count, chunks, bits)
        return call(kernel, shapes, (lists,), vmem, after, (), cost * 2 * flops)

    def add(parts, sizes, rest, bit, after):
        n = sum(sizes) << (len(rest) - 1)
        shapes = [message(n, width), floats(n)]
        kept, came = zip(*parts)
        return call(add_kernel(sizes, rest, bit), shapes, (), (*kept, *came), after)

    own_bits, other_bits = (0, 1), (1, 0)
    sizes = [size for _, size in chunks]
    every = list(range(bits))

    def less(rest, bit):
        return [b for b in rest if b != bit]

    def second(kept, came, size, bit, after):
        sent, kept = add([(kept, came)], [size], less(every, bit), 1 - bit, after)
        return sent, (kept, exchange(sent, 1 - bit))

    p_x = lax.ppermute(p, "col", swap)
    p_r = lax.ppermute(p, "row", swap)
    packed = jax.ShapeDtypeStruct((-(-2 * fan // packing(slots, LANES)), max(slots, LANES)), jnp.int32)
    lists, lists_far = call(pack_kernel, [packed] * 2, (), (ia, ip))

    token = jax.ShapeDtypeStruct((8, width), jnp.float32)
    gate = call(lambda *refs: None, token, (), (), (), (), 10**9)
    gate = call(lambda *refs: None, token, (), (a, p), (gate,))

    (*made, joined), own_came = send(lists, (a, p, p_r), (0, 1), own_bits, True, (gate,), 1)
    own_kept = keep(lists, (a, joined), own_bits, made[:1], 1)
    lists_x = lax.ppermute(hold(lists_far, own_kept[:1]), "col", swap)
    pieces = [jax.ShapeDtypeStruct((held // 2, width, width), p.dtype)] * 2
    pieces = call(split_kernel, pieces, (), (p_x,), (own_kept[0], lists_x))
    p_xr = [lax.ppermute(x, "row", swap) for x in pieces]
    parts, after = [], ()
    for n in range(2):
        sent, part = second(own_kept[n], own_came[n], sizes[n], own_bits[n], after)
        parts.append(part)
        after = (sent,)

    (*made, joined), other_came = send(lists_x, (a, p_x, *p_xr), (0, 1), other_bits, True, after, 0)
    rest, part_sizes, after = every[2:], sizes, made[:1]
    for b in every[2:]:
        sent, kept = add(parts, part_sizes, rest, b, after)
        after = (sent,)
        parts, part_sizes = [(kept, exchange(sent, b))], [count]
        rest = less(rest, b)
    (own,) = parts
    other_kept = keep(lists_x, (a, joined), other_bits, after, 1)

    streams, after = [], (other_kept[0],)
    for n in range(2):
        sent, part = second(other_kept[n], other_came[n], sizes[n], other_bits[n], after)
        streams.append(part)
        after = (sent,)
    rest = every[2:]
    for b in every[2:-1]:
        for n in range(2):
            sent, kept = add([streams[n]], [sizes[n]], rest, b, after)
            after = (sent,)
            streams[n] = (kept, exchange(sent, b))
        rest = less(rest, b)

    own = call(sum_kernel, floats(count), (), own, after)
    moved, top, after = [], rest[0], (own,)
    for n in range(2):
        shapes = [message(sizes[n], width)] + [message(count, width)] * n
        used, used_sizes = ([streams[0]], sizes[:1]) if n == 0 else (streams, sizes)
        kept, came = zip(*used)
        sent = call(cross_kernel(used_sizes, top, n), shapes, (), (*kept, *came), after)
        after = (sent[0],)
        moved.append(cross(sent[0], top))
    near = cross(sent[1], None)
    early = []
    for n, (first, size) in enumerate(chunks):
        early.append(call(early_kernel(first), floats(size), (), (own, moved[n]), early[-1:], (), 10**9))
    result = jax.ShapeDtypeStruct((count, width, width), jnp.bfloat16)
    return call(last_kernel, result, (), (near, *early))[None, None]


def solution(mesh):
    spec = P("row", "col", "layer", None, None, None)
    return jax.shard_map(
        on_device,
        mesh=mesh,
        in_specs=(spec,) * 4,
        out_specs=P("row", "col", "layer", None, None),
        check_vma=False,
    )
```

```python
import jax
import jax.numpy as jnp
from jax import lax
from jax.experimental import pallas as pl
from jax.experimental.pallas import tpu as pltpu
from jax.sharding import PartitionSpec as P

PEAK = 32766.0
ROWS = 16
LANES = 128
GROUP = 8
SMEM = pltpu.MemorySpace.SMEM
VMEM = pltpu.MemorySpace.VMEM


def head_rows(count):
    return -(-count // ROWS) * ROWS


def message(count, width):
    return jax.ShapeDtypeStruct((count * width + head_rows(count), width), jnp.int16)


def encode(tile):
    top = jnp.max(jnp.abs(tile), axis=0, keepdims=True)
    power = jnp.floor(jnp.log2(jnp.maximum(top, 2.0**-100)) + 0.001) + 1.0
    scaled = jnp.round(tile * (jnp.exp2(-power) * PEAK))
    return scaled.astype(jnp.int32).astype(jnp.int16), power.astype(jnp.int32)


def new_head(count, width):
    return jnp.zeros((head_rows(count), width), jnp.int32)


def rows_at(slot, width):
    start = slot * width
    return pl.ds(start if isinstance(start, int) else pl.multiple_of(start, width), width)


def put_tile(ref, slot, tile, head):
    coded, power = encode(tile)
    ref[rows_at(slot, tile.shape[0]), :] = coded
    rows = lax.broadcasted_iota(jnp.int32, head.shape, 0)
    return jnp.where(rows == slot, power, head)


def put_head(ref, head):
    ref[pl.ds(ref.shape[0] - head.shape[0], head.shape[0]), :] = head.astype(jnp.int16)


def get_head(ref, count):
    rows = head_rows(count)
    return ref[pl.ds(ref.shape[0] - rows, rows), :].astype(jnp.int32)


def get_tile(ref, slot, head):
    rows = lax.broadcasted_iota(jnp.int32, head.shape, 0)
    power = jnp.sum(jnp.where(rows == slot, head, 0), axis=0, keepdims=True)
    coded = ref[rows_at(slot, ref.shape[-1]), :]
    return coded.astype(jnp.int32).astype(jnp.float32) * (jnp.exp2(power.astype(jnp.float32)) * (1.0 / PEAK))


def product(a_ref, p_ref, look, fan):
    chosen = [look(f) for f in range(fan)]
    left = jnp.concatenate([a_ref[pa] for pa, _ in chosen], axis=1)
    right = jnp.concatenate([p_ref[pp] for _, pp in chosen], axis=0)
    return jnp.dot(left, right, preferred_element_type=jnp.float32)


def own_bit(bit):
    return (lax.axis_index("layer") >> bit) & 1


def insert(rest, at, bit):
    low = rest & ((1 << at) - 1)
    return ((rest >> at) << (at + 1)) | (bit << at) | low


def loop(turns, body, start):
    return body(0, start) if turns == 1 else lax.fori_loop(0, turns, body, start)


def packing(slots, lanes):
    return max(1, lanes // slots)


def pack_kernel(ia_ref, ip_ref, own_ref, far_ref):
    fan, slots = ia_ref.shape[1:]
    per = packing(slots, own_ref.shape[1])
    col = lax.axis_index("col")
    for out_ref, column in ((own_ref, col), (far_ref, 1 - col)):
        for which, ref in enumerate((ia_ref, ip_ref)):
            lists = ref[column]
            for f in range(fan):
                row, at = divmod(which * fan + f, per)
                out_ref[pl.ds(row, 1), pl.ds(at * slots, slots)] = lists[f : f + 1]


def finder(lists_ref, fan, slots):
    per = packing(slots, lists_ref.shape[1])

    def place(which, f, t):
        row, at = divmod(which * fan + f, per)
        return lists_ref[row, at * slots + t]

    return lambda t: lambda f: (place(0, f, t), place(1, f, t))


def send_kernel(fan, slots, count, chunks, bits, joins):
    def kernel(lists_ref, a_ref, *refs):
        find = finder(lists_ref, fan, slots)
        n_out = len(chunks) + joins
        p_refs, out_refs = refs[:-n_out], refs[-n_out:]
        if joins:
            out_refs, p_ref = out_refs[:-1], out_refs[-1]
            held = p_ref.shape[0] // 2
            row = lax.axis_index("row")
            p_ref[pl.ds(row * held, held)] = p_refs[0][...]
            at = (1 - row) * held
            for ref in p_refs[1:]:
                p_ref[pl.ds(at, ref.shape[0])] = ref[...]
                at += ref.shape[0]
        else:
            (p_ref,) = p_refs
        width = p_ref.shape[-1]
        for (first, size), bit, out_ref in zip(chunks, bits, out_refs):
            side = 1 - own_bit(bit)
            total = out_ref.shape[0] // width

            def body(step, head):
                for k in range(GROUP):
                    slot = step * GROUP + k
                    layer = insert(slot // size, bit, side)
                    tile = product(a_ref, p_ref, find(layer * count + first + slot % size), fan)
                    head = put_tile(out_ref, slot, tile, head)
                return head

            put_head(out_ref, loop(total // GROUP, body, new_head(total, width)))

    return kernel


def keep_kernel(fan, slots, count, chunks, bits):
    def kernel(lists_ref, a_ref, p_ref, *out_refs):
        find = finder(lists_ref, fan, slots)
        for (first, size), bit, out_ref in zip(chunks, bits, out_refs):
            side = own_bit(bit)

            def body(step, _):
                for k in range(GROUP):
                    slot = step * GROUP + k
                    layer = insert(slot // size, bit, side)
                    out_ref[slot] = product(a_ref, p_ref, find(layer * count + first + slot % size), fan)
                return 0

            loop(out_ref.shape[0] // GROUP, body, 0)

    return kernel


def cross_kernel(sizes, bit, whose):
    def kernel(*refs):
        n = len(sizes)
        kept_refs, in_refs, out_refs = refs[:n], refs[n : 2 * n], refs[2 * n :]
        width = out_refs[0].shape[-1]
        mine = own_bit(bit)
        heads = [get_head(ref, ref.shape[0] // width) for ref in in_refs]

        def put(out_ref, side, chosen):
            count = out_ref.shape[0] // width
            head, slot = new_head(count, width), 0
            for c in chosen:
                for i in range(sizes[c]):
                    at = side * sizes[c] + i
                    tile = kept_refs[c][at] + get_tile(in_refs[c], at, heads[c])
                    head = put_tile(out_ref, slot, tile, head)
                    slot += 1
            put_head(out_ref, head)

        put(out_refs[0], 1 - mine, [whose])
        if len(out_refs) > 1:
            put(out_refs[1], mine, range(n))

    return kernel


def add_kernel(sizes, rest, bit):
    at = rest.index(bit)
    full = sum(sizes)
    halves = 1 << (len(rest) - 1)

    def kernel(*refs):
        n = len(sizes)
        kept_refs, in_refs, (sent_ref, stay_ref) = refs[:n], refs[n : 2 * n], refs[2 * n : 2 * n + 2]
        width = sent_ref.shape[-1]
        mine = own_bit(bit)
        heads = [get_head(ref, ref.shape[0] // width) for ref in in_refs]

        def sums(place):
            for size, kept_ref, in_ref, head in zip(sizes, kept_refs, in_refs, heads):
                for i in range(size):
                    slot = place * size + i
                    yield kept_ref[slot] + get_tile(in_ref, slot, head)

        def send(ref, side):
            def body(half, head):
                for i, tile in enumerate(sums(insert(half, at, side))):
                    head = put_tile(ref, half * full + i, tile, head)
                return head

            put_head(ref, lax.fori_loop(0, halves, body, new_head(halves * full, width), unroll=halves <= 4))

        send(sent_ref, 1 - mine)

        def body(half, _):
            for i, tile in enumerate(sums(insert(half, at, mine))):
                stay_ref[half * full + i] = tile
            return 0

        lax.fori_loop(0, halves, body, 0, unroll=halves <= 4)

    return kernel


def sum_kernel(kept_ref, in_ref, out_ref):
    count = out_ref.shape[0]
    head = get_head(in_ref, count)
    for i in range(count):
        out_ref[i] = kept_ref[i] + get_tile(in_ref, i, head)


def early_kernel(first):
    def kernel(own_ref, far_ref, out_ref):
        size = out_ref.shape[0]
        head = get_head(far_ref, size)
        for i in range(size):
            out_ref[i] = own_ref[first + i] + get_tile(far_ref, i, head)

    return kernel


def last_kernel(near_ref, *refs):
    early_refs, out_ref = refs[:-1], refs[-1]
    count = out_ref.shape[0]
    head, at = get_head(near_ref, count), 0
    for ref in early_refs:
        for i in range(ref.shape[0]):
            out_ref[at] = (ref[i] + get_tile(near_ref, at, head)).astype(out_ref.dtype)
            at += 1


def call(kernel, out_shape, smem, vmem, after=(), scratch=(), flops=0):
    outs = out_shape if isinstance(out_shape, (list, tuple)) else [out_shape]
    moved = sum(x.size * x.dtype.itemsize for x in (*smem, *vmem, *outs))
    n_real = len(smem) + len(vmem)

    def wrapped(*refs):
        kernel(*refs[:n_real], *refs[n_real + len(after) :])

    return pl.pallas_call(
        wrapped,
        out_shape=out_shape,
        in_specs=[pl.BlockSpec(memory_space=SMEM)] * len(smem)
        + [pl.BlockSpec(memory_space=VMEM)] * len(vmem)
        + [pl.BlockSpec(memory_space=pl.ANY)] * len(after),
        out_specs=jax.tree.map(lambda _: pl.BlockSpec(memory_space=VMEM), out_shape),
        scratch_shapes=list(scratch),
        compiler_params=pltpu.CompilerParams(vmem_limit_bytes=moved + 4 * 2**20),
        cost_estimate=pl.CostEstimate(flops=5 * flops, bytes_accessed=moved if flops else 1, transcendentals=0),
    )(*smem, *vmem, *after)


def hold(x, after):
    def kernel(*refs):
        pass

    return pl.pallas_call(
        kernel,
        out_shape=jax.ShapeDtypeStruct(x.shape, x.dtype),
        in_specs=[pl.BlockSpec(memory_space=pl.ANY)] * (1 + len(after)),
        out_specs=pl.BlockSpec(memory_space=pl.ANY),
        input_output_aliases={0: 0},
        compiler_params=pltpu.CompilerParams(vmem_limit_bytes=2**20),
    )(x, *after)


def on_device(a_tiles, p_tiles, pair_a, pair_p):
    a, p = a_tiles[0, 0, 0], p_tiles[0, 0, 0]
    ia, ip = jnp.swapaxes(pair_a[0, 0, 0], 1, 2), jnp.swapaxes(pair_p[0, 0, 0], 1, 2)
    fan, slots = ia.shape[1:]
    held, width = p.shape[0], p.shape[-1]
    layers = lax.axis_size("layer")
    bits = layers.bit_length() - 1
    count = slots // layers
    swap = [(0, 1), (1, 0)]

    half = count // 2
    chunks = [(0, half), (half, count - half)]
    flops = layers * half * fan * width**3

    def floats(size):
        return jax.ShapeDtypeStruct((size, width, width), jnp.float32)

    def exchange(x, bit):
        return lax.ppermute(x, "layer", [(i, i ^ (1 << bit)) for i in range(layers)])

    def cross(x, bit):
        flip = 0 if bit is None else 1 << bit
        perm = [(c * layers + i, (1 - c) * layers + (i ^ flip)) for c in range(2) for i in range(layers)]
        return lax.ppermute(x, ("col", "layer"), perm)

    def send(lists, vmem, which, bits, joins, after, cost):
        picked = [chunks[n] for n in which]
        shapes = [message(layers // 2 * size, width) for _, size in picked]
        if joins:
            shapes.append(jax.ShapeDtypeStruct((2 * held, width, width), p.dtype))
        kernel = send_kernel(fan, slots, count, picked, bits, joins)
        made = call(kernel, shapes, (lists,), vmem, after, (), cost * len(which) * flops)
        return made, [exchange(x, b) for x, b in zip(made, bits)]

    def keep(lists, vmem, bits, after, cost):
        shapes = [floats(layers // 2 * size) for _, size in chunks]
        kernel = keep_kernel(fan, slots, count, chunks, bits)
        return call(kernel, shapes, (lists,), vmem, after, (), cost * 2 * flops)

    def add(parts, sizes, rest, bit, after):
        n = sum(sizes) << (len(rest) - 1)
        shapes = [message(n, width), floats(n)]
        kept, came = zip(*parts)
        return call(add_kernel(sizes, rest, bit), shapes, (), (*kept, *came), after)

    own_bits, other_bits = (0, 1), (1, 0)
    sizes = [size for _, size in chunks]
    every = list(range(bits))

    def less(rest, bit):
        return [b for b in rest if b != bit]

    def second(kept, came, size, bit, after):
        sent, kept = add([(kept, came)], [size], less(every, bit), 1 - bit, after)
        return sent, (kept, exchange(sent, 1 - bit))

    p_x = lax.ppermute(p, "col", swap)
    p_r = lax.ppermute(p, "row", swap)
    packed = jax.ShapeDtypeStruct((-(-2 * fan // packing(slots, LANES)), max(slots, LANES)), jnp.int32)
    lists, lists_far = call(pack_kernel, [packed] * 2, (), (ia, ip))

    token = jax.ShapeDtypeStruct((8, width), jnp.float32)
    gate = call(lambda *refs: None, token, (), (), (), (), 10**9)
    gate = call(lambda *refs: None, token, (), (a, p), (gate,))

    (*made, joined), own_came = send(lists, (a, p, p_r), (0, 1), own_bits, True, (gate,), 1)
    own_kept = keep(lists, (a, joined), own_bits, made[:1], 1)
    lists_x = lax.ppermute(hold(lists_far, own_kept[:1]), "col", swap)
    parts, after = [], ()
    for n in range(2):
        sent, part = second(own_kept[n], own_came[n], sizes[n], own_bits[n], after)
        parts.append(part)
        after = (sent,)
    p_x = hold(p_x, (*after, lists_x))
    p_xr = lax.ppermute(p_x, "row", swap)

    (made, joined), came_0 = send(lists_x, (a, p_x, p_xr), (0,), other_bits[:1], True, (), 0)
    (made,), came_1 = send(lists_x, (a, joined), (1,), other_bits[1:], False, (made,), 0)
    other_came = came_0 + came_1
    rest, part_sizes, after = every[2:], sizes, (made,)
    for b in every[2:]:
        sent, kept = add(parts, part_sizes, rest, b, after)
        after = (sent,)
        parts, part_sizes = [(kept, exchange(sent, b))], [count]
        rest = less(rest, b)
    (own,) = parts
    other_kept = keep(lists_x, (a, joined), other_bits, after, 1)

    streams, after = [], (other_kept[0],)
    for n in range(2):
        sent, part = second(other_kept[n], other_came[n], sizes[n], other_bits[n], after)
        streams.append(part)
        after = (sent,)
    rest = every[2:]
    for b in every[2:-1]:
        for n in range(2):
            sent, kept = add([streams[n]], [sizes[n]], rest, b, after)
            after = (sent,)
            streams[n] = (kept, exchange(sent, b))
        rest = less(rest, b)

    own = call(sum_kernel, floats(count), (), own, after)
    moved, top, after = [], rest[0], (own,)
    for n in range(2):
        shapes = [message(sizes[n], width)] + [message(count, width)] * n
        used, used_sizes = ([streams[0]], sizes[:1]) if n == 0 else (streams, sizes)
        kept, came = zip(*used)
        sent = call(cross_kernel(used_sizes, top, n), shapes, (), (*kept, *came), after)
        after = (sent[0],)
        moved.append(cross(sent[0], top))
    near = cross(sent[1], None)
    early = []
    for n, (first, size) in enumerate(chunks):
        early.append(call(early_kernel(first), floats(size), (), (own, moved[n]), early[-1:], (), 10**9))
    result = jax.ShapeDtypeStruct((count, width, width), jnp.bfloat16)
    return call(last_kernel, result, (), (near, *early))[None, None]


def solution(mesh):
    spec = P("row", "col", "layer", None, None, None)
    return jax.shard_map(
        on_device,
        mesh=mesh,
        in_specs=(spec,) * 4,
        out_specs=P("row", "col", "layer", None, None),
        check_vma=False,
    )
```

```python
import jax
import jax.numpy as jnp
from jax import lax
from jax.experimental import pallas as pl
from jax.experimental.pallas import tpu as pltpu
from jax.sharding import PartitionSpec as P

PEAK = 32766.0
ROWS = 16
LANES = 128
GROUP = 8
SMEM = pltpu.MemorySpace.SMEM
VMEM = pltpu.MemorySpace.VMEM


def head_rows(count):
    return -(-count // ROWS) * ROWS


def message(count, width):
    return jax.ShapeDtypeStruct((count * width + head_rows(count), width), jnp.int16)


def encode(tile):
    top = jnp.max(jnp.abs(tile), axis=0, keepdims=True)
    power = jnp.floor(jnp.log2(jnp.maximum(top, 2.0**-100)) + 0.001) + 1.0
    scaled = jnp.round(tile * (jnp.exp2(-power) * PEAK))
    return scaled.astype(jnp.int32).astype(jnp.int16), power.astype(jnp.int32)


def new_head(count, width):
    return jnp.zeros((head_rows(count), width), jnp.int32)


def rows_at(slot, width):
    start = slot * width
    return pl.ds(start if isinstance(start, int) else pl.multiple_of(start, width), width)


def put_tile(ref, slot, tile, head):
    coded, power = encode(tile)
    ref[rows_at(slot, tile.shape[0]), :] = coded
    rows = lax.broadcasted_iota(jnp.int32, head.shape, 0)
    return jnp.where(rows == slot, power, head)


def put_head(ref, head):
    ref[pl.ds(ref.shape[0] - head.shape[0], head.shape[0]), :] = head.astype(jnp.int16)


def get_head(ref, count):
    rows = head_rows(count)
    return ref[pl.ds(ref.shape[0] - rows, rows), :].astype(jnp.int32)


def get_tile(ref, slot, head):
    rows = lax.broadcasted_iota(jnp.int32, head.shape, 0)
    power = jnp.sum(jnp.where(rows == slot, head, 0), axis=0, keepdims=True)
    coded = ref[rows_at(slot, ref.shape[-1]), :]
    return coded.astype(jnp.int32).astype(jnp.float32) * (jnp.exp2(power.astype(jnp.float32)) * (1.0 / PEAK))


def product(a_ref, p_ref, look, fan):
    chosen = [look(f) for f in range(fan)]
    left = jnp.concatenate([a_ref[pa] for pa, _ in chosen], axis=1)
    right = jnp.concatenate([p_ref[pp] for _, pp in chosen], axis=0)
    return jnp.dot(left, right, preferred_element_type=jnp.float32)


def own_bit(bit):
    return (lax.axis_index("layer") >> bit) & 1


def insert(rest, at, bit):
    low = rest & ((1 << at) - 1)
    return ((rest >> at) << (at + 1)) | (bit << at) | low


def loop(turns, body, start):
    return body(0, start) if turns == 1 else lax.fori_loop(0, turns, body, start)


def packing(slots, lanes):
    return max(1, lanes // slots)


def pack_kernel(ia_ref, ip_ref, own_ref, far_ref):
    fan, slots = ia_ref.shape[1:]
    per = packing(slots, own_ref.shape[1])
    col = lax.axis_index("col")
    for out_ref, column in ((own_ref, col), (far_ref, 1 - col)):
        for which, ref in enumerate((ia_ref, ip_ref)):
            lists = ref[column]
            for f in range(fan):
                row, at = divmod(which * fan + f, per)
                out_ref[pl.ds(row, 1), pl.ds(at * slots, slots)] = lists[f : f + 1]


def finder(lists_ref, fan, slots):
    per = packing(slots, lists_ref.shape[1])

    def place(which, f, t):
        row, at = divmod(which * fan + f, per)
        return lists_ref[row, at * slots + t]

    return lambda t: lambda f: (place(0, f, t), place(1, f, t))


def send_kernel(fan, slots, count, chunks, bits, joins):
    def kernel(lists_ref, a_ref, *refs):
        find = finder(lists_ref, fan, slots)
        n_out = len(chunks) + joins
        p_refs, out_refs = refs[:-n_out], refs[-n_out:]
        if joins:
            out_refs, p_ref = out_refs[:-1], out_refs[-1]
            held = p_ref.shape[0] // 2
            row = lax.axis_index("row")
            p_ref[pl.ds(row * held, held)] = p_refs[0][...]
            at = (1 - row) * held
            for ref in p_refs[1:]:
                p_ref[pl.ds(at, ref.shape[0])] = ref[...]
                at += ref.shape[0]
        else:
            (p_ref,) = p_refs
        width = p_ref.shape[-1]
        for (first, size), bit, out_ref in zip(chunks, bits, out_refs):
            side = 1 - own_bit(bit)
            total = out_ref.shape[0] // width

            def body(step, head):
                for k in range(GROUP):
                    slot = step * GROUP + k
                    layer = insert(slot // size, bit, side)
                    tile = product(a_ref, p_ref, find(layer * count + first + slot % size), fan)
                    head = put_tile(out_ref, slot, tile, head)
                return head

            put_head(out_ref, loop(total // GROUP, body, new_head(total, width)))

    return kernel


def keep_kernel(fan, slots, count, chunks, bits):
    def kernel(lists_ref, a_ref, p_ref, *out_refs):
        find = finder(lists_ref, fan, slots)
        for (first, size), bit, out_ref in zip(chunks, bits, out_refs):
            side = own_bit(bit)

            def body(step, _):
                for k in range(GROUP):
                    slot = step * GROUP + k
                    layer = insert(slot // size, bit, side)
                    out_ref[slot] = product(a_ref, p_ref, find(layer * count + first + slot % size), fan)
                return 0

            loop(out_ref.shape[0] // GROUP, body, 0)

    return kernel


def cross_kernel(sizes, bit, whose):
    def kernel(*refs):
        n = len(sizes)
        kept_refs, in_refs, out_refs = refs[:n], refs[n : 2 * n], refs[2 * n :]
        width = out_refs[0].shape[-1]
        mine = own_bit(bit)
        heads = [get_head(ref, ref.shape[0] // width) for ref in in_refs]

        def put(out_ref, side, chosen):
            count = out_ref.shape[0] // width
            head, slot = new_head(count, width), 0
            for c in chosen:
                for i in range(sizes[c]):
                    at = side * sizes[c] + i
                    tile = kept_refs[c][at] + get_tile(in_refs[c], at, heads[c])
                    head = put_tile(out_ref, slot, tile, head)
                    slot += 1
            put_head(out_ref, head)

        put(out_refs[0], 1 - mine, [whose])
        if len(out_refs) > 1:
            put(out_refs[1], mine, range(n))

    return kernel


def add_kernel(sizes, rest, bit):
    at = rest.index(bit)
    full = sum(sizes)
    halves = 1 << (len(rest) - 1)

    def kernel(*refs):
        n = len(sizes)
        kept_refs, in_refs, (sent_ref, stay_ref) = refs[:n], refs[n : 2 * n], refs[2 * n : 2 * n + 2]
        width = sent_ref.shape[-1]
        mine = own_bit(bit)
        heads = [get_head(ref, ref.shape[0] // width) for ref in in_refs]

        def sums(place):
            for size, kept_ref, in_ref, head in zip(sizes, kept_refs, in_refs, heads):
                for i in range(size):
                    slot = place * size + i
                    yield kept_ref[slot] + get_tile(in_ref, slot, head)

        def send(ref, side):
            def body(half, head):
                for i, tile in enumerate(sums(insert(half, at, side))):
                    head = put_tile(ref, half * full + i, tile, head)
                return head

            put_head(ref, lax.fori_loop(0, halves, body, new_head(halves * full, width), unroll=halves <= 4))

        send(sent_ref, 1 - mine)

        def body(half, _):
            for i, tile in enumerate(sums(insert(half, at, mine))):
                stay_ref[half * full + i] = tile
            return 0

        lax.fori_loop(0, halves, body, 0, unroll=halves <= 4)

    return kernel


def sum_kernel(kept_ref, in_ref, out_ref):
    count = out_ref.shape[0]
    head = get_head(in_ref, count)
    for i in range(count):
        out_ref[i] = kept_ref[i] + get_tile(in_ref, i, head)


def early_kernel(first):
    def kernel(own_ref, far_ref, out_ref):
        size = out_ref.shape[0]
        head = get_head(far_ref, size)
        for i in range(size):
            out_ref[i] = own_ref[first + i] + get_tile(far_ref, i, head)

    return kernel


def last_kernel(near_ref, *refs):
    early_refs, out_ref = refs[:-1], refs[-1]
    count = out_ref.shape[0]
    head, at = get_head(near_ref, count), 0
    for ref in early_refs:
        for i in range(ref.shape[0]):
            out_ref[at] = (ref[i] + get_tile(near_ref, at, head)).astype(out_ref.dtype)
            at += 1


def call(kernel, out_shape, smem, vmem, after=(), scratch=(), flops=0):
    outs = out_shape if isinstance(out_shape, (list, tuple)) else [out_shape]
    moved = sum(x.size * x.dtype.itemsize for x in (*smem, *vmem, *outs))
    n_real = len(smem) + len(vmem)

    def wrapped(*refs):
        kernel(*refs[:n_real], *refs[n_real + len(after) :])

    return pl.pallas_call(
        wrapped,
        out_shape=out_shape,
        in_specs=[pl.BlockSpec(memory_space=SMEM)] * len(smem)
        + [pl.BlockSpec(memory_space=VMEM)] * len(vmem)
        + [pl.BlockSpec(memory_space=pl.ANY)] * len(after),
        out_specs=jax.tree.map(lambda _: pl.BlockSpec(memory_space=VMEM), out_shape),
        scratch_shapes=list(scratch),
        compiler_params=pltpu.CompilerParams(vmem_limit_bytes=moved + 4 * 2**20),
        cost_estimate=pl.CostEstimate(flops=int(5 * flops), bytes_accessed=moved if flops else 1, transcendentals=0),
    )(*smem, *vmem, *after)


def hold(x, after):
    def kernel(*refs):
        pass

    return pl.pallas_call(
        kernel,
        out_shape=jax.ShapeDtypeStruct(x.shape, x.dtype),
        in_specs=[pl.BlockSpec(memory_space=pl.ANY)] * (1 + len(after)),
        out_specs=pl.BlockSpec(memory_space=pl.ANY),
        input_output_aliases={0: 0},
        compiler_params=pltpu.CompilerParams(vmem_limit_bytes=2**20),
    )(x, *after)


def on_device(a_tiles, p_tiles, pair_a, pair_p):
    a, p = a_tiles[0, 0, 0], p_tiles[0, 0, 0]
    ia, ip = jnp.swapaxes(pair_a[0, 0, 0], 1, 2), jnp.swapaxes(pair_p[0, 0, 0], 1, 2)
    fan, slots = ia.shape[1:]
    held, width = p.shape[0], p.shape[-1]
    layers = lax.axis_size("layer")
    bits = layers.bit_length() - 1
    count = slots // layers
    swap = [(0, 1), (1, 0)]

    half = count // 2
    chunks = [(0, half), (half, count - half)]
    flops = layers * half * fan * width**3

    def floats(size):
        return jax.ShapeDtypeStruct((size, width, width), jnp.float32)

    def exchange(x, bit):
        return lax.ppermute(x, "layer", [(i, i ^ (1 << bit)) for i in range(layers)])

    def cross(x, bit):
        flip = 0 if bit is None else 1 << bit
        perm = [(c * layers + i, (1 - c) * layers + (i ^ flip)) for c in range(2) for i in range(layers)]
        return lax.ppermute(x, ("col", "layer"), perm)

    def send(lists, vmem, which, bits, joins, after, cost):
        picked = [chunks[n] for n in which]
        shapes = [message(layers // 2 * size, width) for _, size in picked]
        if joins:
            shapes.append(jax.ShapeDtypeStruct((2 * held, width, width), p.dtype))
        kernel = send_kernel(fan, slots, count, picked, bits, joins)
        made = call(kernel, shapes, (lists,), vmem, after, (), cost * len(which) * flops)
        return made, [exchange(x, b) for x, b in zip(made, bits)]

    def keep(lists, vmem, bits, after, cost):
        shapes = [floats(layers // 2 * size) for _, size in chunks]
        kernel = keep_kernel(fan, slots, count, chunks, bits)
        return call(kernel, shapes, (lists,), vmem, after, (), cost * 2 * flops)

    def add(parts, sizes, rest, bit, after):
        n = sum(sizes) << (len(rest) - 1)
        shapes = [message(n, width), floats(n)]
        kept, came = zip(*parts)
        return call(add_kernel(sizes, rest, bit), shapes, (), (*kept, *came), after)

    own_bits, other_bits = (0, 1), (1, 0)
    sizes = [size for _, size in chunks]
    every = list(range(bits))

    def less(rest, bit):
        return [b for b in rest if b != bit]

    def second(kept, came, size, bit, after):
        sent, kept = add([(kept, came)], [size], less(every, bit), 1 - bit, after)
        return sent, (kept, exchange(sent, 1 - bit))

    p_x = lax.ppermute(p, "col", swap)
    p_r = lax.ppermute(p, "row", swap)
    packed = jax.ShapeDtypeStruct((-(-2 * fan // packing(slots, LANES)), max(slots, LANES)), jnp.int32)
    lists, lists_far = call(pack_kernel, [packed] * 2, (), (ia, ip))

    token = jax.ShapeDtypeStruct((8, width), jnp.float32)
    gate = call(lambda *refs: None, token, (), (), (), (), 10**9)
    gate = call(lambda *refs: None, token, (), (a, p), (gate,))

    (*made, joined), own_came = send(lists, (a, p, p_r), (0, 1), own_bits, True, (gate,), 1)
    own_kept = keep(lists, (a, joined), own_bits, made[:1], 1)
    lists_x = lax.ppermute(hold(lists_far, own_kept[:1]), "col", swap)
    parts, after = [], ()
    for n in range(2):
        sent, part = second(own_kept[n], own_came[n], sizes[n], own_bits[n], after)
        parts.append(part)
        after = (sent,)
    p_x = hold(p_x, (*after, lists_x))
    p_xr = lax.ppermute(p_x, "row", swap)

    (made, joined), came_0 = send(lists_x, (a, p_x, p_xr), (0,), other_bits[:1], True, (), 0)
    (made,), came_1 = send(lists_x, (a, joined), (1,), other_bits[1:], False, (made,), 0)
    other_came = came_0 + came_1
    other_kept = keep(lists_x, (a, joined), other_bits, (made,), 1)

    rest, part_sizes, after = every[2:], sizes, other_kept[:1]
    for b in every[2:]:
        sent, kept = add(parts, part_sizes, rest, b, after)
        after = (sent,)
        parts, part_sizes = [(kept, exchange(sent, b))], [count]
        rest = less(rest, b)
    (own,) = parts
    streams = []
    for n in range(2):
        sent, part = second(other_kept[n], other_came[n], sizes[n], other_bits[n], after)
        streams.append(part)
        after = (sent,)
    rest = every[2:]
    for b in every[2:-1]:
        for n in range(2):
            sent, kept = add([streams[n]], [sizes[n]], rest, b, after)
            after = (sent,)
            streams[n] = (kept, exchange(sent, b))
        rest = less(rest, b)

    own = call(sum_kernel, floats(count), (), own, after)
    moved, top, after = [], rest[0], (own,)
    for n in range(2):
        shapes = [message(sizes[n], width)] + [message(count, width)] * n
        used, used_sizes = ([streams[0]], sizes[:1]) if n == 0 else (streams, sizes)
        kept, came = zip(*used)
        sent = call(cross_kernel(used_sizes, top, n), shapes, (), (*kept, *came), after)
        after = (sent[0],)
        moved.append(cross(sent[0], top))
    near = cross(sent[1], None)
    early = []
    for n, (first, size) in enumerate(chunks):
        early.append(call(early_kernel(first), floats(size), (), (own, moved[n]), early[-1:], (), 10**9))
    result = jax.ShapeDtypeStruct((count, width, width), jnp.bfloat16)
    return call(last_kernel, result, (), (near, *early))[None, None]


def solution(mesh):
    spec = P("row", "col", "layer", None, None, None)
    return jax.shard_map(
        on_device,
        mesh=mesh,
        in_specs=(spec,) * 4,
        out_specs=P("row", "col", "layer", None, None),
        check_vma=False,
    )
```

```python
import jax
import jax.numpy as jnp
from jax import lax
from jax.experimental import pallas as pl
from jax.experimental.pallas import tpu as pltpu
from jax.sharding import PartitionSpec as P

PEAK = 32766.0
ROWS = 16
LANES = 128
GROUP = 8
SMEM = pltpu.MemorySpace.SMEM
VMEM = pltpu.MemorySpace.VMEM


def head_rows(count):
    return -(-count // ROWS) * ROWS


def message(count, width):
    return jax.ShapeDtypeStruct((count * width + head_rows(count), width), jnp.int16)


def encode(tile):
    top = jnp.max(jnp.abs(tile), axis=0, keepdims=True)
    power = jnp.floor(jnp.log2(jnp.maximum(top, 2.0**-100)) + 0.001) + 1.0
    scaled = jnp.round(tile * (jnp.exp2(-power) * PEAK))
    return scaled.astype(jnp.int32).astype(jnp.int16), power.astype(jnp.int32)


def new_head(count, width):
    return jnp.zeros((head_rows(count), width), jnp.int32)


def rows_at(slot, width):
    start = slot * width
    return pl.ds(start if isinstance(start, int) else pl.multiple_of(start, width), width)


def put_tile(ref, slot, tile, head):
    coded, power = encode(tile)
    ref[rows_at(slot, tile.shape[0]), :] = coded
    rows = lax.broadcasted_iota(jnp.int32, head.shape, 0)
    return jnp.where(rows == slot, power, head)


def put_head(ref, head):
    ref[pl.ds(ref.shape[0] - head.shape[0], head.shape[0]), :] = head.astype(jnp.int16)


def get_head(ref, count):
    rows = head_rows(count)
    return ref[pl.ds(ref.shape[0] - rows, rows), :].astype(jnp.int32)


def get_tile(ref, slot, head):
    rows = lax.broadcasted_iota(jnp.int32, head.shape, 0)
    power = jnp.sum(jnp.where(rows == slot, head, 0), axis=0, keepdims=True)
    coded = ref[rows_at(slot, ref.shape[-1]), :]
    return coded.astype(jnp.int32).astype(jnp.float32) * (jnp.exp2(power.astype(jnp.float32)) * (1.0 / PEAK))


def product(a_ref, p_ref, look, fan):
    chosen = [look(f) for f in range(fan)]
    left = jnp.concatenate([a_ref[pa] for pa, _ in chosen], axis=1)
    right = jnp.concatenate([p_ref[pp] for _, pp in chosen], axis=0)
    return jnp.dot(left, right, preferred_element_type=jnp.float32)


def own_bit(bit):
    return (lax.axis_index("layer") >> bit) & 1


def insert(rest, at, bit):
    low = rest & ((1 << at) - 1)
    return ((rest >> at) << (at + 1)) | (bit << at) | low


def loop(turns, body, start):
    return body(0, start) if turns == 1 else lax.fori_loop(0, turns, body, start)


def packing(slots, lanes):
    return max(1, lanes // slots)


def pack_kernel(ia_ref, ip_ref, own_ref, far_ref):
    fan, slots = ia_ref.shape[1:]
    per = packing(slots, own_ref.shape[1])
    col = lax.axis_index("col")
    for out_ref, column in ((own_ref, col), (far_ref, 1 - col)):
        for which, ref in enumerate((ia_ref, ip_ref)):
            lists = ref[column]
            for f in range(fan):
                row, at = divmod(which * fan + f, per)
                out_ref[pl.ds(row, 1), pl.ds(at * slots, slots)] = lists[f : f + 1]


def finder(lists_ref, fan, slots):
    per = packing(slots, lists_ref.shape[1])

    def place(which, f, t):
        row, at = divmod(which * fan + f, per)
        return lists_ref[row, at * slots + t]

    return lambda t: lambda f: (place(0, f, t), place(1, f, t))


def send_kernel(fan, slots, count, chunks, bits, joins):
    def kernel(lists_ref, a_ref, *refs):
        find = finder(lists_ref, fan, slots)
        n_out = len(chunks) + joins
        p_refs, out_refs = refs[:-n_out], refs[-n_out:]
        if joins:
            out_refs, p_ref = out_refs[:-1], out_refs[-1]
            held = p_ref.shape[0] // 2
            row = lax.axis_index("row")
            p_ref[pl.ds(row * held, held)] = p_refs[0][...]
            at = (1 - row) * held
            for ref in p_refs[1:]:
                p_ref[pl.ds(at, ref.shape[0])] = ref[...]
                at += ref.shape[0]
        else:
            (p_ref,) = p_refs
        width = p_ref.shape[-1]
        for (first, size), bit, out_ref in zip(chunks, bits, out_refs):
            side = 1 - own_bit(bit)
            total = out_ref.shape[0] // width

            def body(step, head):
                for k in range(GROUP):
                    slot = step * GROUP + k
                    layer = insert(slot // size, bit, side)
                    tile = product(a_ref, p_ref, find(layer * count + first + slot % size), fan)
                    head = put_tile(out_ref, slot, tile, head)
                return head

            put_head(out_ref, loop(total // GROUP, body, new_head(total, width)))

    return kernel


def keep_kernel(fan, slots, count, chunks, bits):
    def kernel(lists_ref, a_ref, p_ref, *out_refs):
        find = finder(lists_ref, fan, slots)
        for (first, size), bit, out_ref in zip(chunks, bits, out_refs):
            side = own_bit(bit)

            def body(step, _):
                for k in range(GROUP):
                    slot = step * GROUP + k
                    layer = insert(slot // size, bit, side)
                    out_ref[slot] = product(a_ref, p_ref, find(layer * count + first + slot % size), fan)
                return 0

            loop(out_ref.shape[0] // GROUP, body, 0)

    return kernel


def cross_kernel(sizes, bit, whose):
    def kernel(*refs):
        n = len(sizes)
        kept_refs, in_refs, out_refs = refs[:n], refs[n : 2 * n], refs[2 * n :]
        width = out_refs[0].shape[-1]
        mine = own_bit(bit)
        heads = [get_head(ref, ref.shape[0] // width) for ref in in_refs]

        def put(out_ref, side, chosen):
            count = out_ref.shape[0] // width
            head, slot = new_head(count, width), 0
            for c in chosen:
                for i in range(sizes[c]):
                    at = side * sizes[c] + i
                    tile = kept_refs[c][at] + get_tile(in_refs[c], at, heads[c])
                    head = put_tile(out_ref, slot, tile, head)
                    slot += 1
            put_head(out_ref, head)

        put(out_refs[0], 1 - mine, [whose])
        if len(out_refs) > 1:
            put(out_refs[1], mine, range(n))

    return kernel


def add_kernel(sizes, rest, bit):
    at = rest.index(bit)
    full = sum(sizes)
    halves = 1 << (len(rest) - 1)

    def kernel(*refs):
        n = len(sizes)
        kept_refs, in_refs, (sent_ref, stay_ref) = refs[:n], refs[n : 2 * n], refs[2 * n : 2 * n + 2]
        width = sent_ref.shape[-1]
        mine = own_bit(bit)
        heads = [get_head(ref, ref.shape[0] // width) for ref in in_refs]

        def sums(place):
            for size, kept_ref, in_ref, head in zip(sizes, kept_refs, in_refs, heads):
                for i in range(size):
                    slot = place * size + i
                    yield kept_ref[slot] + get_tile(in_ref, slot, head)

        def send(ref, side):
            def body(half, head):
                for i, tile in enumerate(sums(insert(half, at, side))):
                    head = put_tile(ref, half * full + i, tile, head)
                return head

            put_head(ref, lax.fori_loop(0, halves, body, new_head(halves * full, width), unroll=halves <= 4))

        send(sent_ref, 1 - mine)

        def body(half, _):
            for i, tile in enumerate(sums(insert(half, at, mine))):
                stay_ref[half * full + i] = tile
            return 0

        lax.fori_loop(0, halves, body, 0, unroll=halves <= 4)

    return kernel


def sum_kernel(kept_ref, in_ref, out_ref):
    count = out_ref.shape[0]
    head = get_head(in_ref, count)
    for i in range(count):
        out_ref[i] = kept_ref[i] + get_tile(in_ref, i, head)


def early_kernel(first):
    def kernel(own_ref, far_ref, out_ref):
        size = out_ref.shape[0]
        head = get_head(far_ref, size)
        for i in range(size):
            out_ref[i] = own_ref[first + i] + get_tile(far_ref, i, head)

    return kernel


def last_kernel(near_ref, *refs):
    early_refs, out_ref = refs[:-1], refs[-1]
    count = out_ref.shape[0]
    head, at = get_head(near_ref, count), 0
    for ref in early_refs:
        for i in range(ref.shape[0]):
            out_ref[at] = (ref[i] + get_tile(near_ref, at, head)).astype(out_ref.dtype)
            at += 1


def call(kernel, out_shape, smem, vmem, after=(), scratch=(), flops=0):
    outs = out_shape if isinstance(out_shape, (list, tuple)) else [out_shape]
    moved = sum(x.size * x.dtype.itemsize for x in (*smem, *vmem, *outs))
    n_real = len(smem) + len(vmem)

    def wrapped(*refs):
        kernel(*refs[:n_real], *refs[n_real + len(after) :])

    return pl.pallas_call(
        wrapped,
        out_shape=out_shape,
        in_specs=[pl.BlockSpec(memory_space=SMEM)] * len(smem)
        + [pl.BlockSpec(memory_space=VMEM)] * len(vmem)
        + [pl.BlockSpec(memory_space=pl.ANY)] * len(after),
        out_specs=jax.tree.map(lambda _: pl.BlockSpec(memory_space=VMEM), out_shape),
        scratch_shapes=list(scratch),
        compiler_params=pltpu.CompilerParams(vmem_limit_bytes=moved + 4 * 2**20),
        cost_estimate=pl.CostEstimate(flops=int(5 * flops), bytes_accessed=moved if flops else 1, transcendentals=0),
    )(*smem, *vmem, *after)


def hold(x, after):
    def kernel(*refs):
        pass

    return pl.pallas_call(
        kernel,
        out_shape=jax.ShapeDtypeStruct(x.shape, x.dtype),
        in_specs=[pl.BlockSpec(memory_space=pl.ANY)] * (1 + len(after)),
        out_specs=pl.BlockSpec(memory_space=pl.ANY),
        input_output_aliases={0: 0},
        compiler_params=pltpu.CompilerParams(vmem_limit_bytes=2**20),
    )(x, *after)


def on_device(a_tiles, p_tiles, pair_a, pair_p):
    a, p = a_tiles[0, 0, 0], p_tiles[0, 0, 0]
    ia, ip = jnp.swapaxes(pair_a[0, 0, 0], 1, 2), jnp.swapaxes(pair_p[0, 0, 0], 1, 2)
    fan, slots = ia.shape[1:]
    held, width = p.shape[0], p.shape[-1]
    layers = lax.axis_size("layer")
    bits = layers.bit_length() - 1
    count = slots // layers
    swap = [(0, 1), (1, 0)]

    half = count // 2
    chunks = [(0, half), (half, count - half)]
    flops = layers * half * fan * width**3

    def floats(size):
        return jax.ShapeDtypeStruct((size, width, width), jnp.float32)

    def exchange(x, bit):
        return lax.ppermute(x, "layer", [(i, i ^ (1 << bit)) for i in range(layers)])

    def cross(x, bit):
        flip = 0 if bit is None else 1 << bit
        perm = [(c * layers + i, (1 - c) * layers + (i ^ flip)) for c in range(2) for i in range(layers)]
        return lax.ppermute(x, ("col", "layer"), perm)

    def send(lists, vmem, which, bits, joins, after, cost):
        picked = [chunks[n] for n in which]
        shapes = [message(layers // 2 * size, width) for _, size in picked]
        if joins:
            shapes.append(jax.ShapeDtypeStruct((2 * held, width, width), p.dtype))
        kernel = send_kernel(fan, slots, count, picked, bits, joins)
        made = call(kernel, shapes, (lists,), vmem, after, (), cost * len(which) * flops)
        return made, [exchange(x, b) for x, b in zip(made, bits)]

    def keep(lists, vmem, bits, after, cost):
        shapes = [floats(layers // 2 * size) for _, size in chunks]
        kernel = keep_kernel(fan, slots, count, chunks, bits)
        return call(kernel, shapes, (lists,), vmem, after, (), cost * 2 * flops)

    def add(parts, sizes, rest, bit, after):
        n = sum(sizes) << (len(rest) - 1)
        shapes = [message(n, width), floats(n)]
        kept, came = zip(*parts)
        return call(add_kernel(sizes, rest, bit), shapes, (), (*kept, *came), after)

    own_bits, other_bits = (0, 1), (1, 0)
    sizes = [size for _, size in chunks]
    every = list(range(bits))

    def less(rest, bit):
        return [b for b in rest if b != bit]

    def second(kept, came, size, bit, after):
        sent, kept = add([(kept, came)], [size], less(every, bit), 1 - bit, after)
        return sent, (kept, exchange(sent, 1 - bit))

    p_x = lax.ppermute(p, "col", swap)
    p_r = lax.ppermute(p, "row", swap)
    packed = jax.ShapeDtypeStruct((-(-2 * fan // packing(slots, LANES)), max(slots, LANES)), jnp.int32)
    lists, lists_far = call(pack_kernel, [packed] * 2, (), (ia, ip))

    token = jax.ShapeDtypeStruct((8, width), jnp.float32)
    gate = call(lambda *refs: None, token, (), (), (), (), 10**9)
    gate = call(lambda *refs: None, token, (), (a, p), (gate,))

    (*made, joined), own_came = send(lists, (a, p, p_r), (0, 1), own_bits, True, (gate,), 1)
    own_kept = keep(lists, (a, joined), own_bits, made[:1], 1)
    lists_x = lax.ppermute(hold(lists_far, own_kept[:1]), "col", swap)
    parts, after = [], ()
    for n in range(2):
        sent, part = second(own_kept[n], own_came[n], sizes[n], own_bits[n], after)
        parts.append(part)
        after = (sent,)
    p_x = hold(p_x, (*after, lists_x))
    p_xr = lax.ppermute(p_x, "row", swap)

    (made, joined), came_0 = send(lists_x, (a, p_x, p_xr), (0,), other_bits[:1], True, (), 0)
    (made,), came_1 = send(lists_x, (a, joined), (1,), other_bits[1:], False, (made,), 0)
    other_came = came_0 + came_1
    other_kept = keep(lists_x, (a, joined), other_bits, (made,), 1)

    rest, part_sizes, after = every[2:], sizes, other_kept[:1]
    for b in every[2:]:
        sent, kept = add(parts, part_sizes, rest, b, after)
        after = (sent,)
        parts, part_sizes = [(kept, exchange(sent, b))], [count]
        rest = less(rest, b)
    (own,) = parts
    streams = []
    for n in range(2):
        sent, part = second(other_kept[n], other_came[n], sizes[n], other_bits[n], after)
        streams.append(part)
        after = (sent,)
    rest = every[2:]
    for b in every[2:-1]:
        for n in range(2):
            sent, kept = add([streams[n]], [sizes[n]], rest, b, after)
            after = (sent,)
            streams[n] = (kept, exchange(sent, b))
        rest = less(rest, b)

    moved, top = [], rest[0]
    for n in range(2):
        shapes = [message(sizes[n], width)] + [message(count, width)] * n
        used, used_sizes = ([streams[0]], sizes[:1]) if n == 0 else (streams, sizes)
        kept, came = zip(*used)
        sent = call(cross_kernel(used_sizes, top, n), shapes, (), (*kept, *came), after)
        after = (sent[0],)
        moved.append(cross(sent[0], top))
        if n == 0:
            own = call(sum_kernel, floats(count), (), own, after)
            after = (own,)
    near = cross(sent[1], None)
    early = []
    for n, (first, size) in enumerate(chunks):
        early.append(call(early_kernel(first), floats(size), (), (own, moved[n]), early[-1:], (), 10**9))
    result = jax.ShapeDtypeStruct((count, width, width), jnp.bfloat16)
    return call(last_kernel, result, (), (near, *early))[None, None]


def solution(mesh):
    spec = P("row", "col", "layer", None, None, None)
    return jax.shard_map(
        on_device,
        mesh=mesh,
        in_specs=(spec,) * 4,
        out_specs=P("row", "col", "layer", None, None),
        check_vma=False,
    )
```

```python
import jax
import jax.numpy as jnp
from jax import lax
from jax.experimental import pallas as pl
from jax.experimental.pallas import tpu as pltpu
from jax.sharding import PartitionSpec as P

PEAK = 32766.0
ROWS = 16
LANES = 128
GROUP = 8
SMEM = pltpu.MemorySpace.SMEM
VMEM = pltpu.MemorySpace.VMEM


def head_rows(count):
    return -(-count // ROWS) * ROWS


def message(count, width):
    return jax.ShapeDtypeStruct((count * width + head_rows(count), width), jnp.int16)


def encode(tile):
    top = jnp.max(jnp.abs(tile), axis=0, keepdims=True)
    power = jnp.floor(jnp.log2(jnp.maximum(top, 2.0**-100)) + 0.001) + 1.0
    scaled = jnp.round(tile * (jnp.exp2(-power) * PEAK))
    return scaled.astype(jnp.int32).astype(jnp.int16), power.astype(jnp.int32)


def new_head(count, width):
    return jnp.zeros((head_rows(count), width), jnp.int32)


def rows_at(slot, width):
    start = slot * width
    return pl.ds(start if isinstance(start, int) else pl.multiple_of(start, width), width)


def put_tile(ref, slot, tile, head):
    coded, power = encode(tile)
    ref[rows_at(slot, tile.shape[0]), :] = coded
    rows = lax.broadcasted_iota(jnp.int32, head.shape, 0)
    return jnp.where(rows == slot, power, head)


def put_head(ref, head):
    ref[pl.ds(ref.shape[0] - head.shape[0], head.shape[0]), :] = head.astype(jnp.int16)


def get_head(ref, count):
    rows = head_rows(count)
    return ref[pl.ds(ref.shape[0] - rows, rows), :].astype(jnp.int32)


def get_tile(ref, slot, head):
    rows = lax.broadcasted_iota(jnp.int32, head.shape, 0)
    power = jnp.sum(jnp.where(rows == slot, head, 0), axis=0, keepdims=True)
    coded = ref[rows_at(slot, ref.shape[-1]), :]
    return coded.astype(jnp.int32).astype(jnp.float32) * (jnp.exp2(power.astype(jnp.float32)) * (1.0 / PEAK))


def product(a_ref, p_ref, look, fan):
    chosen = [look(f) for f in range(fan)]
    left = jnp.concatenate([a_ref[pa] for pa, _ in chosen], axis=1)
    right = jnp.concatenate([p_ref[pp] for _, pp in chosen], axis=0)
    return jnp.dot(left, right, preferred_element_type=jnp.float32)


def own_bit(bit):
    return (lax.axis_index("layer") >> bit) & 1


def insert(rest, at, bit):
    low = rest & ((1 << at) - 1)
    return ((rest >> at) << (at + 1)) | (bit << at) | low


def loop(turns, body, start):
    return body(0, start) if turns == 1 else lax.fori_loop(0, turns, body, start)


def packing(slots, lanes):
    return max(1, lanes // slots)


def pack_kernel(ia_ref, ip_ref, own_ref, far_ref):
    fan, slots = ia_ref.shape[1:]
    per = packing(slots, own_ref.shape[1])
    col = lax.axis_index("col")
    for out_ref, column in ((own_ref, col), (far_ref, 1 - col)):
        for which, ref in enumerate((ia_ref, ip_ref)):
            lists = ref[column]
            for f in range(fan):
                row, at = divmod(which * fan + f, per)
                out_ref[pl.ds(row, 1), pl.ds(at * slots, slots)] = lists[f : f + 1]


def finder(lists_ref, fan, slots):
    per = packing(slots, lists_ref.shape[1])

    def place(which, f, t):
        row, at = divmod(which * fan + f, per)
        return lists_ref[row, at * slots + t]

    return lambda t: lambda f: (place(0, f, t), place(1, f, t))


def send_kernel(fan, slots, count, chunks, bits, joins):
    def kernel(lists_ref, a_ref, *refs):
        find = finder(lists_ref, fan, slots)
        n_out = len(chunks) + joins
        p_refs, out_refs = refs[:-n_out], refs[-n_out:]
        if joins:
            out_refs, p_ref = out_refs[:-1], out_refs[-1]
            held = p_ref.shape[0] // 2
            row = lax.axis_index("row")
            p_ref[pl.ds(row * held, held)] = p_refs[0][...]
            at = (1 - row) * held
            for ref in p_refs[1:]:
                p_ref[pl.ds(at, ref.shape[0])] = ref[...]
                at += ref.shape[0]
        else:
            (p_ref,) = p_refs
        width = p_ref.shape[-1]
        for (first, size), bit, out_ref in zip(chunks, bits, out_refs):
            side = 1 - own_bit(bit)
            total = out_ref.shape[0] // width

            def body(step, head):
                for k in range(GROUP):
                    slot = step * GROUP + k
                    layer = insert(slot // size, bit, side)
                    tile = product(a_ref, p_ref, find(layer * count + first + slot % size), fan)
                    head = put_tile(out_ref, slot, tile, head)
                return head

            put_head(out_ref, loop(total // GROUP, body, new_head(total, width)))

    return kernel


def split_kernel(in_ref, *out_refs):
    at = 0
    for ref in out_refs:
        ref[...] = in_ref[pl.ds(at, ref.shape[0])]
        at += ref.shape[0]


def keep_kernel(fan, slots, count, chunks, bits):
    def kernel(lists_ref, a_ref, p_ref, *out_refs):
        find = finder(lists_ref, fan, slots)
        for (first, size), bit, out_ref in zip(chunks, bits, out_refs):
            side = own_bit(bit)

            def body(step, _):
                for k in range(GROUP):
                    slot = step * GROUP + k
                    layer = insert(slot // size, bit, side)
                    out_ref[slot] = product(a_ref, p_ref, find(layer * count + first + slot % size), fan)
                return 0

            loop(out_ref.shape[0] // GROUP, body, 0)

    return kernel


def cross_kernel(sizes, bit, whose):
    def kernel(*refs):
        n = len(sizes)
        kept_refs, in_refs, out_refs = refs[:n], refs[n : 2 * n], refs[2 * n :]
        width = out_refs[0].shape[-1]
        mine = own_bit(bit)
        heads = [get_head(ref, ref.shape[0] // width) for ref in in_refs]

        def put(out_ref, side, chosen):
            count = out_ref.shape[0] // width
            head, slot = new_head(count, width), 0
            for c in chosen:
                for i in range(sizes[c]):
                    at = side * sizes[c] + i
                    tile = kept_refs[c][at] + get_tile(in_refs[c], at, heads[c])
                    head = put_tile(out_ref, slot, tile, head)
                    slot += 1
            put_head(out_ref, head)

        put(out_refs[0], 1 - mine, [whose])
        if len(out_refs) > 1:
            put(out_refs[1], mine, range(n))

    return kernel


def add_kernel(sizes, rest, bit):
    at = rest.index(bit)
    full = sum(sizes)
    halves = 1 << (len(rest) - 1)

    def kernel(*refs):
        n = len(sizes)
        kept_refs, in_refs, (sent_ref, stay_ref) = refs[:n], refs[n : 2 * n], refs[2 * n : 2 * n + 2]
        width = sent_ref.shape[-1]
        mine = own_bit(bit)
        heads = [get_head(ref, ref.shape[0] // width) for ref in in_refs]

        def sums(place):
            for size, kept_ref, in_ref, head in zip(sizes, kept_refs, in_refs, heads):
                for i in range(size):
                    slot = place * size + i
                    yield kept_ref[slot] + get_tile(in_ref, slot, head)

        def send(ref, side):
            def body(half, head):
                for i, tile in enumerate(sums(insert(half, at, side))):
                    head = put_tile(ref, half * full + i, tile, head)
                return head

            put_head(ref, lax.fori_loop(0, halves, body, new_head(halves * full, width), unroll=halves <= 4))

        send(sent_ref, 1 - mine)

        def body(half, _):
            for i, tile in enumerate(sums(insert(half, at, mine))):
                stay_ref[half * full + i] = tile
            return 0

        lax.fori_loop(0, halves, body, 0, unroll=halves <= 4)

    return kernel


def sum_kernel(kept_ref, in_ref, out_ref):
    count = out_ref.shape[0]
    head = get_head(in_ref, count)
    for i in range(count):
        out_ref[i] = kept_ref[i] + get_tile(in_ref, i, head)


def early_kernel(first):
    def kernel(own_ref, far_ref, out_ref):
        size = out_ref.shape[0]
        head = get_head(far_ref, size)
        for i in range(size):
            out_ref[i] = own_ref[first + i] + get_tile(far_ref, i, head)

    return kernel


def last_kernel(near_ref, *refs):
    early_refs, out_ref = refs[:-1], refs[-1]
    count = out_ref.shape[0]
    head, at = get_head(near_ref, count), 0
    for ref in early_refs:
        for i in range(ref.shape[0]):
            out_ref[at] = (ref[i] + get_tile(near_ref, at, head)).astype(out_ref.dtype)
            at += 1


def call(kernel, out_shape, smem, vmem, after=(), scratch=(), flops=0):
    outs = out_shape if isinstance(out_shape, (list, tuple)) else [out_shape]
    moved = sum(x.size * x.dtype.itemsize for x in (*smem, *vmem, *outs))
    n_real = len(smem) + len(vmem)

    def wrapped(*refs):
        kernel(*refs[:n_real], *refs[n_real + len(after) :])

    return pl.pallas_call(
        wrapped,
        out_shape=out_shape,
        in_specs=[pl.BlockSpec(memory_space=SMEM)] * len(smem)
        + [pl.BlockSpec(memory_space=VMEM)] * len(vmem)
        + [pl.BlockSpec(memory_space=pl.ANY)] * len(after),
        out_specs=jax.tree.map(lambda _: pl.BlockSpec(memory_space=VMEM), out_shape),
        scratch_shapes=list(scratch),
        compiler_params=pltpu.CompilerParams(vmem_limit_bytes=moved + 4 * 2**20),
        cost_estimate=pl.CostEstimate(flops=int(5 * flops), bytes_accessed=moved if flops else 1, transcendentals=0),
    )(*smem, *vmem, *after)


def hold(x, after):
    def kernel(*refs):
        pass

    return pl.pallas_call(
        kernel,
        out_shape=jax.ShapeDtypeStruct(x.shape, x.dtype),
        in_specs=[pl.BlockSpec(memory_space=pl.ANY)] * (1 + len(after)),
        out_specs=pl.BlockSpec(memory_space=pl.ANY),
        input_output_aliases={0: 0},
        compiler_params=pltpu.CompilerParams(vmem_limit_bytes=2**20),
    )(x, *after)


def on_device(a_tiles, p_tiles, pair_a, pair_p):
    a, p = a_tiles[0, 0, 0], p_tiles[0, 0, 0]
    ia, ip = jnp.swapaxes(pair_a[0, 0, 0], 1, 2), jnp.swapaxes(pair_p[0, 0, 0], 1, 2)
    fan, slots = ia.shape[1:]
    held, width = p.shape[0], p.shape[-1]
    layers = lax.axis_size("layer")
    bits = layers.bit_length() - 1
    count = slots // layers
    swap = [(0, 1), (1, 0)]

    half = count // 2
    chunks = [(0, half), (half, count - half)]
    flops = layers * half * fan * width**3

    def floats(size):
        return jax.ShapeDtypeStruct((size, width, width), jnp.float32)

    def exchange(x, bit):
        return lax.ppermute(x, "layer", [(i, i ^ (1 << bit)) for i in range(layers)])

    def cross(x, bit):
        flip = 0 if bit is None else 1 << bit
        perm = [(c * layers + i, (1 - c) * layers + (i ^ flip)) for c in range(2) for i in range(layers)]
        return lax.ppermute(x, ("col", "layer"), perm)

    def send(lists, vmem, which, bits, joins, after, cost):
        picked = [chunks[n] for n in which]
        shapes = [message(layers // 2 * size, width) for _, size in picked]
        if joins:
            shapes.append(jax.ShapeDtypeStruct((2 * held, width, width), p.dtype))
        kernel = send_kernel(fan, slots, count, picked, bits, joins)
        made = call(kernel, shapes, (lists,), vmem, after, (), cost * len(which) * flops)
        return made, [exchange(x, b) for x, b in zip(made, bits)]

    def keep(lists, vmem, bits, after, cost):
        shapes = [floats(layers // 2 * size) for _, size in chunks]
        kernel = keep_kernel(fan, slots, count, chunks, bits)
        return call(kernel, shapes, (lists,), vmem, after, (), cost * 2 * flops)

    def add(parts, sizes, rest, bit, after):
        n = sum(sizes) << (len(rest) - 1)
        shapes = [message(n, width), floats(n)]
        kept, came = zip(*parts)
        return call(add_kernel(sizes, rest, bit), shapes, (), (*kept, *came), after)

    own_bits, other_bits = (0, 1), (1, 0)
    sizes = [size for _, size in chunks]
    every = list(range(bits))

    def less(rest, bit):
        return [b for b in rest if b != bit]

    def second(kept, came, size, bit, after):
        sent, kept = add([(kept, came)], [size], less(every, bit), 1 - bit, after)
        return sent, (kept, exchange(sent, 1 - bit))

    p_x = lax.ppermute(p, "col", swap)
    p_r = lax.ppermute(p, "row", swap)
    packed = jax.ShapeDtypeStruct((-(-2 * fan // packing(slots, LANES)), max(slots, LANES)), jnp.int32)
    lists, lists_far = call(pack_kernel, [packed] * 2, (), (ia, ip))

    token = jax.ShapeDtypeStruct((8, width), jnp.float32)
    gate = call(lambda *refs: None, token, (), (), (), (), 10**9)
    gate = call(lambda *refs: None, token, (), (a, p), (gate,))

    (*made, joined), own_came = send(lists, (a, p, p_r), (0, 1), own_bits, True, (gate,), 1)
    own_kept = keep(lists, (a, joined), own_bits, made[:1], 1)
    lists_x = lax.ppermute(hold(lists_far, own_kept[:1]), "col", swap)
    parts, after = [], ()
    for n in range(2):
        sent, part = second(own_kept[n], own_came[n], sizes[n], own_bits[n], after)
        parts.append(part)
        after = (sent,)
    pieces = [jax.ShapeDtypeStruct((held // 2, width, width), p.dtype)] * 2
    pieces = call(split_kernel, pieces, (), (p_x,), (*after, lists_x))
    p_xr = [lax.ppermute(x, "row", swap) for x in pieces]

    (made, joined), came_0 = send(lists_x, (a, p_x, *p_xr), (0,), other_bits[:1], True, (), 0)
    (made,), came_1 = send(lists_x, (a, joined), (1,), other_bits[1:], False, (made,), 0)
    other_came = came_0 + came_1
    other_kept = keep(lists_x, (a, joined), other_bits, (made,), 1)

    rest, part_sizes, after = every[2:], sizes, other_kept[:1]
    for b in every[2:]:
        sent, kept = add(parts, part_sizes, rest, b, after)
        after = (sent,)
        parts, part_sizes = [(kept, exchange(sent, b))], [count]
        rest = less(rest, b)
    (own,) = parts
    streams = []
    for n in range(2):
        sent, part = second(other_kept[n], other_came[n], sizes[n], other_bits[n], after)
        streams.append(part)
        after = (sent,)
    rest = every[2:]
    for b in every[2:-1]:
        for n in range(2):
            sent, kept = add([streams[n]], [sizes[n]], rest, b, after)
            after = (sent,)
            streams[n] = (kept, exchange(sent, b))
        rest = less(rest, b)

    own = call(sum_kernel, floats(count), (), own, after)
    moved, top, after = [], rest[0], (own,)
    for n in range(2):
        shapes = [message(sizes[n], width)] + [message(count, width)] * n
        used, used_sizes = ([streams[0]], sizes[:1]) if n == 0 else (streams, sizes)
        kept, came = zip(*used)
        sent = call(cross_kernel(used_sizes, top, n), shapes, (), (*kept, *came), after)
        after = (sent[0],)
        moved.append(cross(sent[0], top))
    near = cross(sent[1], None)
    early = []
    for n, (first, size) in enumerate(chunks):
        early.append(call(early_kernel(first), floats(size), (), (own, moved[n]), early[-1:], (), 10**9))
    result = jax.ShapeDtypeStruct((count, width, width), jnp.bfloat16)
    return call(last_kernel, result, (), (near, *early))[None, None]


def solution(mesh):
    spec = P("row", "col", "layer", None, None, None)
    return jax.shard_map(
        on_device,
        mesh=mesh,
        in_specs=(spec,) * 4,
        out_specs=P("row", "col", "layer", None, None),
        check_vma=False,
    )
```

```python
import jax
import jax.numpy as jnp
from jax import lax
from jax.experimental import pallas as pl
from jax.experimental.pallas import tpu as pltpu
from jax.sharding import PartitionSpec as P

PEAK = 32766.0
ROWS = 16
LANES = 128
GROUP = 8
SMEM = pltpu.MemorySpace.SMEM
VMEM = pltpu.MemorySpace.VMEM


def head_rows(count):
    return -(-count // ROWS) * ROWS


def message(count, width):
    return jax.ShapeDtypeStruct((count * width + head_rows(count), width), jnp.int16)


def encode(tile):
    top = jnp.max(jnp.abs(tile), axis=0, keepdims=True)
    power = jnp.floor(jnp.log2(jnp.maximum(top, 2.0**-100)) + 0.001) + 1.0
    scaled = jnp.round(tile * (jnp.exp2(-power) * PEAK))
    return scaled.astype(jnp.int32).astype(jnp.int16), power.astype(jnp.int32)


def new_head(count, width):
    return jnp.zeros((head_rows(count), width), jnp.int32)


def rows_at(slot, width):
    start = slot * width
    return pl.ds(start if isinstance(start, int) else pl.multiple_of(start, width), width)


def put_tile(ref, slot, tile, head):
    coded, power = encode(tile)
    ref[rows_at(slot, tile.shape[0]), :] = coded
    rows = lax.broadcasted_iota(jnp.int32, head.shape, 0)
    return jnp.where(rows == slot, power, head)


def put_head(ref, head):
    ref[pl.ds(ref.shape[0] - head.shape[0], head.shape[0]), :] = head.astype(jnp.int16)


def get_head(ref, count):
    rows = head_rows(count)
    return ref[pl.ds(ref.shape[0] - rows, rows), :].astype(jnp.int32)


def get_tile(ref, slot, head):
    rows = lax.broadcasted_iota(jnp.int32, head.shape, 0)
    power = jnp.sum(jnp.where(rows == slot, head, 0), axis=0, keepdims=True)
    coded = ref[rows_at(slot, ref.shape[-1]), :]
    return coded.astype(jnp.int32).astype(jnp.float32) * (jnp.exp2(power.astype(jnp.float32)) * (1.0 / PEAK))


def product(a_ref, p_ref, look, fan):
    chosen = [look(f) for f in range(fan)]
    left = jnp.concatenate([a_ref[pa] for pa, _ in chosen], axis=1)
    right = jnp.concatenate([p_ref[pp] for _, pp in chosen], axis=0)
    return jnp.dot(left, right, preferred_element_type=jnp.float32)


def own_bit(bit):
    return (lax.axis_index("layer") >> bit) & 1


def insert(rest, at, bit):
    low = rest & ((1 << at) - 1)
    return ((rest >> at) << (at + 1)) | (bit << at) | low


def loop(turns, body, start):
    return body(0, start) if turns == 1 else lax.fori_loop(0, turns, body, start)


def packing(slots, lanes):
    return max(1, lanes // slots)


def pack_kernel(ia_ref, ip_ref, own_ref, far_ref):
    fan, slots = ia_ref.shape[1:]
    per = packing(slots, own_ref.shape[1])
    col = lax.axis_index("col")
    for out_ref, column in ((own_ref, col), (far_ref, 1 - col)):
        for which, ref in enumerate((ia_ref, ip_ref)):
            lists = ref[column]
            for f in range(fan):
                row, at = divmod(which * fan + f, per)
                out_ref[pl.ds(row, 1), pl.ds(at * slots, slots)] = lists[f : f + 1]


def finder(lists_ref, fan, slots):
    per = packing(slots, lists_ref.shape[1])

    def place(which, f, t):
        row, at = divmod(which * fan + f, per)
        return lists_ref[row, at * slots + t]

    return lambda t: lambda f: (place(0, f, t), place(1, f, t))


def send_kernel(fan, slots, count, chunks, bits, joins):
    def kernel(lists_ref, a_ref, *refs):
        find = finder(lists_ref, fan, slots)
        n_out = len(chunks) + joins
        p_refs, out_refs = refs[:-n_out], refs[-n_out:]
        if joins:
            out_refs, p_ref = out_refs[:-1], out_refs[-1]
            held = p_ref.shape[0] // 2
            row = lax.axis_index("row")
            p_ref[pl.ds(row * held, held)] = p_refs[0][...]
            at = (1 - row) * held
            for ref in p_refs[1:]:
                p_ref[pl.ds(at, ref.shape[0])] = ref[...]
                at += ref.shape[0]
        else:
            (p_ref,) = p_refs
        width = p_ref.shape[-1]
        for (first, size), bit, out_ref in zip(chunks, bits, out_refs):
            side = 1 - own_bit(bit)
            total = out_ref.shape[0] // width

            def body(step, head):
                for k in range(GROUP):
                    slot = step * GROUP + k
                    layer = insert(slot // size, bit, side)
                    tile = product(a_ref, p_ref, find(layer * count + first + slot % size), fan)
                    head = put_tile(out_ref, slot, tile, head)
                return head

            put_head(out_ref, loop(total // GROUP, body, new_head(total, width)))

    return kernel


def split_kernel(in_ref, *out_refs):
    at = 0
    for ref in out_refs:
        ref[...] = in_ref[pl.ds(at, ref.shape[0])]
        at += ref.shape[0]


def keep_kernel(fan, slots, count, chunks, bits):
    def kernel(lists_ref, a_ref, p_ref, *out_refs):
        find = finder(lists_ref, fan, slots)
        for (first, size), bit, out_ref in zip(chunks, bits, out_refs):
            side = own_bit(bit)

            def body(step, _):
                for k in range(GROUP):
                    slot = step * GROUP + k
                    layer = insert(slot // size, bit, side)
                    out_ref[slot] = product(a_ref, p_ref, find(layer * count + first + slot % size), fan)
                return 0

            loop(out_ref.shape[0] // GROUP, body, 0)

    return kernel


def cross_kernel(sizes, bit, whose):
    def kernel(*refs):
        n = len(sizes)
        kept_refs, in_refs, out_refs = refs[:n], refs[n : 2 * n], refs[2 * n :]
        width = out_refs[0].shape[-1]
        mine = own_bit(bit)
        heads = [get_head(ref, ref.shape[0] // width) for ref in in_refs]

        def put(out_ref, side, chosen):
            count = out_ref.shape[0] // width
            head, slot = new_head(count, width), 0
            for c in chosen:
                for i in range(sizes[c]):
                    at = side * sizes[c] + i
                    tile = kept_refs[c][at] + get_tile(in_refs[c], at, heads[c])
                    head = put_tile(out_ref, slot, tile, head)
                    slot += 1
            put_head(out_ref, head)

        put(out_refs[0], 1 - mine, [whose])
        if len(out_refs) > 1:
            put(out_refs[1], mine, range(n))

    return kernel


def add_kernel(sizes, rest, bit):
    at = rest.index(bit)
    full = sum(sizes)
    halves = 1 << (len(rest) - 1)

    def kernel(*refs):
        n = len(sizes)
        kept_refs, in_refs, (sent_ref, stay_ref) = refs[:n], refs[n : 2 * n], refs[2 * n : 2 * n + 2]
        width = sent_ref.shape[-1]
        mine = own_bit(bit)
        heads = [get_head(ref, ref.shape[0] // width) for ref in in_refs]

        def sums(place):
            for size, kept_ref, in_ref, head in zip(sizes, kept_refs, in_refs, heads):
                for i in range(size):
                    slot = place * size + i
                    yield kept_ref[slot] + get_tile(in_ref, slot, head)

        def send(ref, side):
            def body(half, head):
                for i, tile in enumerate(sums(insert(half, at, side))):
                    head = put_tile(ref, half * full + i, tile, head)
                return head

            put_head(ref, lax.fori_loop(0, halves, body, new_head(halves * full, width), unroll=halves <= 4))

        send(sent_ref, 1 - mine)

        def body(half, _):
            for i, tile in enumerate(sums(insert(half, at, mine))):
                stay_ref[half * full + i] = tile
            return 0

        lax.fori_loop(0, halves, body, 0, unroll=halves <= 4)

    return kernel


def sum_kernel(kept_ref, in_ref, out_ref):
    count = out_ref.shape[0]
    head = get_head(in_ref, count)
    for i in range(count):
        out_ref[i] = kept_ref[i] + get_tile(in_ref, i, head)


def early_kernel(first):
    def kernel(own_ref, far_ref, out_ref):
        size = out_ref.shape[0]
        head = get_head(far_ref, size)
        for i in range(size):
            out_ref[i] = own_ref[first + i] + get_tile(far_ref, i, head)

    return kernel


def last_kernel(near_ref, *refs):
    early_refs, out_ref = refs[:-1], refs[-1]
    count = out_ref.shape[0]
    head, at = get_head(near_ref, count), 0
    for ref in early_refs:
        for i in range(ref.shape[0]):
            out_ref[at] = (ref[i] + get_tile(near_ref, at, head)).astype(out_ref.dtype)
            at += 1


def call(kernel, out_shape, smem, vmem, after=(), scratch=(), flops=0):
    outs = out_shape if isinstance(out_shape, (list, tuple)) else [out_shape]
    moved = sum(x.size * x.dtype.itemsize for x in (*smem, *vmem, *outs))
    n_real = len(smem) + len(vmem)

    def wrapped(*refs):
        kernel(*refs[:n_real], *refs[n_real + len(after) :])

    return pl.pallas_call(
        wrapped,
        out_shape=out_shape,
        in_specs=[pl.BlockSpec(memory_space=SMEM)] * len(smem)
        + [pl.BlockSpec(memory_space=VMEM)] * len(vmem)
        + [pl.BlockSpec(memory_space=pl.ANY)] * len(after),
        out_specs=jax.tree.map(lambda _: pl.BlockSpec(memory_space=VMEM), out_shape),
        scratch_shapes=list(scratch),
        compiler_params=pltpu.CompilerParams(vmem_limit_bytes=moved + 4 * 2**20),
        cost_estimate=pl.CostEstimate(flops=int(5 * flops), bytes_accessed=moved if flops else 1, transcendentals=0),
    )(*smem, *vmem, *after)


def hold(x, after):
    def kernel(*refs):
        pass

    return pl.pallas_call(
        kernel,
        out_shape=jax.ShapeDtypeStruct(x.shape, x.dtype),
        in_specs=[pl.BlockSpec(memory_space=pl.ANY)] * (1 + len(after)),
        out_specs=pl.BlockSpec(memory_space=pl.ANY),
        input_output_aliases={0: 0},
        compiler_params=pltpu.CompilerParams(vmem_limit_bytes=2**20),
    )(x, *after)


def on_device(a_tiles, p_tiles, pair_a, pair_p):
    a, p = a_tiles[0, 0, 0], p_tiles[0, 0, 0]
    ia, ip = jnp.swapaxes(pair_a[0, 0, 0], 1, 2), jnp.swapaxes(pair_p[0, 0, 0], 1, 2)
    fan, slots = ia.shape[1:]
    held, width = p.shape[0], p.shape[-1]
    layers = lax.axis_size("layer")
    bits = layers.bit_length() - 1
    count = slots // layers
    swap = [(0, 1), (1, 0)]

    half = count // 2
    chunks = [(0, half), (half, count - half)]
    flops = layers * half * fan * width**3

    def floats(size):
        return jax.ShapeDtypeStruct((size, width, width), jnp.float32)

    def exchange(x, bit):
        return lax.ppermute(x, "layer", [(i, i ^ (1 << bit)) for i in range(layers)])

    def cross(x, bit):
        flip = 0 if bit is None else 1 << bit
        perm = [(c * layers + i, (1 - c) * layers + (i ^ flip)) for c in range(2) for i in range(layers)]
        return lax.ppermute(x, ("col", "layer"), perm)

    def send(lists, vmem, which, bits, joins, after, cost):
        picked = [chunks[n] for n in which]
        shapes = [message(layers // 2 * size, width) for _, size in picked]
        if joins:
            shapes.append(jax.ShapeDtypeStruct((2 * held, width, width), p.dtype))
        kernel = send_kernel(fan, slots, count, picked, bits, joins)
        made = call(kernel, shapes, (lists,), vmem, after, (), cost * len(which) * flops)
        return made, [exchange(x, b) for x, b in zip(made, bits)]

    def keep(lists, vmem, bits, after, cost):
        shapes = [floats(layers // 2 * size) for _, size in chunks]
        kernel = keep_kernel(fan, slots, count, chunks, bits)
        return call(kernel, shapes, (lists,), vmem, after, (), cost * 2 * flops)

    def add(parts, sizes, rest, bit, after):
        n = sum(sizes) << (len(rest) - 1)
        shapes = [message(n, width), floats(n)]
        kept, came = zip(*parts)
        return call(add_kernel(sizes, rest, bit), shapes, (), (*kept, *came), after)

    own_bits, other_bits = (0, 1), (0, 1)
    sizes = [size for _, size in chunks]
    every = list(range(bits))

    def less(rest, bit):
        return [b for b in rest if b != bit]

    def second(kept, came, size, bit, after):
        sent, kept = add([(kept, came)], [size], less(every, bit), 1 - bit, after)
        return sent, (kept, exchange(sent, 1 - bit))

    p_x = lax.ppermute(p, "col", swap)
    p_r = lax.ppermute(p, "row", swap)
    packed = jax.ShapeDtypeStruct((-(-2 * fan // packing(slots, LANES)), max(slots, LANES)), jnp.int32)
    lists, lists_far = call(pack_kernel, [packed] * 2, (), (ia, ip))

    token = jax.ShapeDtypeStruct((8, width), jnp.float32)
    gate = call(lambda *refs: None, token, (), (), (), (), 10**9)
    gate = call(lambda *refs: None, token, (), (a, p), (gate,))

    (*made, joined), own_came = send(lists, (a, p, p_r), (0, 1), own_bits, True, (gate,), 1)
    own_kept = keep(lists, (a, joined), own_bits, made[:1], 1)
    lists_x = lax.ppermute(hold(lists_far, own_kept[:1]), "col", swap)
    parts, after = [], ()
    for n in range(2):
        sent, part = second(own_kept[n], own_came[n], sizes[n], own_bits[n], after)
        parts.append(part)
        after = (sent,)
    pieces = [jax.ShapeDtypeStruct((held // 2, width, width), p.dtype)] * 2
    pieces = call(split_kernel, pieces, (), (p_x,), (*after, lists_x))
    p_xr = [lax.ppermute(x, "row", swap) for x in pieces]

    (made, joined), came_0 = send(lists_x, (a, p_x, *p_xr), (0,), other_bits[:1], True, (), 0)
    (made,), came_1 = send(lists_x, (a, joined), (1,), other_bits[1:], False, (made,), 0)
    other_came = came_0 + came_1
    other_kept = keep(lists_x, (a, joined), other_bits, (made,), 1)

    rest, part_sizes, after = every[2:], sizes, other_kept[:1]
    for b in every[2:]:
        sent, kept = add(parts, part_sizes, rest, b, after)
        after = (sent,)
        parts, part_sizes = [(kept, exchange(sent, b))], [count]
        rest = less(rest, b)
    (own,) = parts
    streams = []
    for n in range(2):
        sent, part = second(other_kept[n], other_came[n], sizes[n], other_bits[n], after)
        streams.append(part)
        after = (sent,)
    rest = every[2:]
    for b in every[2:-1]:
        for n in range(2):
            sent, kept = add([streams[n]], [sizes[n]], rest, b, after)
            after = (sent,)
            streams[n] = (kept, exchange(sent, b))
        rest = less(rest, b)

    own = call(sum_kernel, floats(count), (), own, after)
    moved, top, after = [], rest[0], (own,)
    for n in range(2):
        shapes = [message(sizes[n], width)] + [message(count, width)] * n
        used, used_sizes = ([streams[0]], sizes[:1]) if n == 0 else (streams, sizes)
        kept, came = zip(*used)
        sent = call(cross_kernel(used_sizes, top, n), shapes, (), (*kept, *came), after)
        after = (sent[0],)
        moved.append(cross(sent[0], top))
    near = cross(sent[1], None)
    early = []
    for n, (first, size) in enumerate(chunks):
        early.append(call(early_kernel(first), floats(size), (), (own, moved[n]), early[-1:], (), 10**9))
    result = jax.ShapeDtypeStruct((count, width, width), jnp.bfloat16)
    return call(last_kernel, result, (), (near, *early))[None, None]


def solution(mesh):
    spec = P("row", "col", "layer", None, None, None)
    return jax.shard_map(
        on_device,
        mesh=mesh,
        in_specs=(spec,) * 4,
        out_specs=P("row", "col", "layer", None, None),
        check_vma=False,
    )
```

```python
import jax
import jax.numpy as jnp
from jax import lax
from jax.experimental import pallas as pl
from jax.experimental.pallas import tpu as pltpu
from jax.sharding import PartitionSpec as P

PEAK = 32766.0
ROWS = 16
LANES = 128
GROUP = 8
SMEM = pltpu.MemorySpace.SMEM
VMEM = pltpu.MemorySpace.VMEM


def head_rows(count):
    return -(-count // ROWS) * ROWS


def message(count, width):
    return jax.ShapeDtypeStruct((count * width + head_rows(count), width), jnp.int16)


def encode(tile):
    top = jnp.max(jnp.abs(tile), axis=0, keepdims=True)
    power = jnp.floor(jnp.log2(jnp.maximum(top, 2.0**-100)) + 0.001) + 1.0
    scaled = jnp.round(tile * (jnp.exp2(-power) * PEAK))
    return scaled.astype(jnp.int32).astype(jnp.int16), power.astype(jnp.int32)


def new_head(count, width):
    return jnp.zeros((head_rows(count), width), jnp.int32)


def rows_at(slot, width):
    start = slot * width
    return pl.ds(start if isinstance(start, int) else pl.multiple_of(start, width), width)


def put_tile(ref, slot, tile, head):
    coded, power = encode(tile)
    ref[rows_at(slot, tile.shape[0]), :] = coded
    rows = lax.broadcasted_iota(jnp.int32, head.shape, 0)
    return jnp.where(rows == slot, power, head)


def put_head(ref, head):
    ref[pl.ds(ref.shape[0] - head.shape[0], head.shape[0]), :] = head.astype(jnp.int16)


def get_head(ref, count):
    rows = head_rows(count)
    return ref[pl.ds(ref.shape[0] - rows, rows), :].astype(jnp.int32)


def get_tile(ref, slot, head):
    rows = lax.broadcasted_iota(jnp.int32, head.shape, 0)
    power = jnp.sum(jnp.where(rows == slot, head, 0), axis=0, keepdims=True)
    coded = ref[rows_at(slot, ref.shape[-1]), :]
    return coded.astype(jnp.int32).astype(jnp.float32) * (jnp.exp2(power.astype(jnp.float32)) * (1.0 / PEAK))


def product(a_ref, p_ref, look, fan):
    chosen = [look(f) for f in range(fan)]
    left = jnp.concatenate([a_ref[pa] for pa, _ in chosen], axis=1)
    right = jnp.concatenate([p_ref[pp] for _, pp in chosen], axis=0)
    return jnp.dot(left, right, preferred_element_type=jnp.float32)


def own_bit(bit):
    return (lax.axis_index("layer") >> bit) & 1


def insert(rest, at, bit):
    low = rest & ((1 << at) - 1)
    return ((rest >> at) << (at + 1)) | (bit << at) | low


def loop(turns, body, start):
    return body(0, start) if turns == 1 else lax.fori_loop(0, turns, body, start)


def packing(slots, lanes):
    return max(1, lanes // slots)


def pack_kernel(ia_ref, ip_ref, own_ref, far_ref):
    fan, slots = ia_ref.shape[1:]
    per = packing(slots, own_ref.shape[1])
    col = lax.axis_index("col")
    for out_ref, column in ((own_ref, col), (far_ref, 1 - col)):
        for which, ref in enumerate((ia_ref, ip_ref)):
            lists = ref[column]
            for f in range(fan):
                row, at = divmod(which * fan + f, per)
                out_ref[pl.ds(row, 1), pl.ds(at * slots, slots)] = lists[f : f + 1]


def finder(lists_ref, fan, slots):
    per = packing(slots, lists_ref.shape[1])

    def place(which, f, t):
        row, at = divmod(which * fan + f, per)
        return lists_ref[row, at * slots + t]

    return lambda t: lambda f: (place(0, f, t), place(1, f, t))


def send_kernel(fan, slots, count, chunks, bits, joins):
    def kernel(lists_ref, a_ref, *refs):
        find = finder(lists_ref, fan, slots)
        n_out = len(chunks) + joins
        p_refs, out_refs = refs[:-n_out], refs[-n_out:]
        if joins:
            out_refs, p_ref = out_refs[:-1], out_refs[-1]
            held = p_ref.shape[0] // 2
            row = lax.axis_index("row")
            p_ref[pl.ds(row * held, held)] = p_refs[0][...]
            at = (1 - row) * held
            for ref in p_refs[1:]:
                p_ref[pl.ds(at, ref.shape[0])] = ref[...]
                at += ref.shape[0]
        else:
            (p_ref,) = p_refs
        width = p_ref.shape[-1]
        for (first, size), bit, out_ref in zip(chunks, bits, out_refs):
            side = 1 - own_bit(bit)
            total = out_ref.shape[0] // width

            def body(step, head):
                for k in range(GROUP):
                    slot = step * GROUP + k
                    layer = insert(slot // size, bit, side)
                    tile = product(a_ref, p_ref, find(layer * count + first + slot % size), fan)
                    head = put_tile(out_ref, slot, tile, head)
                return head

            put_head(out_ref, loop(total // GROUP, body, new_head(total, width)))

    return kernel


def split_kernel(in_ref, *out_refs):
    at = 0
    for ref in out_refs:
        ref[...] = in_ref[pl.ds(at, ref.shape[0])]
        at += ref.shape[0]


def keep_kernel(fan, slots, count, chunks, bits):
    def kernel(lists_ref, a_ref, p_ref, *out_refs):
        find = finder(lists_ref, fan, slots)
        for (first, size), bit, out_ref in zip(chunks, bits, out_refs):
            side = own_bit(bit)

            def body(step, _):
                for k in range(GROUP):
                    slot = step * GROUP + k
                    layer = insert(slot // size, bit, side)
                    out_ref[slot] = product(a_ref, p_ref, find(layer * count + first + slot % size), fan)
                return 0

            loop(out_ref.shape[0] // GROUP, body, 0)

    return kernel


def cross_kernel(size, bit):
    def kernel(kept_ref, in_ref, far_ref, near_ref):
        width = far_ref.shape[-1]
        mine = own_bit(bit)
        head_in = get_head(in_ref, in_ref.shape[0] // width)
        for out_ref, side in ((far_ref, 1 - mine), (near_ref, mine)):
            head = new_head(size, width)
            for i in range(size):
                at = side * size + i
                head = put_tile(out_ref, i, kept_ref[at] + get_tile(in_ref, at, head_in), head)
            put_head(out_ref, head)

    return kernel


def add_kernel(sizes, rest, bit):
    at = rest.index(bit)
    full = sum(sizes)
    halves = 1 << (len(rest) - 1)

    def kernel(*refs):
        n = len(sizes)
        kept_refs, in_refs, (sent_ref, stay_ref) = refs[:n], refs[n : 2 * n], refs[2 * n : 2 * n + 2]
        width = sent_ref.shape[-1]
        mine = own_bit(bit)
        heads = [get_head(ref, ref.shape[0] // width) for ref in in_refs]

        def sums(place):
            for size, kept_ref, in_ref, head in zip(sizes, kept_refs, in_refs, heads):
                for i in range(size):
                    slot = place * size + i
                    yield kept_ref[slot] + get_tile(in_ref, slot, head)

        def send(ref, side):
            def body(half, head):
                for i, tile in enumerate(sums(insert(half, at, side))):
                    head = put_tile(ref, half * full + i, tile, head)
                return head

            put_head(ref, lax.fori_loop(0, halves, body, new_head(halves * full, width), unroll=halves <= 4))

        send(sent_ref, 1 - mine)

        def body(half, _):
            for i, tile in enumerate(sums(insert(half, at, mine))):
                stay_ref[half * full + i] = tile
            return 0

        lax.fori_loop(0, halves, body, 0, unroll=halves <= 4)

    return kernel


def sum_kernel(kept_ref, in_ref, out_ref):
    count = out_ref.shape[0]
    head = get_head(in_ref, count)
    for i in range(count):
        out_ref[i] = kept_ref[i] + get_tile(in_ref, i, head)


def chunk_sums(own_ref, first, far_ref, near_ref, size):
    heads = [get_head(ref, size) for ref in (far_ref, near_ref)]
    for i in range(size):
        yield own_ref[first + i] + get_tile(far_ref, i, heads[0]) + get_tile(near_ref, i, heads[1])


def early_kernel(own_ref, far_ref, near_ref, out_ref):
    size = out_ref.shape[0]
    for i, total in enumerate(chunk_sums(own_ref, 0, far_ref, near_ref, size)):
        out_ref[i] = total


def last_kernel(early_ref, own_ref, far_ref, near_ref, out_ref):
    first = early_ref.shape[0]
    out_ref[pl.ds(0, first)] = early_ref[...].astype(out_ref.dtype)
    for i, total in enumerate(chunk_sums(own_ref, first, far_ref, near_ref, out_ref.shape[0] - first)):
        out_ref[first + i] = total.astype(out_ref.dtype)


def call(kernel, out_shape, smem, vmem, after=(), scratch=(), flops=0):
    outs = out_shape if isinstance(out_shape, (list, tuple)) else [out_shape]
    moved = sum(x.size * x.dtype.itemsize for x in (*smem, *vmem, *outs))
    n_real = len(smem) + len(vmem)

    def wrapped(*refs):
        kernel(*refs[:n_real], *refs[n_real + len(after) :])

    return pl.pallas_call(
        wrapped,
        out_shape=out_shape,
        in_specs=[pl.BlockSpec(memory_space=SMEM)] * len(smem)
        + [pl.BlockSpec(memory_space=VMEM)] * len(vmem)
        + [pl.BlockSpec(memory_space=pl.ANY)] * len(after),
        out_specs=jax.tree.map(lambda _: pl.BlockSpec(memory_space=VMEM), out_shape),
        scratch_shapes=list(scratch),
        compiler_params=pltpu.CompilerParams(vmem_limit_bytes=moved + 4 * 2**20),
        cost_estimate=pl.CostEstimate(flops=int(5 * flops), bytes_accessed=moved if flops else 1, transcendentals=0),
    )(*smem, *vmem, *after)


def hold(x, after):
    def kernel(*refs):
        pass

    return pl.pallas_call(
        kernel,
        out_shape=jax.ShapeDtypeStruct(x.shape, x.dtype),
        in_specs=[pl.BlockSpec(memory_space=pl.ANY)] * (1 + len(after)),
        out_specs=pl.BlockSpec(memory_space=pl.ANY),
        input_output_aliases={0: 0},
        compiler_params=pltpu.CompilerParams(vmem_limit_bytes=2**20),
    )(x, *after)


def on_device(a_tiles, p_tiles, pair_a, pair_p):
    a, p = a_tiles[0, 0, 0], p_tiles[0, 0, 0]
    ia, ip = jnp.swapaxes(pair_a[0, 0, 0], 1, 2), jnp.swapaxes(pair_p[0, 0, 0], 1, 2)
    fan, slots = ia.shape[1:]
    held, width = p.shape[0], p.shape[-1]
    layers = lax.axis_size("layer")
    bits = layers.bit_length() - 1
    count = slots // layers
    swap = [(0, 1), (1, 0)]

    half = count // 2
    chunks = [(0, half), (half, count - half)]
    flops = layers * half * fan * width**3

    def floats(size):
        return jax.ShapeDtypeStruct((size, width, width), jnp.float32)

    def exchange(x, bit):
        return lax.ppermute(x, "layer", [(i, i ^ (1 << bit)) for i in range(layers)])

    def cross(x, bit):
        flip = 0 if bit is None else 1 << bit
        perm = [(c * layers + i, (1 - c) * layers + (i ^ flip)) for c in range(2) for i in range(layers)]
        return lax.ppermute(x, ("col", "layer"), perm)

    def send(lists, vmem, which, bits, joins, after, cost):
        picked = [chunks[n] for n in which]
        shapes = [message(layers // 2 * size, width) for _, size in picked]
        if joins:
            shapes.append(jax.ShapeDtypeStruct((2 * held, width, width), p.dtype))
        kernel = send_kernel(fan, slots, count, picked, bits, joins)
        made = call(kernel, shapes, (lists,), vmem, after, (), cost * len(which) * flops)
        return made, [exchange(x, b) for x, b in zip(made, bits)]

    def keep(lists, vmem, bits, after, cost):
        shapes = [floats(layers // 2 * size) for _, size in chunks]
        kernel = keep_kernel(fan, slots, count, chunks, bits)
        return call(kernel, shapes, (lists,), vmem, after, (), cost * 2 * flops)

    def add(parts, sizes, rest, bit, after):
        n = sum(sizes) << (len(rest) - 1)
        shapes = [message(n, width), floats(n)]
        kept, came = zip(*parts)
        return call(add_kernel(sizes, rest, bit), shapes, (), (*kept, *came), after)

    own_bits, other_bits = (0, 1), (1, 0)
    sizes = [size for _, size in chunks]
    every = list(range(bits))

    def less(rest, bit):
        return [b for b in rest if b != bit]

    def second(kept, came, size, bit, after):
        sent, kept = add([(kept, came)], [size], less(every, bit), 1 - bit, after)
        return sent, (kept, exchange(sent, 1 - bit))

    p_x = lax.ppermute(p, "col", swap)
    p_r = lax.ppermute(p, "row", swap)
    packed = jax.ShapeDtypeStruct((-(-2 * fan // packing(slots, LANES)), max(slots, LANES)), jnp.int32)
    lists, lists_far = call(pack_kernel, [packed] * 2, (), (ia, ip))

    token = jax.ShapeDtypeStruct((8, width), jnp.float32)
    gate = call(lambda *refs: None, token, (), (), (), (), 10**9)
    gate = call(lambda *refs: None, token, (), (a, p), (gate,))

    (*made, joined), own_came = send(lists, (a, p, p_r), (0, 1), own_bits, True, (gate,), 1)
    own_kept = keep(lists, (a, joined), own_bits, made[:1], 1)
    lists_x = lax.ppermute(hold(lists_far, own_kept[:1]), "col", swap)
    parts, after = [], ()
    for n in range(2):
        sent, part = second(own_kept[n], own_came[n], sizes[n], own_bits[n], after)
        parts.append(part)
        after = (sent,)
    pieces = [jax.ShapeDtypeStruct((held // 2, width, width), p.dtype)] * 2
    pieces = call(split_kernel, pieces, (), (p_x,), (*after, lists_x))
    p_xr = [lax.ppermute(x, "row", swap) for x in pieces]

    (made, joined), came_0 = send(lists_x, (a, p_x, *p_xr), (0,), other_bits[:1], True, (), 0)
    (made,), came_1 = send(lists_x, (a, joined), (1,), other_bits[1:], False, (made,), 0)
    other_came = came_0 + came_1
    other_kept = keep(lists_x, (a, joined), other_bits, (made,), 1)

    rest, part_sizes, after = every[2:], sizes, other_kept[:1]
    for b in every[2:]:
        sent, kept = add(parts, part_sizes, rest, b, after)
        after = (sent,)
        parts, part_sizes = [(kept, exchange(sent, b))], [count]
        rest = less(rest, b)
    (own,) = parts
    streams = []
    for n in range(2):
        sent, part = second(other_kept[n], other_came[n], sizes[n], other_bits[n], after)
        streams.append(part)
        after = (sent,)
    rest = every[2:]
    for b in every[2:-1]:
        for n in range(2):
            sent, kept = add([streams[n]], [sizes[n]], rest, b, after)
            after = (sent,)
            streams[n] = (kept, exchange(sent, b))
        rest = less(rest, b)

    own = call(sum_kernel, floats(count), (), own, after)
    moved, top, after = [], rest[0], (own,)
    for n in range(2):
        shapes = [message(sizes[n], width)] * 2
        far, near = call(cross_kernel(sizes[n], top), shapes, (), streams[n], after)
        after = (far,)
        moved.append((cross(far, top), cross(near, None)))
    early = call(early_kernel, floats(sizes[0]), (), (own, *moved[0]), (), (), 10**9)
    result = jax.ShapeDtypeStruct((count, width, width), jnp.bfloat16)
    return call(last_kernel, result, (), (early, own, *moved[1]))[None, None]


def solution(mesh):
    spec = P("row", "col", "layer", None, None, None)
    return jax.shard_map(
        on_device,
        mesh=mesh,
        in_specs=(spec,) * 4,
        out_specs=P("row", "col", "layer", None, None),
        check_vma=False,
    )
```

```python
import jax
import jax.numpy as jnp
from jax import lax
from jax.experimental import pallas as pl
from jax.experimental.pallas import tpu as pltpu
from jax.sharding import PartitionSpec as P

PEAK = 32766.0
ROWS = 16
LANES = 128
GROUP = 8
SMEM = pltpu.MemorySpace.SMEM
VMEM = pltpu.MemorySpace.VMEM


def head_rows(count):
    return -(-count // ROWS) * ROWS


def message(count, width):
    return jax.ShapeDtypeStruct((count * width + head_rows(count), width), jnp.int16)


def encode(tile):
    top = jnp.max(jnp.abs(tile), axis=0, keepdims=True)
    power = jnp.floor(jnp.log2(jnp.maximum(top, 2.0**-100)) + 0.001) + 1.0
    scaled = jnp.round(tile * (jnp.exp2(-power) * PEAK))
    return scaled.astype(jnp.int32).astype(jnp.int16), power.astype(jnp.int32)


def new_head(count, width):
    return jnp.zeros((head_rows(count), width), jnp.int32)


def rows_at(slot, width):
    start = slot * width
    return pl.ds(start if isinstance(start, int) else pl.multiple_of(start, width), width)


def put_tile(ref, slot, tile, head):
    coded, power = encode(tile)
    ref[rows_at(slot, tile.shape[0]), :] = coded
    rows = lax.broadcasted_iota(jnp.int32, head.shape, 0)
    return jnp.where(rows == slot, power, head)


def put_head(ref, head):
    ref[pl.ds(ref.shape[0] - head.shape[0], head.shape[0]), :] = head.astype(jnp.int16)


def get_head(ref, count):
    rows = head_rows(count)
    return ref[pl.ds(ref.shape[0] - rows, rows), :].astype(jnp.int32)


def get_tile(ref, slot, head):
    rows = lax.broadcasted_iota(jnp.int32, head.shape, 0)
    power = jnp.sum(jnp.where(rows == slot, head, 0), axis=0, keepdims=True)
    coded = ref[rows_at(slot, ref.shape[-1]), :]
    return coded.astype(jnp.int32).astype(jnp.float32) * (jnp.exp2(power.astype(jnp.float32)) * (1.0 / PEAK))


def product(a_ref, p_ref, look, fan):
    chosen = [look(f) for f in range(fan)]
    left = jnp.concatenate([a_ref[pa] for pa, _ in chosen], axis=1)
    right = jnp.concatenate([p_ref[pp] for _, pp in chosen], axis=0)
    return jnp.dot(left, right, preferred_element_type=jnp.float32)


def own_bit(bit):
    return (lax.axis_index("layer") >> bit) & 1


def insert(rest, at, bit):
    low = rest & ((1 << at) - 1)
    return ((rest >> at) << (at + 1)) | (bit << at) | low


def loop(turns, body, start):
    return body(0, start) if turns == 1 else lax.fori_loop(0, turns, body, start)


def packing(slots, lanes):
    return max(1, lanes // slots)


def pack_kernel(ia_ref, ip_ref, own_ref, far_ref):
    fan, slots = ia_ref.shape[1:]
    per = packing(slots, own_ref.shape[1])
    col = lax.axis_index("col")
    for out_ref, column in ((own_ref, col), (far_ref, 1 - col)):
        for which, ref in enumerate((ia_ref, ip_ref)):
            lists = ref[column]
            for f in range(fan):
                row, at = divmod(which * fan + f, per)
                out_ref[pl.ds(row, 1), pl.ds(at * slots, slots)] = lists[f : f + 1]


def finder(lists_ref, fan, slots):
    per = packing(slots, lists_ref.shape[1])

    def place(which, f, t):
        row, at = divmod(which * fan + f, per)
        return lists_ref[row, at * slots + t]

    return lambda t: lambda f: (place(0, f, t), place(1, f, t))


def send_kernel(fan, slots, count, chunks, bits, joins):
    def kernel(lists_ref, a_ref, *refs):
        find = finder(lists_ref, fan, slots)
        n_out = len(chunks) + joins
        p_refs, out_refs = refs[:-n_out], refs[-n_out:]
        if joins:
            out_refs, p_ref = out_refs[:-1], out_refs[-1]
            held = p_ref.shape[0] // 2
            row = lax.axis_index("row")
            p_ref[pl.ds(row * held, held)] = p_refs[0][...]
            at = (1 - row) * held
            for ref in p_refs[1:]:
                p_ref[pl.ds(at, ref.shape[0])] = ref[...]
                at += ref.shape[0]
        else:
            (p_ref,) = p_refs
        width = p_ref.shape[-1]
        for (first, size), bit, out_ref in zip(chunks, bits, out_refs):
            side = 1 - own_bit(bit)
            total = out_ref.shape[0] // width

            def body(step, head):
                for k in range(GROUP):
                    slot = step * GROUP + k
                    layer = insert(slot // size, bit, side)
                    tile = product(a_ref, p_ref, find(layer * count + first + slot % size), fan)
                    head = put_tile(out_ref, slot, tile, head)
                return head

            put_head(out_ref, loop(total // GROUP, body, new_head(total, width)))

    return kernel


def split_kernel(in_ref, *out_refs):
    at = 0
    for ref in out_refs:
        ref[...] = in_ref[pl.ds(at, ref.shape[0])]
        at += ref.shape[0]


def keep_kernel(fan, slots, count, chunks, bits):
    def kernel(lists_ref, a_ref, p_ref, *out_refs):
        find = finder(lists_ref, fan, slots)
        for (first, size), bit, out_ref in zip(chunks, bits, out_refs):
            side = own_bit(bit)

            def body(step, _):
                for k in range(GROUP):
                    slot = step * GROUP + k
                    layer = insert(slot // size, bit, side)
                    out_ref[slot] = product(a_ref, p_ref, find(layer * count + first + slot % size), fan)
                return 0

            loop(out_ref.shape[0] // GROUP, body, 0)

    return kernel


def cross_kernel(sizes, bit, whose):
    def kernel(*refs):
        n = len(sizes)
        kept_refs, in_refs, out_refs = refs[:n], refs[n : 2 * n], refs[2 * n :]
        width = out_refs[0].shape[-1]
        mine = own_bit(bit)
        heads = [get_head(ref, ref.shape[0] // width) for ref in in_refs]

        def put(out_ref, side, chosen):
            count = out_ref.shape[0] // width
            head, slot = new_head(count, width), 0
            for c in chosen:
                for i in range(sizes[c]):
                    at = side * sizes[c] + i
                    tile = kept_refs[c][at] + get_tile(in_refs[c], at, heads[c])
                    head = put_tile(out_ref, slot, tile, head)
                    slot += 1
            put_head(out_ref, head)

        put(out_refs[0], 1 - mine, [whose])
        if len(out_refs) > 1:
            put(out_refs[1], mine, range(n))

    return kernel


def add_kernel(sizes, rest, bit):
    at = rest.index(bit)
    full = sum(sizes)
    halves = 1 << (len(rest) - 1)

    def kernel(*refs):
        n = len(sizes)
        kept_refs, in_refs, (sent_ref, stay_ref) = refs[:n], refs[n : 2 * n], refs[2 * n : 2 * n + 2]
        width = sent_ref.shape[-1]
        mine = own_bit(bit)
        heads = [get_head(ref, ref.shape[0] // width) for ref in in_refs]

        def sums(place):
            for size, kept_ref, in_ref, head in zip(sizes, kept_refs, in_refs, heads):
                for i in range(size):
                    slot = place * size + i
                    yield kept_ref[slot] + get_tile(in_ref, slot, head)

        def send(ref, side):
            def body(half, head):
                for i, tile in enumerate(sums(insert(half, at, side))):
                    head = put_tile(ref, half * full + i, tile, head)
                return head

            put_head(ref, lax.fori_loop(0, halves, body, new_head(halves * full, width), unroll=halves <= 4))

        send(sent_ref, 1 - mine)

        def body(half, _):
            for i, tile in enumerate(sums(insert(half, at, mine))):
                stay_ref[half * full + i] = tile
            return 0

        lax.fori_loop(0, halves, body, 0, unroll=halves <= 4)

    return kernel


def sum_kernel(kept_ref, in_ref, out_ref):
    count = out_ref.shape[0]
    head = get_head(in_ref, count)
    for i in range(count):
        out_ref[i] = kept_ref[i] + get_tile(in_ref, i, head)


def early_kernel(first):
    def kernel(own_ref, far_ref, out_ref):
        size = out_ref.shape[0]
        head = get_head(far_ref, size)
        for i in range(size):
            out_ref[i] = own_ref[first + i] + get_tile(far_ref, i, head)

    return kernel


def last_kernel(near_ref, *refs):
    early_refs, out_ref = refs[:-1], refs[-1]
    count = out_ref.shape[0]
    head, at = get_head(near_ref, count), 0
    for ref in early_refs:
        for i in range(ref.shape[0]):
            out_ref[at] = (ref[i] + get_tile(near_ref, at, head)).astype(out_ref.dtype)
            at += 1


def call(kernel, out_shape, smem, vmem, after=(), scratch=(), flops=0):
    outs = out_shape if isinstance(out_shape, (list, tuple)) else [out_shape]
    moved = sum(x.size * x.dtype.itemsize for x in (*smem, *vmem, *outs))
    n_real = len(smem) + len(vmem)

    def wrapped(*refs):
        kernel(*refs[:n_real], *refs[n_real + len(after) :])

    return pl.pallas_call(
        wrapped,
        out_shape=out_shape,
        in_specs=[pl.BlockSpec(memory_space=SMEM)] * len(smem)
        + [pl.BlockSpec(memory_space=VMEM)] * len(vmem)
        + [pl.BlockSpec(memory_space=pl.ANY)] * len(after),
        out_specs=jax.tree.map(lambda _: pl.BlockSpec(memory_space=VMEM), out_shape),
        scratch_shapes=list(scratch),
        compiler_params=pltpu.CompilerParams(vmem_limit_bytes=moved + 4 * 2**20),
        cost_estimate=pl.CostEstimate(flops=int(5 * flops), bytes_accessed=moved if flops else 1, transcendentals=0),
    )(*smem, *vmem, *after)


def hold(x, after):
    def kernel(*refs):
        pass

    return pl.pallas_call(
        kernel,
        out_shape=jax.ShapeDtypeStruct(x.shape, x.dtype),
        in_specs=[pl.BlockSpec(memory_space=pl.ANY)] * (1 + len(after)),
        out_specs=pl.BlockSpec(memory_space=pl.ANY),
        input_output_aliases={0: 0},
        compiler_params=pltpu.CompilerParams(vmem_limit_bytes=2**20),
    )(x, *after)


def on_device(a_tiles, p_tiles, pair_a, pair_p):
    a, p = a_tiles[0, 0, 0], p_tiles[0, 0, 0]
    ia, ip = jnp.swapaxes(pair_a[0, 0, 0], 1, 2), jnp.swapaxes(pair_p[0, 0, 0], 1, 2)
    fan, slots = ia.shape[1:]
    held, width = p.shape[0], p.shape[-1]
    layers = lax.axis_size("layer")
    bits = layers.bit_length() - 1
    count = slots // layers
    swap = [(0, 1), (1, 0)]

    half = count // 2
    chunks = [(0, half), (half, count - half)]
    flops = layers * half * fan * width**3

    def floats(size):
        return jax.ShapeDtypeStruct((size, width, width), jnp.float32)

    def exchange(x, bit):
        return lax.ppermute(x, "layer", [(i, i ^ (1 << bit)) for i in range(layers)])

    def cross(x, bit):
        flip = 0 if bit is None else 1 << bit
        perm = [(c * layers + i, (1 - c) * layers + (i ^ flip)) for c in range(2) for i in range(layers)]
        return lax.ppermute(x, ("col", "layer"), perm)

    def send(lists, vmem, which, bits, joins, after, cost):
        picked = [chunks[n] for n in which]
        shapes = [message(layers // 2 * size, width) for _, size in picked]
        if joins:
            shapes.append(jax.ShapeDtypeStruct((2 * held, width, width), p.dtype))
        kernel = send_kernel(fan, slots, count, picked, bits, joins)
        made = call(kernel, shapes, (lists,), vmem, after, (), cost * len(which) * flops)
        return made, [exchange(x, b) for x, b in zip(made, bits)]

    def keep(lists, vmem, bits, after, cost):
        shapes = [floats(layers // 2 * size) for _, size in chunks]
        kernel = keep_kernel(fan, slots, count, chunks, bits)
        return call(kernel, shapes, (lists,), vmem, after, (), cost * 2 * flops)

    def add(parts, sizes, rest, bit, after):
        n = sum(sizes) << (len(rest) - 1)
        shapes = [message(n, width), floats(n)]
        kept, came = zip(*parts)
        return call(add_kernel(sizes, rest, bit), shapes, (), (*kept, *came), after)

    own_bits, other_bits = (0, 1), (1, 0)
    sizes = [size for _, size in chunks]
    every = list(range(bits))

    def less(rest, bit):
        return [b for b in rest if b != bit]

    def second(kept, came, size, bit, after):
        sent, kept = add([(kept, came)], [size], less(every, bit), 1 - bit, after)
        return sent, (kept, exchange(sent, 1 - bit))

    p_x = lax.ppermute(p, "col", swap)
    p_r = lax.ppermute(p, "row", swap)
    packed = jax.ShapeDtypeStruct((-(-2 * fan // packing(slots, LANES)), max(slots, LANES)), jnp.int32)
    lists, lists_far = call(pack_kernel, [packed] * 2, (), (ia, ip))

    token = jax.ShapeDtypeStruct((8, width), jnp.float32)
    gate = call(lambda *refs: None, token, (), (), (), (), 10**9)
    gate = call(lambda *refs: None, token, (), (a, p), (gate,))

    (*made, joined), own_came = send(lists, (a, p, p_r), (0, 1), own_bits, True, (gate,), 1)
    own_kept = keep(lists, (a, joined), own_bits, made[:1], 1)
    lists_x = lax.ppermute(hold(lists_far, own_kept[:1]), "col", swap)
    parts, after = [], ()
    for n in range(2):
        sent, part = second(own_kept[n], own_came[n], sizes[n], own_bits[n], after)
        parts.append(part)
        late, after = sent, (sent,)
    pieces = [jax.ShapeDtypeStruct((held // 2, width, width), p.dtype)] * 2
    pieces = call(split_kernel, pieces, (), (p_x,), (*after, lists_x))
    p_xr = [lax.ppermute(x, "row", swap) for x in pieces]

    (made, joined), came_0 = send(lists_x, (a, p_x, *p_xr), (0,), other_bits[:1], True, (), 0)
    parts[1] = (parts[1][0], exchange(hold(late, (made,)), 1 - own_bits[1]))
    (made,), came_1 = send(lists_x, (a, joined), (1,), other_bits[1:], False, (made,), 0)
    other_came = came_0 + came_1
    other_kept = keep(lists_x, (a, joined), other_bits, (made,), 1)

    rest, part_sizes, after = every[2:], sizes, other_kept[:1]
    for b in every[2:]:
        sent, kept = add(parts, part_sizes, rest, b, after)
        after = (sent,)
        parts, part_sizes = [(kept, exchange(sent, b))], [count]
        rest = less(rest, b)
    (own,) = parts
    streams = []
    for n in range(2):
        sent, part = second(other_kept[n], other_came[n], sizes[n], other_bits[n], after)
        streams.append(part)
        after = (sent,)
    rest = every[2:]
    for b in every[2:-1]:
        for n in range(2):
            sent, kept = add([streams[n]], [sizes[n]], rest, b, after)
            after = (sent,)
            streams[n] = (kept, exchange(sent, b))
        rest = less(rest, b)

    own = call(sum_kernel, floats(count), (), own, after)
    moved, top, after = [], rest[0], (own,)
    for n in range(2):
        shapes = [message(sizes[n], width)] + [message(count, width)] * n
        used, used_sizes = ([streams[0]], sizes[:1]) if n == 0 else (streams, sizes)
        kept, came = zip(*used)
        sent = call(cross_kernel(used_sizes, top, n), shapes, (), (*kept, *came), after)
        after = (sent[0],)
        moved.append(cross(sent[0], top))
    near = cross(sent[1], None)
    early = []
    for n, (first, size) in enumerate(chunks):
        early.append(call(early_kernel(first), floats(size), (), (own, moved[n]), early[-1:], (), 10**9))
    result = jax.ShapeDtypeStruct((count, width, width), jnp.bfloat16)
    return call(last_kernel, result, (), (near, *early))[None, None]


def solution(mesh):
    spec = P("row", "col", "layer", None, None, None)
    return jax.shard_map(
        on_device,
        mesh=mesh,
        in_specs=(spec,) * 4,
        out_specs=P("row", "col", "layer", None, None),
        check_vma=False,
    )
```
